32 devices in a mesh: dp: 8 (over z, x), heads: 4 (over y, core).
Axes of the slice: x: 2, y: 2, z: 4, core: 2. Of those that a mesh axis runs over, the one named last changes fastest.
Arguments:
- tokens: bfloat16 [24576, 480], P(('dp', 'heads')), may hold values from -6 to 6
- attn_norm_gain: float32 [480], replicated, may hold values from 0.5 to 1.5
- attn_norm_bias: float32 [480], replicated, may hold values from -3 to 3
- qkv_weight: bfloat16 [480, 1440], P(None, 'heads'), may hold values from -0.25 to 0.25
- qkv_bias: float32 [1440], P('heads'), may hold values from -3 to 3
- out_weight: bfloat16 [480, 480], P('heads'), may hold values from -0.75 to 0.75
- out_bias: float32 [480], replicated, may hold values from -2 to 2
- ffn_norm_gain: float32 [480], replicated, may hold values from 0.5 to 1.5
- ffn_norm_bias: float32 [480], replicated, may hold values from -3 to 3
- up_weight: bfloat16 [480, 1920], P('heads', 'dp'), may hold values from -0.25 to 0.25
- up_bias: float32 [1920], replicated, may hold values from -3 to 3
- down_weight: bfloat16 [1920, 480], P('dp', 'heads'), may hold values from -0.125 to 0.125
- down_bias: float32 [480], replicated, may hold values from -2 to 2
- lengths: int32 [24, 4], P('dp'), may hold values from 0 to 1024, as said below
- cluster_ids: int32 [24, 4], P('dp'), may hold values from 0 to 1023
- cluster_weight: float32 [1024], replicated, may hold values from 0.25 to 4
- grad_out: bfloat16 [24576, 480], P(('dp', 'heads')), may hold values from -6 to 6
Outputs:
- result: bfloat16 [24576, 480], P(('dp', 'heads'))
- d_tokens: float32 [24576, 480], P(('dp', 'heads'))
- d_attn_norm_gain: float32 [480], replicated
- d_attn_norm_bias: float32 [480], replicated
- d_qkv_weight: float32 [480, 1440], P(None, 'heads')
- d_qkv_bias: float32 [1440], P('heads')
- d_out_weight: float32 [480, 480], P('heads')
- d_out_bias: float32 [480], replicated
- d_ffn_norm_gain: float32 [480], replicated
- d_ffn_norm_bias: float32 [480], replicated
- d_up_weight: float32 [480, 1920], P('heads', 'dp')
- d_up_bias: float32 [1920], replicated
- d_down_weight: float32 [1920, 480], P('dp', 'heads')
- d_down_bias: float32 [480], replicated
The draws below stay inside these ranges and needn't reach their ends.
Inputs may be any that keep to these rules, and one draw needn't show every extreme that they name: `lengths`: in each group the 4 slots are proteins lying one after another from the group's first row, summing to at most 1024, the remaining rows padding. The third slot's protein starts before row 256 of its group and ends after row 768; in some group it is 1024 long.
All inputs are finite; a program needn't handle non-finite values.
Results may differ from the reference program's by a relative error of at most 0.015.
Values may be sent and summed in bfloat16 or wider, within the bound.
A program may use at most 256 MiB of HBM per device.

```python
import math
import jax
import jax.numpy as jnp
from jax import lax

D = 480
HEADS = 20
HD = 24
FF = 1920
GPD = 3
GROUP_DEV = 256
PROT = 4
CLUSTERS = 1024
GROUP = 1024
NGROUP = 24
TOKENS = 24576
N_DP = 8
N_HEADS = 4


def draw_lengths(key, part):
    key = jax.random.fold_in(key, 17)
    key_list = jax.random.split(key, 4)
    half_dev = GROUP_DEV // 2
    short_lens = jax.random.randint(key_list[0], (NGROUP, 2), 0, half_dev, dtype=jnp.int32)
    chosen = jax.random.randint(key_list[1], (), 0, NGROUP, dtype=jnp.int32)
    full_group = jnp.arange(NGROUP, dtype=jnp.int32) == chosen
    short_lens = jnp.where(full_group[:, None], 0, short_lens)
    before = short_lens[:, 0] + short_lens[:, 1]
    least_len = 3 * GROUP_DEV + 1 - before
    most_len = GROUP - before
    spread_draw = jax.random.randint(key_list[2], (NGROUP,), 0, 1 << 20, dtype=jnp.int32)
    longest = least_len + spread_draw % (most_len - least_len + 1)
    longest = jnp.where(full_group, GROUP, longest)
    room_left = GROUP - before - longest
    tail_draw = jax.random.randint(key_list[3], (NGROUP,), 0, 1 << 20, dtype=jnp.int32)
    tail_len = tail_draw % (room_left + 1)
    return jnp.stack([short_lens[:, 0], short_lens[:, 1], longest, tail_len], axis=1).astype(jnp.int32)


def set_ends(drawn, rng, smallest, top_value):
    longest = drawn.shape.index(max(drawn.shape))
    spots = []
    for shift in (0, 1):
        where = [jax.random.randint(jax.random.fold_in(rng, axis), (), 0, length) for axis, length in enumerate(drawn.shape)]
        where[longest] = (where[longest] + shift) % drawn.shape[longest]
        spots.append(tuple(where))
    return drawn.at[spots[0]].set(smallest).at[spots[1]].set(top_value)


def steps_of(key, shape, cuts, low, largest):
    level, own = 1.0, jax.random.fold_in(key, 6)
    for axis_at, shards_of in cuts:
        draws = jnp.exp(jax.random.uniform(jax.random.fold_in(own, axis_at), (shards_of,), jnp.float32, low / len(cuts), largest / len(cuts)))
        level = level * jnp.repeat(draws, shape[axis_at] // shards_of).reshape([-1 if axis == axis_at else 1 for axis in range(len(shape))])
    return level


def bell_draw(rng, dims, spread, reach, shards=(), kind=jnp.bfloat16):
    result = spread * jax.random.normal(rng, dims, jnp.float32)
    if shards:
        result = result * steps_of(rng, dims, shards, -0.22, 0.18)
    return jnp.clip(result, -reach, reach).astype(kind)


def setup_inputs(seed: int = 0) -> dict:
    keys = jax.random.split(jax.random.key(seed), 18)
    tokens = bell_draw(keys[0], (TOKENS, D), 1.0, 6.0, ((0, 32),))
    attn_norm_gain = jnp.clip(1.0 + 0.1 * jax.random.normal(keys[1], (D,), jnp.float32), 0.5, 1.5)
    attn_norm_bias = bell_draw(keys[2], (D,), 0.5, 3.0, (), jnp.float32)
    qkv_weight = bell_draw(keys[3], (D, 3 * D), D ** -0.5, 0.25, ((1, 4),))
    qkv_bias = bell_draw(keys[4], (3 * D,), 0.5, 3.0, ((0, 4),), jnp.float32)
    out_weight = bell_draw(keys[5], (D, D), (D // 8) ** -0.5, 0.75, ((0, 4),))
    out_bias = bell_draw(keys[6], (D,), 0.3, 2.0, (), jnp.float32)
    ffn_norm_gain = jnp.clip(1.0 + 0.1 * jax.random.normal(keys[7], (D,), jnp.float32), 0.5, 1.5)
    ffn_norm_bias = bell_draw(keys[8], (D,), 0.5, 3.0, (), jnp.float32)
    up_weight = bell_draw(keys[9], (D, FF), D ** -0.5, 0.25, ((0, 4), (1, 8)))
    up_bias = bell_draw(keys[10], (FF,), 0.5, 3.0, (), jnp.float32)
    down_weight = bell_draw(keys[11], (FF, D), FF ** -0.5, 0.125, ((0, 8), (1, 4)))
    down_bias = bell_draw(keys[12], (D,), 0.3, 2.0, (), jnp.float32)
    lengths = draw_lengths(jax.random.fold_in(keys[17], 71), 0)
    cluster_ids = set_ends(jax.random.randint(keys[14], (NGROUP, PROT), 0, CLUSTERS), jax.random.fold_in(keys[14], 1), 0, CLUSTERS - 1).astype(jnp.int32)
    cluster_weight = jnp.clip(jnp.exp(jax.random.uniform(keys[15], (CLUSTERS,), jnp.float32, math.log(0.25), math.log(4.0))), 0.25, 4.0)
    grad_out = bell_draw(keys[16], (TOKENS, D), 1.0, 6.0, ((0, 32),))
    return dict(tokens=tokens, attn_norm_gain=attn_norm_gain, attn_norm_bias=attn_norm_bias, qkv_weight=qkv_weight, qkv_bias=qkv_bias, out_weight=out_weight, out_bias=out_bias, ffn_norm_gain=ffn_norm_gain, ffn_norm_bias=ffn_norm_bias, up_weight=up_weight, up_bias=up_bias, down_weight=down_weight, down_bias=down_bias, lengths=lengths, cluster_ids=cluster_ids, cluster_weight=cluster_weight, grad_out=grad_out)


EPSILON = 1e-05
HIGHEST = lax.Precision.HIGHEST

@jax.custom_vjp
def low(v):
    return lax.optimization_barrier(v.astype(jnp.bfloat16)).astype(jnp.float32)

@jax.custom_vjp
def low_back(v):
    return v

def low_keep(v):
    return (low(v), None)

def low_pass(kept, grad):
    return (grad,)

def back_keep(v):
    return (v, None)

def back_low(kept, grad):
    return (low(grad),)
low.defvjp(low_keep, low_pass)
low_back.defvjp(back_keep, back_low)

def matmul(left_side, right_side):
    return jnp.dot(left_side, right_side, precision=HIGHEST, preferred_element_type=jnp.float32)

def layer_norm(values, scale_vec, shift_vec):
    average = lax.optimization_barrier(jnp.mean(values, axis=-1, keepdims=True))
    centred = values - average
    variance = lax.optimization_barrier(jnp.mean(centred * centred, axis=-1, keepdims=True))
    return centred * lax.rsqrt(variance + EPSILON) * scale_vec + shift_vec

def rotate(vectors, cos_table, sin_table):
    half_size = vectors.shape[-1] // 2
    first_half = vectors[..., :half_size]
    second_half = vectors[..., half_size:]
    return jnp.concatenate([first_half * cos_table - second_half * sin_table, second_half * cos_table + first_half * sin_table], axis=-1)

def angles(position, head_size):
    frequency = 10000.0 ** (-2.0 * jnp.arange(head_size // 2, dtype=jnp.float32) / head_size)
    turn_angle = position[:, None] * frequency[None, :]
    return (jnp.cos(turn_angle)[:, None, :], jnp.sin(turn_angle)[:, None, :])

def structure(lengths_row, ids_row, weight_table, row_total):
    protein_ends = jnp.cumsum(lengths_row, dtype=jnp.int32)
    row_index = jnp.arange(row_total, dtype=jnp.int32)
    passed_ends = (row_index[:, None] >= protein_ends[None, :]).astype(jnp.int32)
    segment = lax.optimization_barrier(jnp.sum(passed_ends, axis=1, dtype=jnp.int32))
    offset = lax.optimization_barrier(jnp.sum(passed_ends * lengths_row[None, :], axis=1, dtype=jnp.int32))
    position = (row_index - offset).astype(jnp.float32)
    slot_ids = jnp.arange(lengths_row.shape[0], dtype=jnp.int32)
    member = (segment[:, None] == slot_ids[None, :]).astype(jnp.float32)
    row_weight = lax.optimization_barrier(jnp.sum(member * weight_table[ids_row][None, :], axis=1))
    return (segment, position, row_weight)

def attend(queries, key_rows, values, segment):
    row_total = queries.shape[0]
    block_rows = min(512, row_total)

    def one_block(row_start):
        query_block = lax.dynamic_slice_in_dim(queries, row_start, block_rows, 0)
        segment_block = lax.dynamic_slice_in_dim(segment, row_start, block_rows, 0)
        scores = low_back(jnp.einsum('qhd,khd->hqk', query_block, key_rows, precision=HIGHEST))
        allowed = segment_block[:, None] == segment[None, :]
        scores = jnp.where(allowed[None], scores, -1e+30)
        weights_low = low(jax.nn.softmax(scores, axis=-1))
        return jnp.einsum('hqk,khd->qhd', weights_low, values, precision=HIGHEST)
    block_starts = jnp.arange(row_total // block_rows, dtype=jnp.int32) * block_rows
    context = lax.map(jax.checkpoint(one_block), block_starts)
    return context.reshape(row_total, queries.shape[1] * queries.shape[2])

def layer_forward(param_set, tokens_block, segment, position):
    attn_gain, attn_shift, qkv_weight, qkv_bias, out_weight, out_bias, ffn_gain, ffn_shift, up_weight, up_bias, down_weight, down_bias = param_set
    row_total = tokens_block.shape[0]
    normed_one = low(layer_norm(tokens_block, attn_gain, attn_shift))
    qkv_proj = low_back(matmul(normed_one, qkv_weight) + qkv_bias).reshape(row_total, HEADS, 3, HD)
    cos_table, sin_table = angles(position, HD)
    queries = low(rotate(qkv_proj[:, :, 0], cos_table, sin_table) * HD ** (-0.5))
    key_rows = low(rotate(qkv_proj[:, :, 1], cos_table, sin_table))
    values = low(qkv_proj[:, :, 2])
    context = low_back(low(attend(queries, key_rows, values, segment)))
    attn_out = low_back(matmul(context, out_weight) + out_bias)
    middle = tokens_block + attn_out
    normed_two = low(layer_norm(middle, ffn_gain, ffn_shift))
    up_proj = low_back(matmul(normed_two, up_weight) + up_bias)
    hidden = low(jax.nn.gelu(up_proj, approximate=False))
    ffn_out = low_back(matmul(hidden, down_weight) + down_bias)
    return middle + ffn_out

def to_groups(rows):
    return rows.reshape(N_DP, N_HEADS, GPD, GROUP_DEV, D).transpose(0, 2, 1, 3, 4).reshape(NGROUP, GROUP, D)

def from_groups(rows):
    return rows.reshape(N_DP, GPD, N_HEADS, GROUP_DEV, D).transpose(0, 2, 1, 3, 4).reshape(TOKENS, D)

def reference(tokens, attn_norm_gain, attn_norm_bias, qkv_weight, qkv_bias, out_weight, out_bias, ffn_norm_gain, ffn_norm_bias, up_weight, up_bias, down_weight, down_bias, lengths, cluster_ids, cluster_weight, grad_out):
    params = tuple((array_in.astype(jnp.float32) for array_in in (attn_norm_gain, attn_norm_bias, qkv_weight, qkv_bias, out_weight, out_bias, ffn_norm_gain, ffn_norm_bias, up_weight, up_bias, down_weight, down_bias)))
    group_tokens = to_groups(tokens.astype(jnp.float32))
    group_grads = to_groups(grad_out.astype(jnp.float32))

    def group_step(summed, group_item):
        tokens_block, grads_block, lengths_row, ids_row = group_item
        segment, position, row_weight = structure(lengths_row, ids_row, cluster_weight, GROUP)
        output, pullback = jax.vjp(lambda param_set, inputs: layer_forward(param_set, inputs, segment, position), params, tokens_block)
        param_grads, token_grads = pullback(grads_block * row_weight[:, None])
        summed = jax.tree.map(jnp.add, summed, param_grads)
        return (summed, (output.astype(jnp.bfloat16), token_grads))
    initial = jax.tree.map(jnp.zeros_like, params)
    summed, (outputs, token_grads) = lax.scan(group_step, initial, (group_tokens, group_grads, lengths, cluster_ids))
    g_attn_gain, g_attn_bias, g_qkv_weight, g_qkv_bias, g_out_weight, g_out_bias, g_ffn_gain, g_ffn_bias, g_up_weight, g_up_bias, g_down_weight, g_down_bias = summed
    return (from_groups(outputs), from_groups(token_grads), g_attn_gain, g_attn_bias, g_qkv_weight, g_qkv_bias, g_out_weight, g_out_bias, g_ffn_gain, g_ffn_bias, g_up_weight, g_up_bias, g_down_weight, g_down_bias)
```

```python
from functools import partial

import jax
import jax.numpy as jnp
import numpy as np
from jax import lax
from jax.experimental import pallas as pl
from jax.experimental.pallas import tpu as pltpu
from jax.sharding import PartitionSpec as P

F32, BF16 = jnp.float32, jnp.bfloat16
MESH = pl.DeviceIdType.MESH
HD = 24
HEADS = 5
USED = HEADS * HD
LANES = 128
EPSILON = 1e-05
LOG2E = 1.4426950408889634
BIG = 1e30
BLOCK = 256
FF_TILE = 384


def dims(a, b, ca, cb, precision=None):
    return lax.dot_general(
        a, b, (((ca,), (cb,)), ((), ())), preferred_element_type=F32, precision=precision
    )


def nn(a, b):
    return dims(a, b, 1, 0)


def nt(a, b):
    return dims(a, b, 1, 1)


def tn(a, b):
    return dims(a, b, 0, 0)


def lane(rows, width=LANES):
    return lax.broadcasted_iota(jnp.int32, (rows, width), 1)


def head_lanes(rows, j):
    at = lane(rows)
    return (at >= HD * j) & (at < HD * (j + 1))


def partner(x):
    at = lane(x.shape[0])
    half = HD // 2
    return jnp.where(
        at % HD < half, pltpu.roll(x, LANES - half, 1), pltpu.roll(x, half, 1)
    )


def norm(x):
    centred = x - jnp.mean(x, axis=-1, keepdims=True)
    rstd = lax.rsqrt(jnp.mean(centred * centred, axis=-1, keepdims=True) + EPSILON)
    return centred * rstd, rstd


def norm_back(g, gain, xhat, rstd):
    n = g * gain
    return rstd * (
        n
        - jnp.mean(n, axis=-1, keepdims=True)
        - xhat * jnp.mean(n * xhat, axis=-1, keepdims=True)
    )


def body(
    tok, grad, wqkv, wout, upt, down, attn_gain, attn_bias, qkv_bias, out_bias, ffn_gain,
    ffn_bias, up_bias, down_bias, perm, cos, sin, lengths, ids, cw,
    result, dtok, dwqkv, dwout, dup, ddown, sums, dupb, dqkvb, phbm,
    n1, wq, wo, qkv_b, q_s, k_s, v_s, ctx, ctxb, invl, pslot,
    rs_core_out, rs_core_in, rs_y_out, rs_y_in, rs_own,
    mid, n2, df, facc, dn2, gup, gdown, da, do_s, dot_t, q_t, dq, dk_t, dv_t, dqkv,
    ag_s, ag_r, rs_s, rs_r, p_s,
):
    d, h = lax.axis_index("dp"), lax.axis_index("heads")
    core, y = h % 2, h // 2
    h_sib = h + 1 - 2 * core
    h_y = (h + 2) % 4
    sib, ypart = (d, h_sib), (d, h_y)
    groups = lengths.shape[0]
    width = tok.shape[1]
    group_rows = 4 * BLOCK
    steps = 4

    def send(src, dst, s, r, to):
        return pltpu.make_async_remote_copy(
            src_ref=src, dst_ref=dst, send_sem=s, recv_sem=r, device_id=to, device_id_type=MESH
        )

    def gather_copy(use, buf, k, n):
        block, to = ((h, sib), (h, ypart), (h_y, sib))[n]
        return send(
            buf.at[k, block], buf.at[k, block], ag_s.at[use, k, n], ag_r.at[use, k, n], to
        )

    def gather_start(use, buf, k):
        gather_copy(use, buf, k, 1).start()
        gather_copy(use, buf, k, 0).start()

    def gather_forward(use, buf, k):
        gather_copy(use, buf, k, 1).wait_recv()
        gather_copy(use, buf, k, 2).start()

    def gather_finish(use, buf, k):
        gather_copy(use, buf, k, 0).wait_recv()
        gather_copy(use, buf, k, 2).wait_recv()

    def gather_sent(use, buf, k):
        for n in range(3):
            gather_copy(use, buf, k, n).wait_send()

    def sum_copy(use, k, n):
        src, dst, to = ((rs_core_out, rs_core_in, sib), (rs_y_out, rs_y_in, ypart))[n]
        return send(src.at[k], dst.at[k], rs_s.at[use, k, n], rs_r.at[use, k, n], to)

    def sum_start(use, k, part):
        for other in (0, 1):
            rs_core_out[k, other] = part(2 * other + 1 - core).astype(BF16)
        sum_copy(use, k, 0).start()
        for other in (0, 1):
            rs_own[k, other] = part(2 * other + core)

    def sum_forward(use, k):
        sum_copy(use, k, 0).wait_recv()
        rs_y_out[k] = (rs_own[k, 1 - y] + rs_core_in[k, 1 - y].astype(F32)).astype(BF16)
        sum_copy(use, k, 1).start()

    def sum_finish(use, k):
        sum_copy(use, k, 1).wait_recv()
        return rs_own[k, y] + rs_core_in[k, y].astype(F32) + rs_y_in[k].astype(F32)

    def sum_sent(use, k):
        for n in range(2):
            sum_copy(use, k, n).wait_send()

    def rows_of(k):
        return slice(k * BLOCK, (k + 1) * BLOCK)

    def add_sum(row, value):
        sums[row : row + 1, 0:width] += value

    barrier = pltpu.get_barrier_semaphore()
    for other in (sib, ypart):
        pl.semaphore_signal(barrier, inc=1, device_id=other, device_id_type=MESH)

    def first_norm(k):
        xhat, _ = norm(tok[rows_of(k), :].astype(F32))
        n1[k, h, :, 0:width] = (xhat * attn_gain[...] + attn_bias[...]).astype(BF16)
        n1[k, h, :, width:512] = jnp.zeros((BLOCK, 512 - width), BF16)

    first_norm(0)
    pl.semaphore_wait(barrier, 2)
    gather_start(0, n1, 0)
    for k in range(1, groups):
        first_norm(k)
        gather_start(0, n1, k)

    wq[0:width, :] = nn(wqkv[...], perm[...]).astype(BF16)
    wq[width:512, :] = jnp.zeros((512 - width, 3 * LANES), BF16)
    qkv_b[...] = dims(qkv_bias[...], perm[...].astype(F32), 1, 0, lax.Precision.HIGHEST)
    wo[:, width:512] = jnp.zeros((LANES, 512 - width), BF16)
    wo[:, 0:width] = jnp.concatenate(
        [wout[...].astype(F32), jnp.zeros((LANES - USED, width), F32)], axis=0
    ).astype(BF16)
    sums[...] = jnp.zeros_like(sums)
    dwqkv[...] = jnp.zeros_like(dwqkv)
    dwout[...] = jnp.zeros_like(dwout)
    dqkvb[...] = jnp.zeros_like(dqkvb)
    dupb[...] = jnp.zeros_like(dupb)
    n2[:, width:512] = jnp.zeros((groups * BLOCK, 512 - width), BF16)
    df[:, width:512] = jnp.zeros((groups * BLOCK, 512 - width), BF16)
    for k in range(groups):
        da[k, h, :, width:512] = jnp.zeros((BLOCK, 512 - width), BF16)

    def ends_of(k):
        total, ends = 0, []
        for p in range(4):
            total = total + lengths[k, p]
            ends.append(total)
        return ends

    def project(k):
        ends = ends_of(k)
        at1 = lane(1)
        lo = jnp.where(at1 == USED, 0, group_rows + 1)
        hi = jnp.where(at1 == USED + 4, group_rows + 1, 0)
        for p in range(4):
            lo = jnp.where(at1 == USED + 1 + p, ends[p], lo)
            hi = jnp.where(at1 == USED + p, ends[p], hi)

        def step(i, _):
            r = pl.ds(pl.multiple_of(i * BLOCK, BLOCK), BLOCK)
            x = nn(n1[k, i], wq[...]) + qkv_b[...]
            c, s = cos[r, :], sin[r, :]
            at = lane(BLOCK)
            row = lax.broadcasted_iota(jnp.int32, (BLOCK, LANES), 0) + i * BLOCK
            inside = (row >= lo) & (row < hi)
            marks = (at >= USED) & (at < USED + 5)
            q = x[:, 0:LANES]
            q = (q * c + partner(q) * s) * (HD ** (-0.5) * LOG2E)
            q_s[k, r, :] = jnp.where(at < USED, q, jnp.where(inside, 1.0, 0.0)).astype(BF16)
            key = x[:, LANES : 2 * LANES]
            key = key * c + partner(key) * s
            k_s[k, r, :] = jnp.where(
                at < USED, key, jnp.where(marks & jnp.logical_not(inside), -BIG, 0.0)
            ).astype(BF16)
            v_s[k, r, :] = jnp.where(
                at < USED, x[:, 2 * LANES : 3 * LANES], jnp.where(at < USED + 2, 1.0, 0.0)
            ).astype(BF16)
            return 0

        lax.fori_loop(0, steps, step, 0)

    def p_out(k, i):
        slot = (k * steps + i) % 2
        return pltpu.make_async_copy(pslot.at[slot], phbm.at[k, i], p_s.at[slot])

    def p_in(n):
        slot = n % 2
        return pltpu.make_async_copy(phbm.at[n // steps, n % steps], pslot.at[slot], p_s.at[slot])

    def attend(k, first, last):
        def step(i, _):
            n = k * steps + i
            slot = n % 2

            @pl.when(n >= 2)
            def _():
                p_out(k, i).wait()

            r = pl.ds(pl.multiple_of(i * BLOCK, BLOCK), BLOCK)
            q = q_s[k, r, :]
            keys, vals = k_s[k], v_s[k]
            at = lane(BLOCK)

            def score(j):
                return nt(jnp.where(head_lanes(BLOCK, j) | (at >= USED), q, 0), keys)

            acc = jnp.zeros((BLOCK, LANES), F32)
            inv = jnp.zeros((BLOCK, LANES), F32)
            s = score(0)
            for j in range(HEADS):
                later = score(j + 1) if j + 1 < HEADS else None
                e = jnp.exp2(s - jnp.max(s, axis=1, keepdims=True)).astype(BF16)
                pslot[slot, j] = e
                o = nn(e, vals)
                one = 1.0 / o[:, USED : USED + 1]
                acc = jnp.where(head_lanes(BLOCK, j), o * one, acc)
                inv = jnp.where(head_lanes(BLOCK, j), one, inv)
                s = later
            ctx[k, r, :] = acc
            ctxb[k, r, :] = acc.astype(BF16)
            invl[k, r, :] = inv
            p_out(k, i).start()
            return 0

        lax.fori_loop(first, last, step, 0)

    def out_part(k):
        def part(i):
            r = pl.ds(pl.multiple_of(i * BLOCK, BLOCK), BLOCK)
            return nn(ctxb[k, r, :], wo[...])

        return part

    gather_forward(0, n1, 0)
    for k in range(groups):
        gather_finish(0, n1, k)
        project(k)
        if k > 0:
            sum_forward(0, k - 1)
        attend(k, 0, steps - 1)
        if k + 1 < groups:
            gather_forward(0, n1, k + 1)
        attend(k, steps - 1, steps)
        sum_start(0, k, out_part(k))
    sum_forward(0, groups - 1)
    for n in (groups * steps, groups * steps + 1):
        p_in(n % 2).wait()
    p_in(0).start()
    p_in(1).start()

    def weight_of(k):
        ends = ends_of(k)
        row = lax.broadcasted_iota(jnp.int32, (BLOCK, 1), 0) + h * BLOCK
        w = jnp.zeros((BLOCK, 1), F32)
        for p in reversed(range(4)):
            w = jnp.where(row < ends[p], cw[ids[k, p]], w)
        return w

    def ffn_pre(k):
        r = rows_of(k)
        middle = tok[r, :].astype(F32) + sum_finish(0, k)[:, 0:width] + out_bias[...]
        mid[r, :] = middle
        xhat, _ = norm(middle)
        n2[r, 0:width] = (xhat * ffn_gain[...] + ffn_bias[...]).astype(BF16)
        d_ffn = (grad[r, :].astype(F32) * weight_of(k)).astype(BF16)
        df[r, 0:width] = d_ffn
        add_sum(5, jnp.sum(d_ffn.astype(F32), axis=0, keepdims=True))

    def ffn_core(first, last):
        r = slice(first * BLOCK, last * BLOCK)

        def step(t, _):
            f = pl.ds(pl.multiple_of(t * FF_TILE, FF_TILE), FF_TILE)
            wu, wd = upt[f, :], down[f, :]
            x, g = n2[r, :], df[r, :]
            u = nt(x, wu) + up_bias[:, f]
            phi = 0.5 + 0.5 * lax.erf(u * (0.5**0.5))
            hid = (u * phi).astype(BF16)
            slope = phi + u * (jnp.exp(u * u * -0.5) * 0.3989422804014327)
            out = nn(hid, wd)
            du = (nt(g, wd) * slope).astype(BF16)
            dx = nn(du, wu)
            gu, gd = tn(du, x), tn(hid, g)
            dupb[:, f] += jnp.sum(du.astype(F32), axis=0, keepdims=True)

            @pl.when(t == 0)
            def _():
                facc[r, :] = out
                dn2[r, :] = dx

            @pl.when(t > 0)
            def _():
                facc[r, :] += out
                dn2[r, :] += dx

            if first == 0:
                gup[f, :] = gu
                gdown[f, :] = gd
            else:
                gup[f, :] += gu
                gdown[f, :] += gd
            return 0

        lax.fori_loop(0, upt.shape[0] // FF_TILE, step, 0)

    def ffn_post(k):
        r = rows_of(k)
        middle = mid[r, :]
        result[r, :] = (middle + facc[r, 0:width] + down_bias[...]).astype(BF16)
        g = dn2[r, 0:width]
        xhat, rstd = norm(middle)
        add_sum(3, jnp.sum(g * xhat, axis=0, keepdims=True))
        add_sum(4, jnp.sum(g, axis=0, keepdims=True))
        d_result = grad[r, :].astype(F32) * weight_of(k)
        d_middle = d_result + norm_back(g, ffn_gain[...], xhat, rstd)
        dtok[r, :] = d_middle
        low = d_middle.astype(BF16)
        da[k, h, :, 0:width] = low
        add_sum(2, jnp.sum(low.astype(F32), axis=0, keepdims=True))
        gather_start(1, da, k)

    for k in range(groups - 1):
        ffn_pre(k)
    ffn_core(0, groups - 1)
    for k in range(groups - 1):
        ffn_post(k)
    ffn_pre(groups - 1)
    ffn_core(groups - 1, groups)
    ffn_post(groups - 1)
    dup[...] = gup[...].astype(BF16)
    ddown[...] = gdown[...].astype(BF16)
    for k in range(groups):
        gather_sent(0, n1, k)
        sum_sent(0, k)

    def back_prep(k):
        def step(i, _):
            r = pl.ds(pl.multiple_of(i * BLOCK, BLOCK), BLOCK)
            g = nt(da[k, i], wo[...]).astype(BF16).astype(F32)
            g = (g * invl[k, r, :]).astype(BF16)
            do_s[r, :] = g
            dot_t[:, r] = g.astype(F32).T
            q_t[:, r] = q_s[k, r, :].astype(F32).T
            dwout[...] += tn(ctxb[k, r, :], da[k, i])
            return 0

        lax.fori_loop(0, steps, step, 0)
        dk_t[...] = jnp.zeros_like(dk_t)
        dv_t[...] = jnp.zeros_like(dv_t)

    def back(k, first, last):
        def step(i, _):
            n = k * steps + i
            slot = n % 2
            p_in(n).wait()
            r = pl.ds(pl.multiple_of(i * BLOCK, BLOCK), BLOCK)
            g = do_s[r, :].astype(F32)
            prod = g * ctx[k, r, :]
            keys, vals = k_s[k], v_s[k]
            at = lane(BLOCK)

            def d_prob(j):
                mine = head_lanes(BLOCK, j)
                inner = jnp.sum(jnp.where(mine, prod, 0.0), axis=1, keepdims=True)
                top = inner.astype(BF16).astype(F32)
                row = jnp.where(at == USED, -top, jnp.where(at == USED + 1, top - inner, 0.0))
                return nt(jnp.where(mine, g, row).astype(BF16), vals)

            acc = jnp.zeros((BLOCK, LANES), F32)
            dp = d_prob(0)
            for j in range(HEADS):
                later = d_prob(j + 1) if j + 1 < HEADS else None
                e = pslot[slot, j]
                ds = (e.astype(F32) * dp).astype(BF16)
                acc = jnp.where(head_lanes(BLOCK, j), nn(ds, keys), acc)
                hs = slice(j * HD, (j + 1) * HD)
                dk_t[hs, :] += nn(q_t[hs, r].astype(BF16), ds)
                dv_t[hs, :] += nn(dot_t[hs, r].astype(BF16), e)
                dp = later
            dq[r, :] = acc

            @pl.when(n + 2 < groups * steps)
            def _():
                p_in(n + 2).start()

            return 0

        lax.fori_loop(first, last, step, 0)

    def back_post(k):
        def step(i, _):
            r = pl.ds(pl.multiple_of(i * BLOCK, BLOCK), BLOCK)
            c, s = cos[r, :], sin[r, :]
            a = dq[r, :] * HD ** (-0.5)
            a = a * c - partner(a) * s
            b = dk_t[:, r].T * (1.0 / LOG2E)
            b = b * c - partner(b) * s
            g = jnp.concatenate([a, b, dv_t[:, r].T], axis=1).astype(BF16)
            dqkv[r, :] = g
            dqkvb[...] += jnp.sum(g.astype(F32), axis=0, keepdims=True)
            dwqkv[...] += tn(g, n1[k, i])
            return 0

        lax.fori_loop(0, steps, step, 0)

    def tokens_part(i):
        r = pl.ds(pl.multiple_of(i * BLOCK, BLOCK), BLOCK)
        return nt(dqkv[r, :], wq[...])

    def last_norm(k):
        r = rows_of(k)
        g = sum_finish(1, k)[:, 0:width]
        xhat, rstd = norm(tok[r, :].astype(F32))
        add_sum(0, jnp.sum(g * xhat, axis=0, keepdims=True))
        add_sum(1, jnp.sum(g, axis=0, keepdims=True))
        dtok[r, :] += norm_back(g, attn_gain[...], xhat, rstd)

    for k in range(groups - 1):
        gather_forward(1, da, k)
    for k in range(groups):
        gather_finish(1, da, k)
        back_prep(k)
        if k > 0:
            sum_forward(1, k - 1)
        if k == 0:
            back(k, 0, 1)
            gather_forward(1, da, groups - 1)
            back(k, 1, steps)
        else:
            back(k, 0, steps)
        back_post(k)
        sum_start(1, k, tokens_part)
    for k in range(groups - 1):
        last_norm(k)
    sum_forward(1, groups - 1)
    last_norm(groups - 1)
    for k in range(groups):
        gather_sent(1, da, k)
        sum_sent(1, k)


def permutation():
    table = np.zeros((3 * USED, 3 * LANES), np.float32)
    for j in range(HEADS):
        for part in range(3):
            for i in range(HD):
                table[(j * 3 + part) * HD + i, part * LANES + j * HD + i] = 1.0
    return table


def turns(group_rows):
    freq = 10000.0 ** (-2.0 * np.arange(HD // 2) / HD)
    angle = np.arange(group_rows)[:, None] * freq[None, :]
    c = np.zeros((group_rows, LANES), np.float32)
    s = np.zeros((group_rows, LANES), np.float32)
    c[:, :USED] = np.tile(np.cos(angle), (1, 2 * HEADS))
    s[:, :USED] = np.tile(np.concatenate([-np.sin(angle), np.sin(angle)], axis=1), (1, HEADS))
    return c, s


def layer(
    tokens, wqkv, wout, upt, down, attn_gain, attn_bias, qkv_bias, out_bias, ffn_gain,
    ffn_bias, up_bias, down_bias, lengths, ids, cw, grad,
):
    own, width = tokens.shape
    groups = lengths.shape[0]
    ff = up_bias.shape[0]
    group_rows = 4 * BLOCK
    c, s = turns(group_rows)
    vm = pl.BlockSpec(memory_space=pltpu.VMEM)
    sm = pl.BlockSpec(memory_space=pltpu.SMEM)
    anywhere = pl.BlockSpec(memory_space=pl.ANY)
    shape = jax.ShapeDtypeStruct
    row = lambda v: v.reshape(1, -1)
    v, dma = pltpu.VMEM, pltpu.SemaphoreType.DMA
    return pl.pallas_call(
        body,
        out_shape=(
            shape((own, width), BF16),
            shape((own, width), F32),
            shape((3 * LANES, 512), F32),
            shape((LANES, 512), F32),
            shape((ff, 512), BF16),
            shape((ff, 512), BF16),
            shape((8, 512), F32),
            shape((1, ff), F32),
            shape((1, 3 * LANES), F32),
            shape((groups, 4, HEADS, BLOCK, group_rows), BF16),
        ),
        in_specs=[vm] * 17 + [sm] * 3,
        out_specs=(vm,) * 9 + (anywhere,),
        scratch_shapes=[
            v((groups, 4, BLOCK, 512), BF16),
            v((512, 3 * LANES), BF16),
            v((LANES, 512), BF16),
            v((1, 3 * LANES), F32),
            v((groups, group_rows, LANES), BF16),
            v((groups, group_rows, LANES), BF16),
            v((groups, group_rows, LANES), BF16),
            v((groups, group_rows, LANES), F32),
            v((groups, group_rows, LANES), BF16),
            v((groups, group_rows, LANES), F32),
            v((2, HEADS, BLOCK, group_rows), BF16),
            v((groups, 2, BLOCK, 512), BF16),
            v((groups, 2, BLOCK, 512), BF16),
            v((groups, BLOCK, 512), BF16),
            v((groups, BLOCK, 512), BF16),
            v((groups, 2, BLOCK, 512), F32),
            v((own, width), F32),
            v((own, 512), BF16),
            v((own, 512), BF16),
            v((own, 512), F32),
            v((own, 512), F32),
            v((ff, 512), F32),
            v((ff, 512), F32),
            v((groups, 4, BLOCK, 512), BF16),
            v((group_rows, LANES), BF16),
            v((LANES, group_rows), F32),
            v((LANES, group_rows), F32),
            v((group_rows, LANES), F32),
            v((LANES, group_rows), F32),
            v((LANES, group_rows), F32),
            v((group_rows, 3 * LANES), BF16),
            dma((2, groups, 3)),
            dma((2, groups, 3)),
            dma((2, groups, 2)),
            dma((2, groups, 2)),
            dma((2,)),
        ],
        compiler_params=pltpu.CompilerParams(
            collective_id=0, has_side_effects=True, vmem_limit_bytes=62 * 2**20
        ),
        name="layer",
    )(
        tokens, grad, wqkv, wout, upt, down, row(attn_gain), row(attn_bias), row(qkv_bias),
        row(out_bias), row(ffn_gain), row(ffn_bias), row(up_bias), row(down_bias),
        jnp.asarray(permutation(), BF16), jnp.asarray(c), jnp.asarray(s), lengths, ids, cw,
    )


def local(
    tokens, attn_norm_gain, attn_norm_bias, qkv_weight, qkv_bias, out_weight, out_bias,
    ffn_norm_gain, ffn_norm_bias, up_weight, up_bias, down_weight, down_bias, lengths,
    cluster_ids, cluster_weight, grad_out,
):
    width = tokens.shape[1]
    ff = up_bias.shape[0]
    part = jnp.stack([up_weight.T, down_weight], axis=0)
    part = lax.all_gather(part, "dp", axis=1, tiled=True)
    part = lax.all_gather(part, "heads", axis=2, tiled=True)
    part = jnp.pad(part, ((0, 0), (0, 0), (0, 512 - width)))
    result, dtok, dwqkv, dwout, dup, ddown, sums, dupb, dqkvb, _ = layer(
        tokens, qkv_weight, out_weight, part[0], part[1], attn_norm_gain, attn_norm_bias,
        qkv_bias, out_bias, ffn_norm_gain, ffn_norm_bias, up_bias, down_bias, lengths,
        cluster_ids, cluster_weight, grad_out,
    )
    dwqkv, dwout, dqkvb = lax.psum((dwqkv, dwout, dqkvb), "dp")
    sums, dupb = lax.psum((sums, dupb), ("dp", "heads"))
    grads = jnp.stack([dup[:, :width], ddown[:, :width]], axis=0)
    grads = lax.psum_scatter(grads, "heads", scatter_dimension=2, tiled=True).astype(F32)
    grads = lax.psum_scatter(grads, "dp", scatter_dimension=1, tiled=True)
    dwqkv = dwqkv.reshape(3, LANES, 512)[:, :USED, :width].reshape(3, HEADS, HD, width)
    dwqkv = dwqkv.transpose(3, 1, 0, 2).reshape(width, 3 * USED)
    dqkvb = dqkvb.reshape(3, LANES)[:, :USED].reshape(3, HEADS, HD).transpose(1, 0, 2).reshape(-1)
    return (
        result, dtok, sums[0, :width], sums[1, :width], dwqkv, dqkvb, dwout[:USED, :width],
        sums[2, :width], sums[3, :width], sums[4, :width], grads[0].T, dupb.reshape(ff),
        grads[1], sums[5, :width],
    )


def solution(mesh):
    placed = (
        P(("dp", "heads"), None), P(), P(), P(None, "heads"), P("heads"), P("heads", None), P(),
        P(), P(), P("heads", "dp"), P(), P("dp", "heads"), P(), P("dp", None), P("dp", None),
        P(), P(("dp", "heads"), None),
    )
    given = (
        P(("dp", "heads"), None), P(("dp", "heads"), None), P(), P(), P(None, "heads"), P("heads"),
        P("heads", None), P(), P(), P(), P("heads", "dp"), P(), P("dp", "heads"), P(),
    )
    return jax.shard_map(local, mesh=mesh, in_specs=placed, out_specs=given, check_vma=False)
```

```python
from functools import partial

import jax
import jax.numpy as jnp
import numpy as np
from jax import lax
from jax.experimental import pallas as pl
from jax.experimental.pallas import tpu as pltpu
from jax.sharding import PartitionSpec as P

F32, BF16 = jnp.float32, jnp.bfloat16
MESH = pl.DeviceIdType.MESH
HD = 24
HEADS = 5
USED = HEADS * HD
LANES = 128
EPSILON = 1e-05
LOG2E = 1.4426950408889634
BIG = 1e30
BLOCK = 256


def dims(a, b, ca, cb, precision=None):
    return lax.dot_general(
        a, b, (((ca,), (cb,)), ((), ())), preferred_element_type=F32, precision=precision
    )


def nn(a, b):
    return dims(a, b, 1, 0)


def nt(a, b):
    return dims(a, b, 1, 1)


def tn(a, b):
    return dims(a, b, 0, 0)


def lane(rows, width=LANES):
    return lax.broadcasted_iota(jnp.int32, (rows, width), 1)


def head_lanes(rows, j):
    at = lane(rows)
    return (at >= HD * j) & (at < HD * (j + 1))


def partner(x):
    at = lane(x.shape[0])
    half = HD // 2
    return jnp.where(
        at % HD < half, pltpu.roll(x, LANES - half, 1), pltpu.roll(x, half, 1)
    )


def norm(x):
    centred = x - jnp.mean(x, axis=-1, keepdims=True)
    rstd = lax.rsqrt(jnp.mean(centred * centred, axis=-1, keepdims=True) + EPSILON)
    return centred * rstd, rstd


def norm_back(g, gain, xhat, rstd):
    n = g * gain
    return rstd * (
        n
        - jnp.mean(n, axis=-1, keepdims=True)
        - xhat * jnp.mean(n * xhat, axis=-1, keepdims=True)
    )


def body(
    inner, tok, grad, wqkv, wout, w_in, attn_gain, attn_bias, qkv_bias, out_bias, ffn_gain,
    ffn_bias, up_bias, down_bias, perm, spread, cos, sin, lengths, ids, cw,
    result, dtok, d_first, small, phbm,
    n1, wq, wo, qkv_b, q_s, k_s, v_s, ctx, ctxb, invl, pslot,
    rs_core_out, rs_core_in, rs_y_out, rs_y_in, rs_own,
    mid, n2, df, n2p, dfp, facc, dn2, wup, wdown, da, do_s, dot_t, q_t, dq, dk_t, dv_t, dqkv,
    sums, acc, ag_s, ag_r, rs_s, rs_r, p_s, remote,
):
    d, h = lax.axis_index("dp"), lax.axis_index("heads")
    core, y = h % 2, h // 2
    h_sib = h + 1 - 2 * core
    h_y = (h + 2) % 4
    sib, ypart = (d, h_sib), (d, h_y)
    groups = lengths.shape[0]
    width = tok.shape[1]
    group_rows = 4 * BLOCK
    steps = 4

    def send(src, dst, s, r, to):
        return pltpu.make_async_remote_copy(
            src_ref=src, dst_ref=dst, send_sem=s, recv_sem=r, device_id=to, device_id_type=MESH
        )

    def gather_copy(use, buf, k, n):
        block, to = ((h, sib), (h, ypart), (h_y, sib))[n]
        return send(
            buf.at[k, block], buf.at[k, block], ag_s.at[use, k, n], ag_r.at[use, k, n], to
        )

    def gather_start(use, buf, k):
        gather_copy(use, buf, k, 1).start()
        gather_copy(use, buf, k, 0).start()

    def gather_forward(use, buf, k):
        gather_copy(use, buf, k, 1).wait_recv()
        gather_copy(use, buf, k, 2).start()

    def gather_finish(use, buf, k):
        gather_copy(use, buf, k, 0).wait_recv()
        gather_copy(use, buf, k, 2).wait_recv()

    def gather_sent(use, buf, k):
        for n in range(3):
            gather_copy(use, buf, k, n).wait_send()

    def sum_copy(use, k, n):
        src, dst, to = ((rs_core_out, rs_core_in, sib), (rs_y_out, rs_y_in, ypart))[n]
        return send(src.at[k], dst.at[k], rs_s.at[use, k, n], rs_r.at[use, k, n], to)

    def sum_start(use, k, part):
        for other in (0, 1):
            rs_core_out[k, other] = part(2 * other + 1 - core).astype(BF16)
        sum_copy(use, k, 0).start()
        rs_y_out[k] = part(2 * (1 - y) + core).astype(BF16)
        rs_own[k] = part(h)

    def sum_forward(use, k):
        sum_copy(use, k, 0).wait_recv()
        rs_y_out[k] = (rs_y_out[k].astype(F32) + rs_core_in[k, 1 - y].astype(F32)).astype(BF16)
        sum_copy(use, k, 1).start()

    def sum_finish(use, k):
        sum_copy(use, k, 1).wait_recv()
        return rs_own[k] + rs_core_in[k, y].astype(F32) + rs_y_in[k].astype(F32)

    def sum_sent(use, k):
        for n in range(2):
            sum_copy(use, k, n).wait_send()

    if inner:
        (g, rc, rx, rz, ry, wsum, wall, wres, heads_in, dp_out, dp_in,
         w_s, w_r, c_s, c_r, f_s, f_r, m_s, m_r) = remote
        wup_in, wdown_in = w_in
        dwqkv, dwout, dup, ddown = d_first
        gw = gg = g
        z, x = d // 2, d % 2
        xpart, above, below = (d + 1 - 2 * x, h), (d + 2, h), (d - 2, h)
        peers = [lax.rem(d + n, 8) for n in range(1, 8)]
        greeted = [sib, ypart, (d, (h_sib + 2) % 4)] + [(p, h) for p in peers]
    else:
        gw, (acc_out, gg) = w_in[0], d_first
        greeted = [sib, ypart]

    def w_y():
        block = g.at[core, z, x, y]
        return send(block, block, w_s.at[0], w_r.at[0], ypart)

    def w_up(s, origin):
        pair = g.at[core, origin, x]
        return send(pair, pair, w_s.at[s], w_r.at[s], above)

    def w_down(s, origin):
        pair = g.at[core, origin, x]
        return send(pair, pair, w_s.at[3 + s], w_r.at[3 + s], below)

    def w_x(origin, side):
        pair = g.at[core, origin, side]
        return send(pair, pair, w_s.at[7 + origin], w_r.at[7 + origin], xpart)

    def w_core(origin, side, at):
        pair = g.at[at, origin, side]
        n = 11 + 2 * origin + side
        return send(pair, pair, w_s.at[n], w_r.at[n], sib)

    def w_begin():
        g[core, z, x, y] = jnp.zeros((480, LANES), BF16)
        g[core, z, x, y, 0:240, 0:USED] = wup_in[...].astype(F32).T.astype(BF16)
        g[core, z, x, y, 240:480, 0:USED] = wdown_in[...]
        w_y().start()

    def w_here(origin):
        w_x(origin, x).start()
        w_core(origin, x, core).start()

    def w_first():
        w_y().wait_recv()

        @pl.when(z < 3)
        def _():
            w_up(1, z).start()

        @pl.when(z > 0)
        def _():
            w_down(1, z).start()

        w_here(z)

    def w_step(s):
        @pl.when(z >= s)
        def _():
            w_up(s, z - s).wait_recv()
            if s < 3:

                @pl.when(z < 3)
                def _():
                    w_up(s + 1, z - s).start()

            w_here(z - s)

        @pl.when(z + s <= 3)
        def _():
            w_down(s, z + s).wait_recv()
            if s < 3:

                @pl.when(z > 0)
                def _():
                    w_down(s + 1, z + s).start()

            w_here(z + s)

    def w_other(s):
        def one(origin):
            w_x(origin, 1 - x).wait_recv()
            w_core(origin, 1 - x, core).start()

        if s == 0:
            one(z)
        else:
            pl.when(z >= s)(lambda: one(z - s))
            pl.when(z + s <= 3)(lambda: one(z + s))

    def w_end():
        for origin in range(4):
            for side in (0, 1):
                w_core(origin, side, 1 - core).wait_recv()

    def w_sent():
        w_y().wait_send()
        for s in (1, 2, 3):
            pl.when((z >= s - 1) & (z < 3))(lambda: w_up(s, z - s + 1).wait_send())
            pl.when((z + s - 1 <= 3) & (z > 0))(lambda: w_down(s, z + s - 1).wait_send())
        for origin in range(4):
            w_x(origin, x).wait_send()
            for side in (0, 1):
                w_core(origin, side, core).wait_send()

    def assemble():
        def step(i, _):
            parts = [gw[n % 2, i // 2, i % 2, n // 2] for n in range(4)]
            full = nn(jnp.concatenate(parts, axis=1), spread[...]).astype(BF16)
            r = pl.ds(pl.multiple_of(i * 240, 240), 240)
            wup[r, :] = full[0:240]
            wdown[r, :] = full[240:480]
            return 0

        lax.fori_loop(0, 8, step, 0)

    order = (3, 0, 2, 1)

    def g_core(origin):
        return send(
            g.at[1 - core, origin], rc.at[origin], c_s.at[origin], c_r.at[origin], sib
        )

    def g_x(origin):
        return send(
            g.at[core, origin, 1 - x], rx.at[origin], c_s.at[4 + origin], c_r.at[4 + origin], xpart
        )

    def g_up(s, to):
        return send(g.at[core, to, x], rz.at[0, s - 1], c_s.at[7 + s], c_r.at[7 + s], above)

    def g_down(s, to):
        return send(g.at[core, to, x], rz.at[1, s - 1], c_s.at[10 + s], c_r.at[10 + s], below)

    def g_y():
        return send(g.at[core, z, x, 1 - y], ry, c_s.at[14], c_r.at[14], ypart)

    def add_pair(origin, side, ref):
        for n in (0, 1):
            g[core, origin, side, n] = (
                g[core, origin, side, n].astype(F32) + ref[n].astype(F32)
            ).astype(BF16)

    def g_begin():
        for origin in order:
            g_core(origin).start()

    def g_first():
        for origin in order:
            g_core(origin).wait_recv()
            add_pair(origin, 1 - x, rc.at[origin, 1 - x])
            g_x(origin).start()
        for origin in order:
            add_pair(origin, x, rc.at[origin, x])

    def g_add_x(origins):
        for origin in origins:
            g_x(origin).wait_recv()
            add_pair(origin, x, rx.at[origin])

    def g_send(s):
        pl.when(z < s)(lambda: g_up(s, 4 - s + z).start())
        pl.when(3 - z < s)(lambda: g_down(s, s + z - 4).start())

    def g_recv(s):
        @pl.when((z >= 1) & (z <= s))
        def _():
            g_up(s, 0).wait_recv()
            add_pair(3 - s + z, x, rz.at[0, s - 1])

        @pl.when((z <= 2) & (z >= 3 - s))
        def _():
            g_down(s, 0).wait_recv()
            add_pair(s + z - 3, x, rz.at[1, s - 1])

    def g_last():
        g_y().wait_recv()
        total = g[core, z, x, y].astype(F32) + ry[...].astype(F32)
        dup[...] = total[0:240].T[0:USED]
        ddown[...] = total[240:480, 0:USED]
        for n in range(4):
            g_core(n).wait_send()
            g_x(n).wait_send()
        for s in (1, 2, 3):
            pl.when(z < s)(lambda: g_up(s, 0).wait_send())
            pl.when(3 - z < s)(lambda: g_down(s, 0).wait_send())
        g_y().wait_send()

    spans = ((384, 512), (256, 384), (0, 256))

    def slot_of(n):
        first, last = spans[n]
        size = (last - first) // 8
        return first, size

    def f_part(n, p):
        first, size = slot_of(n)
        return pl.ds(pl.multiple_of(first + p * size, 16), size)

    def f_in(n, p):
        first, size = slot_of(n)
        return pl.ds(pl.multiple_of(first + p * size, 16), size)

    def f_out_copy(n, p):
        return send(
            wall.at[f_part(n, p)], wsum.at[f_in(n, d)], f_s.at[0, n, p], f_r.at[0, n, d], (p, h)
        )

    def f_in_copy(n, p):
        return send(
            wall.at[f_part(n, p)], wsum.at[f_in(n, p)], f_s.at[0, n, p], f_r.at[0, n, p], (p, h)
        )

    def f_back_copy(n, p, at):
        return send(
            wres.at[f_part(n, at)], wres.at[f_part(n, at)], f_s.at[1, n, p], f_r.at[1, n, at], (p, h)
        )

    def f_begin(n):
        first, last = spans[n]
        wall[first:last, :] = acc[first:last, :].astype(BF16)
        wsum[f_in(n, d), :] = wall[f_part(n, d), :]
        for p in peers:
            f_out_copy(n, p).start()

    def f_back(n):
        first, size = slot_of(n)
        for p in peers:
            f_in_copy(n, p).wait_recv()
        total = jnp.zeros((size, 512), F32)
        for p in range(8):
            total = total + wsum[first + p * size : first + (p + 1) * size, :].astype(F32)
        wres[f_part(n, d), :] = total.astype(BF16)
        for p in peers:
            f_back_copy(n, p, d).start()

    def f_end(n):
        for p in peers:
            f_back_copy(n, p, p).wait_recv()

    def f_sent(n):
        for p in peers:
            f_out_copy(n, p).wait_send()
            f_back_copy(n, p, d).wait_send()

    near = (sib, ypart, (d, (h_sib + 2) % 4))

    def m_heads(b, n, at):
        return send(sums.at[b], heads_in.at[b, at], m_s.at[b, n], m_r.at[b, at], near[n])

    def m_dp(b, n, at):
        return send(
            dp_out.at[b], dp_in.at[b, at], m_s.at[b, 3 + n], m_r.at[b, 4 + at], (peers[n], h)
        )

    def m_begin(b):
        heads_in[b, h] = sums[b]
        for n in range(3):
            m_heads(b, n, h).start()

    def m_middle(b):
        for n in range(3):
            m_heads(b, n, near[n][1]).wait_recv()
        total = heads_in[b, 0] + heads_in[b, 1] + heads_in[b, 2] + heads_in[b, 3]
        if b == 0:
            row = lax.broadcasted_iota(jnp.int32, total.shape, 0)
            total = jnp.where(row == 2, sums[b], total)
        dp_out[b] = total
        dp_in[b, d] = total
        for n in range(7):
            m_dp(b, n, d).start()

    def m_end(b):
        for n in range(7):
            m_dp(b, n, peers[n]).wait_recv()
        total = dp_in[b, 0]
        for p in range(1, 8):
            total = total + dp_in[b, p]
        small[8 * b : 8 * b + 8, :] = total
        for n in range(3):
            m_heads(b, n, h).wait_send()
        for n in range(7):
            m_dp(b, n, d).wait_send()

    def rows_of(k):
        return slice(k * BLOCK, (k + 1) * BLOCK)

    def add_sum(row, value):
        b, at = row // 8, row % 8
        sums[b, at : at + 1, 0 : value.shape[1]] += value

    barrier = pltpu.get_barrier_semaphore()
    for other in greeted:
        pl.semaphore_signal(barrier, inc=1, device_id=other, device_id_type=MESH)

    def first_norm(k):
        xhat, _ = norm(tok[rows_of(k), :].astype(F32))
        n1[k, h, :, 0:width] = (xhat * attn_gain[...] + attn_bias[...]).astype(BF16)
        n1[k, h, :, width:512] = jnp.zeros((BLOCK, 512 - width), BF16)

    first_norm(0)
    pl.semaphore_wait(barrier, len(greeted))
    gather_start(0, n1, 0)
    if inner:
        w_begin()
    for k in range(1, groups):
        first_norm(k)
        gather_start(0, n1, k)

    wq[0:width, :] = nn(wqkv[...], perm[...]).astype(BF16)
    wq[width:512, :] = jnp.zeros((512 - width, 3 * LANES), BF16)
    qkv_b[...] = dims(qkv_bias[...], perm[...].astype(F32), 1, 0, lax.Precision.HIGHEST)
    wo[:, width:512] = jnp.zeros((LANES, 512 - width), BF16)
    wo[:, 0:width] = jnp.concatenate(
        [wout[...].astype(F32), jnp.zeros((LANES - USED, width), F32)], axis=0
    ).astype(BF16)
    sums[...] = jnp.zeros_like(sums)
    acc[...] = jnp.zeros_like(acc)
    n2[:, width:512] = jnp.zeros((groups * BLOCK, 512 - width), BF16)
    df[:, width:512] = jnp.zeros((groups * BLOCK, 512 - width), BF16)
    for k in range(groups):
        da[k, h, :, width:512] = jnp.zeros((BLOCK, 512 - width), BF16)

    def ends_of(k):
        total, ends = 0, []
        for p in range(4):
            total = total + lengths[k, p]
            ends.append(total)
        return ends

    def project(k):
        ends = ends_of(k)
        at1 = lane(1)
        lo = jnp.where(at1 == USED, 0, group_rows + 1)
        hi = jnp.where(at1 == USED + 4, group_rows + 1, 0)
        for p in range(4):
            lo = jnp.where(at1 == USED + 1 + p, ends[p], lo)
            hi = jnp.where(at1 == USED + p, ends[p], hi)

        def step(i, _):
            r = pl.ds(pl.multiple_of(i * BLOCK, BLOCK), BLOCK)
            x_ = nn(n1[k, i], wq[...]) + qkv_b[...]
            c, s = cos[r, :], sin[r, :]
            at = lane(BLOCK)
            row = lax.broadcasted_iota(jnp.int32, (BLOCK, LANES), 0) + i * BLOCK
            inside = (row >= lo) & (row < hi)
            marks = (at >= USED) & (at < USED + 5)
            q = x_[:, 0:LANES]
            q = (q * c + partner(q) * s) * (HD ** (-0.5) * LOG2E)
            q_s[k, r, :] = jnp.where(at < USED, q, jnp.where(inside, 1.0, 0.0)).astype(BF16)
            key = x_[:, LANES : 2 * LANES]
            key = key * c + partner(key) * s
            k_s[k, r, :] = jnp.where(
                at < USED, key, jnp.where(marks & jnp.logical_not(inside), -BIG, 0.0)
            ).astype(BF16)
            v_s[k, r, :] = jnp.where(
                at < USED, x_[:, 2 * LANES : 3 * LANES], jnp.where(at < USED + 2, 1.0, 0.0)
            ).astype(BF16)
            return 0

        lax.fori_loop(0, steps, step, 0)

    def p_out(k, i):
        slot = (k * steps + i) % 2
        return pltpu.make_async_copy(pslot.at[slot], phbm.at[k, i], p_s.at[slot])

    def p_in(n):
        slot = n % 2
        return pltpu.make_async_copy(phbm.at[n // steps, n % steps], pslot.at[slot], p_s.at[slot])

    def run_hooks(hooks, i):
        for at, todo in hooks.items():

            @pl.when(i == at)
            def _():
                for one in todo:
                    one()

    def attend(k, hooks):
        def step(i, _):
            n = k * steps + i
            slot = n % 2
            run_hooks(hooks, i)

            @pl.when(n >= 2)
            def _():
                p_out(k, i).wait()

            r = pl.ds(pl.multiple_of(i * BLOCK, BLOCK), BLOCK)
            q = q_s[k, r, :]
            keys, vals = k_s[k], v_s[k]
            at = lane(BLOCK)

            def score(j):
                return nt(jnp.where(head_lanes(BLOCK, j) | (at >= USED), q, 0), keys)

            out = jnp.zeros((BLOCK, LANES), F32)
            inv = jnp.zeros((BLOCK, LANES), F32)
            s = score(0)
            for j in range(HEADS):
                later = score(j + 1) if j + 1 < HEADS else None
                e = jnp.exp2(s - jnp.max(s, axis=1, keepdims=True)).astype(BF16)
                pslot[slot, j] = e
                o = nn(e, vals)
                one = 1.0 / o[:, USED : USED + 1]
                out = jnp.where(head_lanes(BLOCK, j), o * one, out)
                inv = jnp.where(head_lanes(BLOCK, j), one, inv)
                s = later
            ctx[k, r, :] = out
            ctxb[k, r, :] = out.astype(BF16)
            invl[k, r, :] = inv
            p_out(k, i).start()
            return 0

        lax.fori_loop(0, steps, step, 0)

    def out_part(k):
        def part(i):
            r = pl.ds(pl.multiple_of(i * BLOCK, BLOCK), BLOCK)
            return nn(ctxb[k, r, :], wo[...])

        return part

    gather_forward(0, n1, 0)
    for k in range(groups):
        gather_finish(0, n1, k)
        project(k)
        if k > 0:
            sum_forward(0, k - 1)
        hooks = {}
        if k + 1 < groups:
            hooks[3] = [partial(gather_forward, 0, n1, k + 1)]
        if inner:
            if k == 0:
                hooks[0] = [w_first]
                hooks[3] += [partial(w_step, 1), partial(w_other, 0)]
            if k == 1:
                hooks[2] = [partial(w_step, 2), partial(w_other, 1)]
            if k == 2:
                hooks[0] = [partial(w_step, 3), partial(w_other, 2)]
                hooks[3] = [partial(w_other, 3)]
        attend(k, hooks)
        sum_start(0, k, out_part(k))
    sum_forward(0, groups - 1)
    for n in (groups * steps, groups * steps + 1):
        p_in(n % 2).wait()
    p_in(0).start()
    p_in(1).start()
    if inner:
        w_end()
    assemble()
    if inner:
        w_sent()

    def weight_of(k):
        ends = ends_of(k)
        row = lax.broadcasted_iota(jnp.int32, (BLOCK, 1), 0) + h * BLOCK
        w = jnp.zeros((BLOCK, 1), F32)
        for p in reversed(range(4)):
            w = jnp.where(row < ends[p], cw[ids[k, p]], w)
        return w

    def ffn_pre(k):
        r = rows_of(k)
        middle = tok[r, :].astype(F32) + sum_finish(0, k)[:, 0:width] + out_bias[...]
        mid[r, :] = middle
        xhat, _ = norm(middle)
        n2[r, 0:width] = (xhat * ffn_gain[...] + ffn_bias[...]).astype(BF16)
        d_ffn = (grad[r, :].astype(F32) * weight_of(k)).astype(BF16)
        df[r, 0:width] = d_ffn
        add_sum(15, jnp.sum(d_ffn.astype(F32), axis=0, keepdims=True))
        n2p[r, :] = nt(n2[r, :], spread[...]).astype(BF16)
        dfp[r, :] = nt(df[r, :], spread[...]).astype(BF16)

    def ffn_core(first, last):
        r = slice(first * BLOCK, last * BLOCK)

        def step(t, _):
            f = pl.ds(pl.multiple_of(t * 480, 480), 480)
            wu, wd = wup[f, :], wdown[f, :]
            u = nt(n2[r, :], wu) + up_bias[pl.ds(t, 1), :]
            phi = 0.5 + 0.5 * lax.erf(u * (0.5**0.5))
            hid = (u * phi).astype(BF16)
            slope = phi + u * (jnp.exp(u * u * -0.5) * 0.3989422804014327)
            out = nn(hid, wd)
            du = (nt(df[r, :], wd) * slope).astype(BF16)
            dx = nn(du, wu)
            sums[1, pl.ds(t, 1), 0:480] += jnp.sum(du.astype(F32), axis=0, keepdims=True)

            @pl.when(t == 0)
            def _():
                facc[r, :] = out
                dn2[r, :] = dx

            @pl.when(t > 0)
            def _():
                facc[r, :] += out
                dn2[r, :] += dx

            for part, wide in enumerate((tn(du, n2p[r, :]), tn(hid, dfp[r, :]))):
                fr = slice(part * 240, part * 240 + 240)
                for side in (0, 1):
                    for n in range(4):
                        new = wide[side * 240 : side * 240 + 240, n * LANES : (n + 1) * LANES]
                        if first > 0:
                            new = new + gg[n % 2, t, side, n // 2, fr, :].astype(F32)
                        gg[n % 2, t, side, n // 2, fr, :] = new.astype(BF16)
            return 0

        lax.fori_loop(0, 4, step, 0)

    def ffn_post(k):
        r = rows_of(k)
        middle = mid[r, :]
        result[r, :] = (middle + facc[r, 0:width] + down_bias[...]).astype(BF16)
        g_ = dn2[r, 0:width]
        xhat, rstd = norm(middle)
        add_sum(13, jnp.sum(g_ * xhat, axis=0, keepdims=True))
        add_sum(14, jnp.sum(g_, axis=0, keepdims=True))
        d_result = grad[r, :].astype(F32) * weight_of(k)
        d_middle = d_result + norm_back(g_, ffn_gain[...], xhat, rstd)
        dtok[r, :] = d_middle
        low = d_middle.astype(BF16)
        da[k, h, :, 0:width] = low
        add_sum(12, jnp.sum(low.astype(F32), axis=0, keepdims=True))
        gather_start(1, da, k)

    for k in range(groups - 1):
        ffn_pre(k)
    ffn_core(0, groups - 1)
    for k in range(groups - 1):
        ffn_post(k)
    ffn_pre(groups - 1)
    ffn_core(groups - 1, groups)
    if inner:
        g_begin()
    ffn_post(groups - 1)
    if inner:
        m_begin(1)
    for k in range(groups):
        gather_sent(0, n1, k)
        sum_sent(0, k)

    def back_prep(k):
        def step(i, _):
            r = pl.ds(pl.multiple_of(i * BLOCK, BLOCK), BLOCK)
            g_ = nt(da[k, i], wo[...]).astype(BF16).astype(F32)
            g_ = (g_ * invl[k, r, :]).astype(BF16)
            do_s[r, :] = g_
            dot_t[:, r] = g_.astype(F32).T
            q_t[:, r] = q_s[k, r, :].astype(F32).T
            acc[3 * LANES : 4 * LANES, :] += tn(ctxb[k, r, :], da[k, i])
            return 0

        lax.fori_loop(0, steps, step, 0)
        dk_t[...] = jnp.zeros_like(dk_t)
        dv_t[...] = jnp.zeros_like(dv_t)

    def back(k, hooks):
        def step(i, _):
            n = k * steps + i
            slot = n % 2
            run_hooks(hooks, i)
            p_in(n).wait()
            r = pl.ds(pl.multiple_of(i * BLOCK, BLOCK), BLOCK)
            g_ = do_s[r, :].astype(F32)
            prod = g_ * ctx[k, r, :]
            keys, vals = k_s[k], v_s[k]
            at = lane(BLOCK)

            def d_prob(j):
                mine = head_lanes(BLOCK, j)
                total = jnp.sum(jnp.where(mine, prod, 0.0), axis=1, keepdims=True)
                top = total.astype(BF16).astype(F32)
                row = jnp.where(at == USED, -top, jnp.where(at == USED + 1, top - total, 0.0))
                return nt(jnp.where(mine, g_, row).astype(BF16), vals)

            out = jnp.zeros((BLOCK, LANES), F32)
            dp = d_prob(0)
            for j in range(HEADS):
                later = d_prob(j + 1) if j + 1 < HEADS else None
                e = pslot[slot, j]
                ds = (e.astype(F32) * dp).astype(BF16)
                out = jnp.where(head_lanes(BLOCK, j), nn(ds, keys), out)
                hs = slice(j * HD, (j + 1) * HD)
                dk_t[hs, :] += nn(q_t[hs, r].astype(BF16), ds)
                dv_t[hs, :] += nn(dot_t[hs, r].astype(BF16), e)
                dp = later
            dq[r, :] = out

            @pl.when(n + 2 < groups * steps)
            def _():
                p_in(n + 2).start()

            return 0

        lax.fori_loop(0, steps, step, 0)

    def back_post(k):
        def step(i, _):
            r = pl.ds(pl.multiple_of(i * BLOCK, BLOCK), BLOCK)
            c, s = cos[r, :], sin[r, :]
            a = dq[r, :] * HD ** (-0.5)
            a = a * c - partner(a) * s
            b = dk_t[:, r].T * (1.0 / LOG2E)
            b = b * c - partner(b) * s
            g_ = jnp.concatenate([a, b, dv_t[:, r].T], axis=1).astype(BF16)
            dqkv[r, :] = g_
            add_sum(2, jnp.sum(g_.astype(F32), axis=0, keepdims=True))
            acc[0 : 3 * LANES, :] += tn(g_, n1[k, i])
            return 0

        lax.fori_loop(0, steps, step, 0)

    def tokens_part(i):
        r = pl.ds(pl.multiple_of(i * BLOCK, BLOCK), BLOCK)
        return nt(dqkv[r, :], wq[...])

    def last_norm(k):
        r = rows_of(k)
        g_ = sum_finish(1, k)[:, 0:width]
        xhat, rstd = norm(tok[r, :].astype(F32))
        add_sum(0, jnp.sum(g_ * xhat, axis=0, keepdims=True))
        add_sum(1, jnp.sum(g_, axis=0, keepdims=True))
        dtok[r, :] += norm_back(g_, attn_gain[...], xhat, rstd)

    for k in range(groups - 1):
        gather_forward(1, da, k)
    for k in range(groups):
        gather_finish(1, da, k)
        back_prep(k)
        if k > 0:
            sum_forward(1, k - 1)
        hooks = {}
        if k == 0:
            hooks[1] = [partial(gather_forward, 1, da, groups - 1)]
        if inner:
            if k == 0:
                hooks[0] = [g_first, partial(m_middle, 1)]
            if k == 1:
                hooks[0] = [partial(g_add_x, order[:2]), partial(g_send, 1), partial(m_end, 1)]
                hooks[3] = [partial(g_add_x, order[2:]), partial(g_recv, 1), partial(g_send, 2)]
            if k == 2:
                hooks[0] = [partial(f_begin, 0)]
                hooks[1] = [partial(g_recv, 2), partial(g_send, 3)]
                hooks[2] = [partial(f_back, 0)]
                hooks[3] = [partial(g_recv, 3), g_y().start]
        back(k, hooks)
        back_post(k)
        if inner and k == groups - 1:
            f_begin(1)
            f_begin(2)
        sum_start(1, k, tokens_part)
    for k in range(groups - 1):
        last_norm(k)
    sum_forward(1, groups - 1)
    if inner:
        f_back(1)
        f_back(2)
    last_norm(groups - 1)
    if inner:
        m_begin(0)
        g_last()
        m_middle(0)
        for n in range(3):
            f_end(n)
        dwqkv[...] = dims(wres[0 : 3 * LANES, :], perm[...], 0, 1)[0:width]
        dwout[...] = wres[3 * LANES : 4 * LANES, :].astype(F32)[0:USED, 0:width]
        m_end(0)
        for n in range(3):
            f_sent(n)
    else:
        small[0:8, :] = sums[0]
        small[8:16, :] = sums[1]
        acc_out[...] = acc[...]
    for k in range(groups):
        gather_sent(1, da, k)
        sum_sent(1, k)


def permutation():
    table = np.zeros((3 * USED, 3 * LANES), np.float32)
    for j in range(HEADS):
        for part in range(3):
            for i in range(HD):
                table[(j * 3 + part) * HD + i, part * LANES + j * HD + i] = 1.0
    return table


def turns(group_rows):
    freq = 10000.0 ** (-2.0 * np.arange(HD // 2) / HD)
    angle = np.arange(group_rows)[:, None] * freq[None, :]
    c = np.zeros((group_rows, LANES), np.float32)
    s = np.zeros((group_rows, LANES), np.float32)
    c[:, :USED] = np.tile(np.cos(angle), (1, 2 * HEADS))
    s[:, :USED] = np.tile(np.concatenate([-np.sin(angle), np.sin(angle)], axis=1), (1, HEADS))
    return c, s


def spreading():
    table = np.zeros((4 * LANES, 4 * LANES), np.float32)
    for n in range(4):
        for i in range(USED):
            table[n * LANES + i, n * USED + i] = 1.0
    return table


def layer(
    inner, tokens, wqkv, wout, w_in, attn_gain, attn_bias, qkv_bias, out_bias, ffn_gain,
    ffn_bias, up_bias, down_bias, lengths, ids, cw, grad,
):
    own, width = tokens.shape
    groups = lengths.shape[0]
    ff = up_bias.shape[0]
    group_rows = 4 * BLOCK
    c, s = turns(group_rows)
    vm = pl.BlockSpec(memory_space=pltpu.VMEM)
    sm = pl.BlockSpec(memory_space=pltpu.SMEM)
    anywhere = pl.BlockSpec(memory_space=pl.ANY)
    shape = jax.ShapeDtypeStruct
    row = lambda v: v.reshape(1, -1)
    v, dma = pltpu.VMEM, pltpu.SemaphoreType.DMA
    chunks = (2, 4, 2, 2, 480, LANES)
    if inner:
        first = (
            shape((width, 3 * USED), F32),
            shape((USED, width), F32),
            shape((USED, 240), F32),
            shape((240, USED), F32),
        )
        remote = [
            v(chunks, BF16),
            v((4, 2, 2, 480, LANES), BF16),
            v((4, 2, 480, LANES), BF16),
            v((2, 3, 2, 480, LANES), BF16),
            v((480, LANES), BF16),
            v((4 * LANES, 512), BF16),
            v((4 * LANES, 512), BF16),
            v((4 * LANES, 512), BF16),
            v((2, 4, 8, 512), F32),
            v((2, 8, 512), F32),
            v((2, 8, 8, 512), F32),
            dma((19,)),
            dma((19,)),
            dma((15,)),
            dma((15,)),
            dma((2, 3, 8)),
            dma((2, 3, 8)),
            dma((2, 10)),
            dma((2, 12)),
        ]
    else:
        first = (shape((4 * LANES, 512), F32), shape(chunks, BF16))
        remote = []
    return pl.pallas_call(
        partial(body, inner),
        out_shape=(
            shape((own, width), BF16),
            shape((own, width), F32),
            first,
            shape((16, 512), F32),
            shape((groups, 4, HEADS, BLOCK, group_rows), BF16),
        ),
        in_specs=[vm] * 4 + [[vm] * len(w_in)] + [vm] * 12 + [sm] * 3,
        out_specs=(vm, vm, (vm,) * len(first), vm, anywhere),
        scratch_shapes=[
            v((groups, 4, BLOCK, 512), BF16),
            v((512, 3 * LANES), BF16),
            v((LANES, 512), BF16),
            v((1, 3 * LANES), F32),
            v((groups, group_rows, LANES), BF16),
            v((groups, group_rows, LANES), BF16),
            v((groups, group_rows, LANES), BF16),
            v((groups, group_rows, LANES), F32),
            v((groups, group_rows, LANES), BF16),
            v((groups, group_rows, LANES), F32),
            v((2, HEADS, BLOCK, group_rows), BF16),
            v((groups, 2, BLOCK, 512), BF16),
            v((groups, 2, BLOCK, 512), BF16),
            v((groups, BLOCK, 512), BF16),
            v((groups, BLOCK, 512), BF16),
            v((groups, BLOCK, 512), F32),
            v((own, width), F32),
            v((own, 512), BF16),
            v((own, 512), BF16),
            v((own, 512), BF16),
            v((own, 512), BF16),
            v((own, 512), F32),
            v((own, 512), F32),
            v((ff, 512), BF16),
            v((ff, 512), BF16),
            v((groups, 4, BLOCK, 512), BF16),
            v((group_rows, LANES), BF16),
            v((LANES, group_rows), F32),
            v((LANES, group_rows), F32),
            v((group_rows, LANES), F32),
            v((LANES, group_rows), F32),
            v((LANES, group_rows), F32),
            v((group_rows, 3 * LANES), BF16),
            v((2, 8, 512), F32),
            v((4 * LANES, 512), F32),
            dma((2, groups, 3)),
            dma((2, groups, 3)),
            dma((2, groups, 2)),
            dma((2, groups, 2)),
            dma((2,)),
            remote,
        ],
        compiler_params=pltpu.CompilerParams(
            collective_id=0, has_side_effects=True, vmem_limit_bytes=62 * 2**20
        ),
        name="layer",
    )(
        tokens, grad, wqkv, wout, w_in, row(attn_gain), row(attn_bias), row(qkv_bias),
        row(out_bias), row(ffn_gain), row(ffn_bias), up_bias.reshape(4, 480), row(down_bias),
        jnp.asarray(permutation(), BF16), jnp.asarray(spreading(), BF16), jnp.asarray(c),
        jnp.asarray(s), lengths, ids, cw,
    )


def local(
    tokens, attn_norm_gain, attn_norm_bias, qkv_weight, qkv_bias, out_weight, out_bias,
    ffn_norm_gain, ffn_norm_bias, up_weight, up_bias, down_weight, down_bias, lengths,
    cluster_ids, cluster_weight, grad_out,
):
    width = tokens.shape[1]
    ff = up_bias.shape[0]
    inner = lax.axis_size("dp") == 8
    if inner:
        w_in = [up_weight, down_weight]
    else:
        part = jnp.stack([up_weight.T, down_weight], axis=0)
        part = lax.all_gather(part, "dp", axis=1, tiled=True)
        part = lax.all_gather(part, "heads", axis=0)
        part = jnp.pad(part, ((0, 0),) * 3 + ((0, LANES - USED),))
        part = part.reshape(2, 2, 2, 4, 2, 240, LANES)
        w_in = [part.transpose(1, 3, 4, 0, 2, 5, 6).reshape(2, 4, 2, 2, 480, LANES)]
    result, dtok, first, small, _ = layer(
        inner, tokens, qkv_weight, out_weight, w_in, attn_norm_gain, attn_norm_bias,
        qkv_bias, out_bias, ffn_norm_gain, ffn_norm_bias, up_bias, down_bias, lengths,
        cluster_ids, cluster_weight, grad_out,
    )
    if inner:
        dwqkv, dwout, dup, ddown = first
    else:
        acc, grads = first
        acc, own_sums = lax.psum((acc, small[2]), "dp")
        small = lax.psum(small, ("dp", "heads")).at[2].set(own_sums)
        grads = grads.reshape(2, 4, 2, 2, 2, 240, LANES).transpose(3, 0, 4, 1, 2, 5, 6)
        grads = grads.reshape(4, 2, ff, LANES)[..., :USED]
        grads = lax.psum_scatter(grads, "heads", scatter_dimension=0).astype(F32)
        grads = lax.psum_scatter(grads, "dp", scatter_dimension=1, tiled=True)
        dup, ddown = grads[0].T, grads[1]
        dwqkv = acc[: 3 * LANES, :width].reshape(3, LANES, width)[:, :USED]
        dwqkv = dwqkv.reshape(3, HEADS, HD, width).transpose(3, 1, 0, 2).reshape(width, 3 * USED)
        dwout = acc[3 * LANES : 3 * LANES + USED, :width]
    dqkvb = small[2, : 3 * LANES].reshape(3, LANES)[:, :USED].reshape(3, HEADS, HD)
    dqkvb = dqkvb.transpose(1, 0, 2).reshape(-1)
    return (
        result, dtok, small[0, :width], small[1, :width], dwqkv, dqkvb, dwout,
        small[12, :width], small[13, :width], small[14, :width], dup,
        small[8:12, :480].reshape(ff), ddown, small[15, :width],
    )


def solution(mesh):
    placed = (
        P(("dp", "heads"), None), P(), P(), P(None, "heads"), P("heads"), P("heads", None), P(),
        P(), P(), P("heads", "dp"), P(), P("dp", "heads"), P(), P("dp", None), P("dp", None),
        P(), P(("dp", "heads"), None),
    )
    given = (
        P(("dp", "heads"), None), P(("dp", "heads"), None), P(), P(), P(None, "heads"), P("heads"),
        P("heads", None), P(), P(), P(), P("heads", "dp"), P(), P("dp", "heads"), P(),
    )
    return jax.shard_map(local, mesh=mesh, in_specs=placed, out_specs=given, check_vma=False)
```

```python
from functools import partial

import jax
import jax.numpy as jnp
import numpy as np
from jax import lax
from jax.experimental import pallas as pl
from jax.experimental.pallas import tpu as pltpu
from jax.sharding import PartitionSpec as P

F32, BF16 = jnp.float32, jnp.bfloat16
MESH = pl.DeviceIdType.MESH
HD = 24
HEADS = 5
USED = HEADS * HD
LANES = 128
EPSILON = 1e-05
LOG2E = 1.4426950408889634
BIG = 1e30
BLOCK = 256


def dims(a, b, ca, cb, precision=None):
    return lax.dot_general(
        a, b, (((ca,), (cb,)), ((), ())), preferred_element_type=F32, precision=precision
    )


def nn(a, b):
    return dims(a, b, 1, 0)


def nt(a, b):
    return dims(a, b, 1, 1)


def tn(a, b):
    return dims(a, b, 0, 0)


def lane(rows, width=LANES):
    return lax.broadcasted_iota(jnp.int32, (rows, width), 1)


def head_lanes(rows, j):
    at = lane(rows)
    return (at >= HD * j) & (at < HD * (j + 1))


def partner(x):
    at = lane(x.shape[0])
    half = HD // 2
    return jnp.where(
        at % HD < half, pltpu.roll(x, LANES - half, 1), pltpu.roll(x, half, 1)
    )


def norm(x):
    centred = x - jnp.mean(x, axis=-1, keepdims=True)
    rstd = lax.rsqrt(jnp.mean(centred * centred, axis=-1, keepdims=True) + EPSILON)
    return centred * rstd, rstd


def norm_back(g, gain, xhat, rstd):
    n = g * gain
    return rstd * (
        n
        - jnp.mean(n, axis=-1, keepdims=True)
        - xhat * jnp.mean(n * xhat, axis=-1, keepdims=True)
    )


def body(
    inner, tok_hbm, grad_hbm, wqkv, wout, w_in, attn_gain, attn_bias, qkv_bias, out_bias, ffn_gain,
    ffn_bias, up_bias, down_bias, perm, spread, cos, sin, lengths, ids, cw,
    result, dtok_out, d_first, small, phbm,
    grad_t, tok, grad, in_s,
    n1, wq, wqt, wo, qkv_b, q_s, k_s, v_s, ctx, invl, pslot,
    rs_core_out, rs_core_in, rs_y_out, rs_y_in, rs_own,
    mid, n2, df, n2p, dfp, facc, dn2, wup, wdown, da, do_s, dot_t, q_t, dq, dk_t, dv_t, dqkv,
    sums, acc, ag_s, ag_r, rs_s, rs_r, p_s, remote,
):
    d, h = lax.axis_index("dp"), lax.axis_index("heads")
    core, y = h % 2, h // 2
    h_sib = h + 1 - 2 * core
    h_y = (h + 2) % 4
    sib, ypart = (d, h_sib), (d, h_y)
    groups = lengths.shape[0]
    width = tok.shape[1]
    group_rows = 4 * BLOCK
    steps = 4

    def send(src, dst, s, r, to):
        return pltpu.make_async_remote_copy(
            src_ref=src, dst_ref=dst, send_sem=s, recv_sem=r, device_id=to, device_id_type=MESH
        )

    def gather_copy(use, buf, k, n):
        block, to = ((h, sib), (h, ypart), (h_y, sib))[n]
        return send(
            buf.at[k, block], buf.at[k, block], ag_s.at[use, k, n], ag_r.at[use, k, n], to
        )

    def gather_start(use, buf, k):
        gather_copy(use, buf, k, 1).start()
        gather_copy(use, buf, k, 0).start()

    def gather_forward(use, buf, k):
        gather_copy(use, buf, k, 1).wait_recv()
        gather_copy(use, buf, k, 2).start()

    def gather_finish(use, buf, k):
        gather_copy(use, buf, k, 0).wait_recv()
        gather_copy(use, buf, k, 2).wait_recv()

    def gather_sent(use, buf, k):
        for n in range(3):
            gather_copy(use, buf, k, n).wait_send()

    def sum_copy(use, k, n):
        src, dst, to = ((rs_core_out, rs_core_in, sib), (rs_y_out, rs_y_in, ypart))[n]
        return send(src.at[k], dst.at[k], rs_s.at[use, k, n], rs_r.at[use, k, n], to)

    def sum_start(use, k, part):
        for other in (0, 1):
            rs_core_out[k, other] = part(2 * other + 1 - core).astype(BF16)
        sum_copy(use, k, 0).start()
        rs_y_out[k] = part(2 * (1 - y) + core).astype(BF16)
        rs_own[k] = part(h)

    def sum_forward(use, k):
        sum_copy(use, k, 0).wait_recv()
        rs_y_out[k] = (rs_y_out[k].astype(F32) + rs_core_in[k, 1 - y].astype(F32)).astype(BF16)
        sum_copy(use, k, 1).start()

    def sum_finish(use, k):
        sum_copy(use, k, 1).wait_recv()
        return rs_own[k] + rs_core_in[k, y].astype(F32) + rs_y_in[k].astype(F32)

    def sum_sent(use, k):
        for n in range(2):
            sum_copy(use, k, n).wait_send()

    if inner:
        (g, rc, rx, rz, ry, f_send, f_got, wres, vecs, heads_in, dp_out, dp_in,
         w_s, w_r, c_s, c_r, f_s, f_r, m_s, m_r) = remote
        wup_in, wdown_in = w_in
        dwqkv, dwout, dup, ddown = d_first
        gw = gg = g
        z, x = d // 2, d % 2
        xpart, above, below = (d + 1 - 2 * x, h), (d + 2, h), (d - 2, h)
        peers = [lax.rem(d + n, 8) for n in range(1, 8)]
        greeted = [sib, ypart, (d, (h_sib + 2) % 4)] + [(p, h) for p in peers]
    else:
        gw, (acc_out, gg) = w_in[0], d_first
        greeted = [sib, ypart]

    def w_y():
        block = g.at[core, y, z, x]
        return send(block, block, w_s.at[0], w_r.at[0], ypart)

    def w_up(v, s, origin):
        block = g.at[core, y + v - 2 * y * v, origin, x]
        n = 3 * v + s
        return send(block, block, w_s.at[n], w_r.at[n], above)

    def w_down(v, s, origin):
        block = g.at[core, y + v - 2 * y * v, origin, x]
        n = 6 + 3 * v + s
        return send(block, block, w_s.at[n], w_r.at[n], below)

    def w_x(v, origin, side):
        block = g.at[core, y + v - 2 * y * v, origin, side]
        n = 13 + 4 * v + origin
        return send(block, block, w_s.at[n], w_r.at[n], xpart)

    def w_core(v, origin, side, at):
        block = g.at[at, y + v - 2 * y * v, origin, side]
        n = 21 + 8 * v + 2 * origin + side
        return send(block, block, w_s.at[n], w_r.at[n], sib)

    def w_begin():
        g[core, y, z, x] = jnp.zeros((480, LANES), BF16)
        g[core, y, z, x, 0:240, 0:USED] = wup_in[...].astype(F32).T.astype(BF16)
        g[core, y, z, x, 240:480, 0:USED] = wdown_in[...]

    def w_here(v, origin):
        w_x(v, origin, x).start()
        w_core(v, origin, x, core).start()

    def w_first(v):
        if v:
            w_y().wait_recv()
        else:
            w_y().start()
        pl.when(z < 3)(lambda: w_up(v, 1, z).start())
        pl.when(z > 0)(lambda: w_down(v, 1, z).start())
        w_here(v, z)

    def w_step(v, s):
        @pl.when(z >= s)
        def _():
            w_up(v, s, z - s).wait_recv()
            if s < 3:
                pl.when(z < 3)(lambda: w_up(v, s + 1, z - s).start())
            w_here(v, z - s)

        @pl.when(z + s <= 3)
        def _():
            w_down(v, s, z + s).wait_recv()
            if s < 3:
                pl.when(z > 0)(lambda: w_down(v, s + 1, z + s).start())
            w_here(v, z + s)

    def w_other(v, s):
        def one(origin):
            w_x(v, origin, 1 - x).wait_recv()
            w_core(v, origin, 1 - x, core).start()

        if s == 0:
            one(z)
        else:
            pl.when(z >= s)(lambda: one(z - s))
            pl.when(z + s <= 3)(lambda: one(z + s))

    def w_end():
        for v in (0, 1):
            for origin in range(4):
                for side in (0, 1):
                    w_core(v, origin, side, 1 - core).wait_recv()

    def w_sent():
        w_y().wait_send()
        for v in (0, 1):
            for s in (1, 2, 3):
                pl.when((z >= s - 1) & (z < 3))(lambda: w_up(v, s, z - s + 1).wait_send())
                pl.when((z + s - 1 <= 3) & (z > 0))(lambda: w_down(v, s, z + s - 1).wait_send())
            for origin in range(4):
                w_x(v, origin, x).wait_send()
                for side in (0, 1):
                    w_core(v, origin, side, core).wait_send()

    def assemble():
        def step(i, _):
            parts = [gw[n % 2, n // 2, i // 2, i % 2] for n in range(4)]
            full = nn(jnp.concatenate(parts, axis=1), spread[...]).astype(BF16)
            r = pl.ds(pl.multiple_of(i * 240, 240), 240)
            wup[r, :] = full[0:240]
            wdown[r, :] = full[240:480]
            return 0

        lax.fori_loop(0, 8, step, 0)

    order = (3, 0, 2, 1)

    def g_core(v, origin):
        n = 4 * v + origin
        return send(g.at[1 - core, v, origin], rc.at[v, origin], c_s.at[n], c_r.at[n], sib)

    def g_x(v, origin):
        n = 8 + 4 * v + origin
        return send(g.at[core, v, origin, 1 - x], rx.at[v, origin], c_s.at[n], c_r.at[n], xpart)

    def g_up(v, s, to):
        n = 15 + 3 * v + s
        return send(g.at[core, v, to, x], rz.at[0, v, s - 1], c_s.at[n], c_r.at[n], above)

    def g_down(v, s, to):
        n = 21 + 3 * v + s
        return send(g.at[core, v, to, x], rz.at[1, v, s - 1], c_s.at[n], c_r.at[n], below)

    def g_y():
        return send(g.at[core, 1 - y, z, x], ry, c_s.at[28], c_r.at[28], ypart)

    def add_block(v, origin, side, ref):
        g[core, v, origin, side] = (
            g[core, v, origin, side].astype(F32) + ref[...].astype(F32)
        ).astype(BF16)

    def g_begin():
        for v in (0, 1):
            for origin in order:
                g_core(v, origin).start()

    def g_first(v):
        for origin in order:
            g_core(v, origin).wait_recv()
            add_block(v, origin, 1 - x, rc.at[v, origin, 1 - x])
            g_x(v, origin).start()
        for origin in order:
            add_block(v, origin, x, rc.at[v, origin, x])

    def g_add_x(v, origins):
        for origin in origins:
            g_x(v, origin).wait_recv()
            add_block(v, origin, x, rx.at[v, origin])

    def g_send(v, s):
        pl.when(z < s)(lambda: g_up(v, s, 4 - s + z).start())
        pl.when(3 - z < s)(lambda: g_down(v, s, s + z - 4).start())

    def g_recv(v, s):
        @pl.when((z >= 1) & (z <= s))
        def _():
            g_up(v, s, 0).wait_recv()
            add_block(v, 3 - s + z, x, rz.at[0, v, s - 1])

        @pl.when((z <= 2) & (z >= 3 - s))
        def _():
            g_down(v, s, 0).wait_recv()
            add_block(v, s + z - 3, x, rz.at[1, v, s - 1])

    def g_y_begin(v):
        pl.when(y != v)(lambda: g_y().start())

    def g_last():
        g_y().wait_recv()
        total = g[core, y, z, x].astype(F32) + ry[...].astype(F32)
        dup[...] = total[0:240].T[0:USED]
        ddown[...] = total[240:480, 0:USED]
        for v in (0, 1):
            for n in range(4):
                g_core(v, n).wait_send()
                g_x(v, n).wait_send()
            for s in (1, 2, 3):
                pl.when(z < s)(lambda: g_up(v, s, 0).wait_send())
                pl.when(3 - z < s)(lambda: g_down(v, s, 0).wait_send())
        g_y().wait_send()

    spans = ((384, 512), (256, 384), (0, 256))

    def f_size(n):
        return (spans[n][1] - spans[n][0]) // 8

    def f_rows(n, p):
        return pl.ds(pl.multiple_of(spans[n][0] + p * f_size(n), 16), f_size(n))

    def f_out(n, p, slot):
        return send(
            f_send[n].at[p], f_got[n].at[slot], f_s.at[0, n, p], f_r.at[0, n, slot], (p, h)
        )

    def f_home(n, p, at):
        rows = wres.at[f_rows(n, at)]
        return send(rows, rows, f_s.at[1, n, p], f_r.at[1, n, at], (p, h))

    def f_begin(n):
        first, size = spans[n][0], f_size(n)
        if n == 2:
            for at in range(3):
                row = sums[0, at : at + 1, :]
                top = row.astype(BF16).astype(F32)
                vecs[2 * at : 2 * at + 1, :] = top
                vecs[2 * at + 1 : 2 * at + 2, :] = row - top
            extra = vecs[...].astype(BF16)
        for p in range(8):
            f_send[n][p, 0:size, :] = acc[first + p * size : first + (p + 1) * size, :].astype(BF16)
            if n == 2:
                f_send[n][p, size : size + 16, :] = extra
        f_got[n][d] = f_send[n][d]
        for p in peers:
            f_out(n, p, d).start()

    def f_back(n):
        size = f_size(n)
        for p in peers:
            f_out(n, p, p).wait_recv()
        total = f_got[n][0].astype(F32)
        for p in range(1, 8):
            total = total + f_got[n][p].astype(F32)
        wres[f_rows(n, d), :] = total[0:size].astype(BF16)
        for p in peers:
            f_home(n, p, d).start()
        if n == 2:
            for at in range(3):
                row = size + 2 * at
                sums[0, at : at + 1, :] = total[row : row + 1] + total[row + 1 : row + 2]
            m_begin(0)

    def f_end(n):
        for p in peers:
            f_home(n, p, p).wait_recv()

    def f_sent(n):
        for p in peers:
            f_out(n, p, d).wait_send()
            f_home(n, p, d).wait_send()

    near = (sib, ypart, (d, (h_sib + 2) % 4))

    def m_heads(b, n, at):
        return send(sums.at[b], heads_in.at[b, at], m_s.at[b, n], m_r.at[b, at], near[n])

    def m_dp(n, at):
        return send(dp_out, dp_in.at[at], m_s.at[1, 3 + n], m_r.at[1, 4 + at], (peers[n], h))

    def m_begin(b):
        heads_in[b, h] = sums[b]
        for n in range(3):
            m_heads(b, n, h).start()

    def m_total(b):
        for n in range(3):
            m_heads(b, n, near[n][1]).wait_recv()
        return heads_in[b, 0] + heads_in[b, 1] + heads_in[b, 2] + heads_in[b, 3]

    def m_middle():
        dp_out[...] = m_total(1)
        dp_in[d] = dp_out[...]
        for n in range(7):
            m_dp(n, d).start()

    def m_end():
        for n in range(7):
            m_dp(n, peers[n]).wait_recv()
        total = dp_in[0]
        for p in range(1, 8):
            total = total + dp_in[p]
        small[8:16, :] = total
        for n in range(3):
            m_heads(1, n, h).wait_send()
        for n in range(7):
            m_dp(n, d).wait_send()

    def m_last():
        total = m_total(0)
        small[0:8, :] = total
        small[0:1, 0:width] = (
            total[0:1, 0:width] - attn_bias[...] * total[1:2, 0:width]
        ) / attn_gain[...]
        small[2:3, :] = sums[0, 2:3, :]
        for n in range(3):
            m_heads(0, n, h).wait_send()

    def rows_of(k):
        return slice(k * BLOCK, (k + 1) * BLOCK)

    def add_sum(row, value):
        b, at = row // 8, row % 8
        sums[b, at : at + 1, 0 : value.shape[1]] += value

    barrier = pltpu.get_barrier_semaphore()
    for other in greeted:
        pl.semaphore_signal(barrier, inc=1, device_id=other, device_id_type=MESH)

    def first_norm(k):
        tok_in(k).wait()
        x_ = result[:, rows_of(k)].astype(F32).T
        tok[rows_of(k), :] = x_.astype(BF16)
        xhat, _ = norm(x_)
        n1[k, h, :, 0:width] = (xhat * attn_gain[...] + attn_bias[...]).astype(BF16)
        n1[k, h, :, width:512] = jnp.zeros((BLOCK, 512 - width), BF16)

    def tok_in(k):
        cols = pl.ds(k * BLOCK, BLOCK)
        return pltpu.make_async_copy(tok_hbm.at[:, cols], result.at[:, cols], in_s.at[k])

    grad_in = pltpu.make_async_copy(grad_hbm, grad_t, in_s.at[groups])
    for k in range(groups):
        tok_in(k).start()
    grad_in.start()
    first_norm(0)
    pl.semaphore_wait(barrier, len(greeted))
    gather_start(0, n1, 0)
    if inner:
        w_begin()
        w_first(0)
    for k in range(1, groups):
        first_norm(k)
        gather_start(0, n1, k)

    wq[0:width, :] = nn(wqkv[...], perm[...]).astype(BF16)
    wq[width:512, :] = jnp.zeros((512 - width, 3 * LANES), BF16)
    wqt[:, 0:width] = dims(perm[...], wqkv[...], 0, 1).astype(BF16)
    wqt[:, width:512] = jnp.zeros((3 * LANES, 512 - width), BF16)
    qkv_b[...] = dims(qkv_bias[...], perm[...].astype(F32), 1, 0, lax.Precision.HIGHEST)
    wo[:, width:512] = jnp.zeros((LANES, 512 - width), BF16)
    wo[:, 0:width] = jnp.concatenate(
        [wout[...].astype(F32), jnp.zeros((LANES - USED, width), F32)], axis=0
    ).astype(BF16)
    sums[...] = jnp.zeros_like(sums)
    acc[...] = jnp.zeros_like(acc)
    n2[:, width:512] = jnp.zeros((groups * BLOCK, 512 - width), BF16)
    df[:, width:512] = jnp.zeros((groups * BLOCK, 512 - width), BF16)
    for k in range(groups):
        da[k, h, :, width:512] = jnp.zeros((BLOCK, 512 - width), BF16)

    def ends_of(k):
        total, ends = 0, []
        for p in range(4):
            total = total + lengths[k, p]
            ends.append(total)
        return ends

    def project(k):
        ends = ends_of(k)
        at1 = lane(1)
        lo = jnp.where(at1 == USED, 0, group_rows + 1)
        hi = jnp.where(at1 == USED + 4, group_rows + 1, 0)
        for p in range(4):
            lo = jnp.where(at1 == USED + 1 + p, ends[p], lo)
            hi = jnp.where(at1 == USED + p, ends[p], hi)

        def step(i, _):
            r = pl.ds(pl.multiple_of(i * BLOCK, BLOCK), BLOCK)
            x_ = nn(n1[k, i], wq[...]) + qkv_b[...]
            c, s = cos[r, :], sin[r, :]
            at = lane(BLOCK)
            row = lax.broadcasted_iota(jnp.int32, (BLOCK, LANES), 0) + i * BLOCK
            inside = (row >= lo) & (row < hi)
            marks = (at >= USED) & (at < USED + 5)
            q = x_[:, 0:LANES]
            q = (q * c + partner(q) * s) * (HD ** (-0.5) * LOG2E)
            q_s[k, r, :] = jnp.where(at < USED, q, jnp.where(inside, 1.0, 0.0)).astype(BF16)
            key = x_[:, LANES : 2 * LANES]
            key = key * c + partner(key) * s
            k_s[k, r, :] = jnp.where(
                at < USED, key, jnp.where(marks & jnp.logical_not(inside), -BIG, 0.0)
            ).astype(BF16)
            v_s[k, r, :] = jnp.where(
                at < USED, x_[:, 2 * LANES : 3 * LANES], jnp.where(at < USED + 2, 1.0, 0.0)
            ).astype(BF16)
            return 0

        lax.fori_loop(0, steps, step, 0)

    def p_out(k, i):
        slot = (k * steps + i) % 2
        return pltpu.make_async_copy(pslot.at[slot], phbm.at[k, i], p_s.at[slot])

    def p_in(n):
        slot = n % 2
        return pltpu.make_async_copy(phbm.at[n // steps, n % steps], pslot.at[slot], p_s.at[slot])

    def run_hooks(hooks, i):
        for at, todo in hooks.items():

            @pl.when(i == at)
            def _():
                for one in todo:
                    one()

    def attend(k, hooks):
        def step(i, _):
            n = k * steps + i
            slot = n % 2
            run_hooks(hooks, i)

            @pl.when(n >= 2)
            def _():
                p_out(k, i).wait()

            r = pl.ds(pl.multiple_of(i * BLOCK, BLOCK), BLOCK)
            q = q_s[k, r, :]
            keys, vals = k_s[k], v_s[k]
            at = lane(BLOCK)

            def score(j):
                return nt(jnp.where(head_lanes(BLOCK, j) | (at >= USED), q, 0), keys)

            out = jnp.zeros((BLOCK, LANES), F32)
            inv = jnp.zeros((BLOCK, LANES), F32)
            s = score(0)
            for j in range(HEADS):
                later = score(j + 1) if j + 1 < HEADS else None
                e = jnp.exp2(s - jnp.max(s, axis=1, keepdims=True)).astype(BF16)
                pslot[slot, j] = e
                o = nn(e, vals)
                one = 1.0 / o[:, USED : USED + 1]
                out = jnp.where(head_lanes(BLOCK, j), o * one, out)
                inv = jnp.where(head_lanes(BLOCK, j), one, inv)
                s = later
            ctx[k, r, :] = out
            invl[k, r, :] = inv
            p_out(k, i).start()
            return 0

        lax.fori_loop(0, steps, step, 0)

    def out_part(k):
        def part(i):
            r = pl.ds(pl.multiple_of(i * BLOCK, BLOCK), BLOCK)
            return nn(ctx[k, r, :].astype(BF16), wo[...])

        return part

    if inner:
        first, step, other = (
            (lambda *a, f=f: partial(f, *a)) for f in (w_first, w_step, w_other)
        )
        w_plan = (
            {1: [first(1), step(0, 2)], 3: [step(1, 1), step(0, 3)]},
            {0: [step(1, 2), other(0, 0), other(0, 1), other(1, 0)],
             2: [step(1, 3), other(0, 2), other(1, 1)]},
            {0: [other(0, 3), other(1, 2)], 2: [other(1, 3)]},
        )
    gather_forward(0, n1, 0)
    if inner:
        w_step(0, 1)
    for k in range(groups):
        gather_finish(0, n1, k)
        project(k)
        if k > 0:
            sum_forward(0, k - 1)
        hooks = {}
        if k + 1 < groups:
            hooks[3] = [partial(gather_forward, 0, n1, k + 1)]
        if inner:
            for at, todo in w_plan[k].items():
                hooks.setdefault(at, []).extend(todo)
        attend(k, hooks)
        sum_start(0, k, out_part(k))
    sum_forward(0, groups - 1)
    for n in (groups * steps, groups * steps + 1):
        p_in(n % 2).wait()
    p_in(0).start()
    p_in(1).start()
    if inner:
        w_end()
    assemble()
    if inner:
        w_sent()

    grad_in.wait()

    def weight_of(k):
        ends = ends_of(k)
        row = lax.broadcasted_iota(jnp.int32, (BLOCK, 1), 0) + h * BLOCK
        w = jnp.zeros((BLOCK, 1), F32)
        for p in reversed(range(4)):
            w = jnp.where(row < ends[p], cw[ids[k, p]], w)
        return w

    def ffn_pre(k):
        r = rows_of(k)
        middle = tok[r, :].astype(F32) + sum_finish(0, k)[:, 0:width] + out_bias[...]
        mid[r, :] = middle
        xhat, _ = norm(middle)
        n2[r, 0:width] = (xhat * ffn_gain[...] + ffn_bias[...]).astype(BF16)
        grad[r, :] = grad_t[:, r].astype(F32).T.astype(BF16)
        d_ffn = (grad[r, :].astype(F32) * weight_of(k)).astype(BF16)
        df[r, 0:width] = d_ffn
        add_sum(15, jnp.sum(d_ffn.astype(F32), axis=0, keepdims=True))
        n2p[r, :] = nt(n2[r, :], spread[...]).astype(BF16)
        dfp[r, :] = nt(df[r, :], spread[...]).astype(BF16)

    def ffn_core(first, last):
        r = slice(first * BLOCK, last * BLOCK)

        def step(t, _):
            f = pl.ds(pl.multiple_of(t * 480, 480), 480)
            wu, wd = wup[f, :], wdown[f, :]
            u = nt(n2[r, :], wu) + up_bias[pl.ds(t, 1), :]
            phi = 0.5 + 0.5 * lax.erf(u * (0.5**0.5))
            hid = (u * phi).astype(BF16)
            slope = phi + u * (jnp.exp(u * u * -0.5) * 0.3989422804014327)
            out = nn(hid, wd)
            du = (nt(df[r, :], wd) * slope).astype(BF16)
            dx = nn(du, wu)
            sums[1, pl.ds(t, 1), 0:480] += jnp.sum(du.astype(F32), axis=0, keepdims=True)

            @pl.when(t == 0)
            def _():
                facc[r, :] = out
                dn2[r, :] = dx

            @pl.when(t > 0)
            def _():
                facc[r, :] += out
                dn2[r, :] += dx

            for part, wide in enumerate((tn(du, n2p[r, :]), tn(hid, dfp[r, :]))):
                fr = slice(part * 240, part * 240 + 240)
                for side in (0, 1):
                    for n in range(4):
                        new = wide[side * 240 : side * 240 + 240, n * LANES : (n + 1) * LANES]
                        if first > 0:
                            new = new + gg[n % 2, n // 2, t, side, fr, :].astype(F32)
                        gg[n % 2, n // 2, t, side, fr, :] = new.astype(BF16)
            return 0

        lax.fori_loop(0, 4, step, 0)

    def ffn_post(k):
        r = rows_of(k)
        middle = mid[r, :]
        result[:, r] = (middle + facc[r, 0:width] + down_bias[...]).T.astype(BF16)
        g_ = dn2[r, 0:width]
        xhat, rstd = norm(middle)
        add_sum(13, jnp.sum(g_ * xhat, axis=0, keepdims=True))
        add_sum(14, jnp.sum(g_, axis=0, keepdims=True))
        d_result = grad[r, :].astype(F32) * weight_of(k)
        d_middle = d_result + norm_back(g_, ffn_gain[...], xhat, rstd)
        mid[r, :] = d_middle
        low = d_middle.astype(BF16)
        da[k, h, :, 0:width] = low
        add_sum(12, jnp.sum(low.astype(F32), axis=0, keepdims=True))
        gather_start(1, da, k)

    for k in range(groups - 1):
        ffn_pre(k)
    ffn_core(0, groups - 1)
    for k in range(groups - 1):
        ffn_post(k)
    ffn_pre(groups - 1)
    ffn_core(groups - 1, groups)
    if inner:
        g_begin()
    ffn_post(groups - 1)
    if inner:
        m_begin(1)
    for k in range(groups):
        gather_sent(0, n1, k)
        sum_sent(0, k)

    def back_prep(k):
        def step(i, _):
            r = pl.ds(pl.multiple_of(i * BLOCK, BLOCK), BLOCK)
            g_ = nt(da[k, i], wo[...]).astype(BF16).astype(F32)
            g_ = (g_ * invl[k, r, :]).astype(BF16)
            do_s[r, :] = g_
            dot_t[:, r] = g_.astype(F32).T
            q_t[:, r] = q_s[k, r, :].astype(F32).T
            acc[3 * LANES : 4 * LANES, :] += tn(ctx[k, r, :].astype(BF16), da[k, i])
            return 0

        lax.fori_loop(0, steps, step, 0)
        dk_t[...] = jnp.zeros_like(dk_t)
        dv_t[...] = jnp.zeros_like(dv_t)

    def back(k, hooks):
        def step(i, _):
            n = k * steps + i
            slot = n % 2
            run_hooks(hooks, i)
            p_in(n).wait()
            r = pl.ds(pl.multiple_of(i * BLOCK, BLOCK), BLOCK)
            g_ = do_s[r, :].astype(F32)
            prod = g_ * ctx[k, r, :]
            keys, vals = k_s[k], v_s[k]
            at = lane(BLOCK)

            def d_prob(j):
                mine = head_lanes(BLOCK, j)
                total = jnp.sum(jnp.where(mine, prod, 0.0), axis=1, keepdims=True)
                top = total.astype(BF16).astype(F32)
                row = jnp.where(at == USED, -top, jnp.where(at == USED + 1, top - total, 0.0))
                return nt(jnp.where(mine, g_, row).astype(BF16), vals)

            out = jnp.zeros((BLOCK, LANES), F32)
            dp = d_prob(0)
            for j in range(HEADS):
                later = d_prob(j + 1) if j + 1 < HEADS else None
                e = pslot[slot, j]
                ds = (e.astype(F32) * dp).astype(BF16)
                out = jnp.where(head_lanes(BLOCK, j), nn(ds, keys), out)
                hs = slice(j * HD, (j + 1) * HD)
                dk_t[hs, :] += nn(q_t[hs, r].astype(BF16), ds)
                if k < groups - 1:
                    dv_t[hs, :] += nn(dot_t[hs, r].astype(BF16), e)
                dp = later
            dq[r, :] = out

            @pl.when(n + 2 < groups * steps)
            def _():
                p_in(n + 2).start()

            return 0

        lax.fori_loop(0, steps, step, 0)

    def back_post(k):
        def step(i, _):
            r = pl.ds(pl.multiple_of(i * BLOCK, BLOCK), BLOCK)
            c, s = cos[r, :], sin[r, :]
            a = dq[r, :] * HD ** (-0.5)
            a = a * c - partner(a) * s
            b = dk_t[:, r].T * (1.0 / LOG2E)
            b = b * c - partner(b) * s
            if k < groups - 1:
                g_ = jnp.concatenate([a, b, dv_t[:, r].T], axis=1).astype(BF16)
            else:
                g_ = jnp.concatenate([a, b], axis=1).astype(BF16)
            cols = g_.shape[1]
            dqkv[r, 0:cols] = g_
            add_sum(2, jnp.sum(g_.astype(F32), axis=0, keepdims=True))
            acc[0:cols, :] += tn(g_, n1[k, i])
            return 0

        lax.fori_loop(0, steps, step, 0)

    def back_values(k):
        def step(i, _):
            n = k * steps + i
            slot = n % 2
            p_in(n).wait()
            r = pl.ds(pl.multiple_of(i * BLOCK, BLOCK), BLOCK)
            for j in range(HEADS):
                hs = slice(j * HD, (j + 1) * HD)
                dv_t[hs, :] += nn(dot_t[hs, r].astype(BF16), pslot[slot, j])
            p_in(k * steps + (i + 2) % steps).start()
            return 0

        lax.fori_loop(0, steps, step, 0)

        def post(i, _):
            r = pl.ds(pl.multiple_of(i * BLOCK, BLOCK), BLOCK)
            g_ = dv_t[:, r].T.astype(BF16)
            dqkv[r, 2 * LANES : 3 * LANES] = g_
            sums[0, 2:3, 2 * LANES : 3 * LANES] += jnp.sum(g_.astype(F32), axis=0, keepdims=True)
            acc[2 * LANES : 3 * LANES, :] += tn(g_, n1[k, i])
            return 0

        lax.fori_loop(0, steps, post, 0)

    def norm_sums():
        add_sum(0, jnp.sum(acc[0 : 3 * LANES, :] * wqt[...].astype(F32), axis=0, keepdims=True))
        add_sum(1, dims(sums[0, 2:3, 0 : 3 * LANES], wqt[...].astype(F32), 1, 0, lax.Precision.HIGHEST))

    def tokens_part(i):
        r = pl.ds(pl.multiple_of(i * BLOCK, BLOCK), BLOCK)
        return nt(dqkv[r, :], wq[...])

    def last_norm(k):
        r = rows_of(k)
        g_ = sum_finish(1, k)[:, 0:width]
        xhat, rstd = norm(tok[r, :].astype(F32))
        dtok_out[:, r] = (mid[r, :] + norm_back(g_, attn_gain[...], xhat, rstd)).T

    if inner:
        wait_x, go, take, first = (
            (lambda *a, f=f: partial(f, *a)) for f in (g_add_x, g_send, g_recv, g_first)
        )
        a, b = order[:2], order[2:]
        g_plan = (
            {0: [first(0)], 1: [first(1), m_middle], 3: [wait_x(0, a), go(0, 1)]},
            {0: [wait_x(0, b), take(0, 1), go(0, 2), m_end],
             2: [wait_x(1, a), go(1, 1), take(0, 2), go(0, 3)]},
            {0: [take(0, 3), partial(g_y_begin, 0), wait_x(1, b), take(1, 1), go(1, 2)],
             2: [take(1, 2), go(1, 3), partial(f_back, 0)],
             3: [partial(f_back, 1)]},
        )
    gather_forward(1, da, 0)
    for k in range(groups):
        gather_finish(1, da, k)
        back_prep(k)
        if k > 0:
            sum_forward(1, k - 1)
        if k == groups - 1:
            if inner:
                f_begin(0)
            back_values(k)
            if inner:
                f_begin(1)
        hooks = {}
        if k == 0:
            hooks[1] = [partial(gather_forward, 1, da, 1)]
            hooks[3] = [partial(gather_forward, 1, da, 2)]
        if inner:
            for at, todo in g_plan[k].items():
                hooks.setdefault(at, []).extend(todo)
        back(k, hooks)
        back_post(k)
        if k == groups - 1:
            norm_sums()
        if inner and k == groups - 1:
            f_begin(2)
        sum_start(1, k, tokens_part)
    for k in range(groups - 1):
        last_norm(k)
    if inner:
        g_recv(1, 3)
        g_y_begin(1)
    sum_forward(1, groups - 1)
    if inner:
        f_back(2)
    last_norm(groups - 1)
    if inner:
        g_last()
        for n in range(3):
            f_end(n)
        dwqkv[...] = dims(wres[0 : 3 * LANES, :], perm[...], 0, 1)[0:width]
        dwout[...] = wres[3 * LANES : 4 * LANES, :].astype(F32)[0:USED, 0:width]
        m_last()
        for n in range(3):
            f_sent(n)
    else:
        small[0:8, :] = sums[0]
        small[8:16, :] = sums[1]
        acc_out[...] = acc[...]
    for k in range(groups):
        gather_sent(1, da, k)
        sum_sent(1, k)


def permutation():
    table = np.zeros((3 * USED, 3 * LANES), np.float32)
    for j in range(HEADS):
        for part in range(3):
            for i in range(HD):
                table[(j * 3 + part) * HD + i, part * LANES + j * HD + i] = 1.0
    return table


def turns(group_rows):
    freq = 10000.0 ** (-2.0 * np.arange(HD // 2) / HD)
    angle = np.arange(group_rows)[:, None] * freq[None, :]
    c = np.zeros((group_rows, LANES), np.float32)
    s = np.zeros((group_rows, LANES), np.float32)
    c[:, :USED] = np.tile(np.cos(angle), (1, 2 * HEADS))
    s[:, :USED] = np.tile(np.concatenate([-np.sin(angle), np.sin(angle)], axis=1), (1, HEADS))
    return c, s


def spreading():
    table = np.zeros((4 * LANES, 4 * LANES), np.float32)
    for n in range(4):
        for i in range(USED):
            table[n * LANES + i, n * USED + i] = 1.0
    return table


def layer(
    inner, tokens, wqkv, wout, w_in, attn_gain, attn_bias, qkv_bias, out_bias, ffn_gain,
    ffn_bias, up_bias, down_bias, lengths, ids, cw, grad,
):
    own, width = tokens.shape
    groups = lengths.shape[0]
    ff = up_bias.shape[0]
    group_rows = 4 * BLOCK
    c, s = turns(group_rows)
    vm = pl.BlockSpec(memory_space=pltpu.VMEM)
    sm = pl.BlockSpec(memory_space=pltpu.SMEM)
    anywhere = pl.BlockSpec(memory_space=pl.ANY)
    shape = jax.ShapeDtypeStruct
    row = lambda v: v.reshape(1, -1)
    v, dma = pltpu.VMEM, pltpu.SemaphoreType.DMA
    chunks = (2, 2, 4, 2, 480, LANES)
    if inner:
        first = (
            shape((width, 3 * USED), F32),
            shape((USED, width), F32),
            shape((USED, 240), F32),
            shape((240, USED), F32),
        )
        remote = [
            v(chunks, BF16),
            v((2, 4, 2, 480, LANES), BF16),
            v((2, 4, 480, LANES), BF16),
            v((2, 2, 3, 480, LANES), BF16),
            v((480, LANES), BF16),
            [v((8, n, 512), BF16) for n in (16, 16, 48)],
            [v((8, n, 512), BF16) for n in (16, 16, 48)],
            v((4 * LANES, 512), BF16),
            v((16, 512), F32),
            v((2, 4, 8, 512), F32),
            v((8, 512), F32),
            v((8, 8, 512), F32),
            dma((37,)),
            dma((37,)),
            dma((29,)),
            dma((29,)),
            dma((2, 3, 8)),
            dma((2, 3, 8)),
            dma((2, 10)),
            dma((2, 12)),
        ]
    else:
        first = (shape((4 * LANES, 512), F32), shape(chunks, BF16))
        remote = []
    return pl.pallas_call(
        partial(body, inner),
        out_shape=(
            shape((width, own), BF16),
            shape((width, own), F32),
            first,
            shape((16, 512), F32),
            shape((groups, 4, HEADS, BLOCK, group_rows), BF16),
        ),
        in_specs=[anywhere] * 2 + [vm] * 2 + [[vm] * len(w_in)] + [vm] * 12 + [sm] * 3,
        out_specs=(vm, vm, (vm,) * len(first), vm, anywhere),
        scratch_shapes=[
            v((width, own), BF16),
            v((own, width), BF16),
            v((own, width), BF16),
            dma((groups + 1,)),
            v((groups, 4, BLOCK, 512), BF16),
            v((512, 3 * LANES), BF16),
            v((3 * LANES, 512), BF16),
            v((LANES, 512), BF16),
            v((1, 3 * LANES), F32),
            v((groups, group_rows, LANES), BF16),
            v((groups, group_rows, LANES), BF16),
            v((groups, group_rows, LANES), BF16),
            v((groups, group_rows, LANES), F32),
            v((groups, group_rows, LANES), F32),
            v((2, HEADS, BLOCK, group_rows), BF16),
            v((groups, 2, BLOCK, 512), BF16),
            v((groups, 2, BLOCK, 512), BF16),
            v((groups, BLOCK, 512), BF16),
            v((groups, BLOCK, 512), BF16),
            v((groups, BLOCK, 512), F32),
            v((own, width), F32),
            v((own, 512), BF16),
            v((own, 512), BF16),
            v((own, 512), BF16),
            v((own, 512), BF16),
            v((own, 512), F32),
            v((own, 512), F32),
            v((ff, 512), BF16),
            v((ff, 512), BF16),
            v((groups, 4, BLOCK, 512), BF16),
            v((group_rows, LANES), BF16),
            v((LANES, group_rows), F32),
            v((LANES, group_rows), F32),
            v((group_rows, LANES), F32),
            v((LANES, group_rows), F32),
            v((LANES, group_rows), F32),
            v((group_rows, 3 * LANES), BF16),
            v((2, 8, 512), F32),
            v((4 * LANES, 512), F32),
            dma((2, groups, 3)),
            dma((2, groups, 3)),
            dma((2, groups, 2)),
            dma((2, groups, 2)),
            dma((2,)),
            remote,
        ],
        compiler_params=pltpu.CompilerParams(
            collective_id=0, has_side_effects=True, vmem_limit_bytes=62 * 2**20
        ),
        name="layer",
    )(
        tokens.T, grad.T, wqkv, wout, w_in, row(attn_gain), row(attn_bias), row(qkv_bias),
        row(out_bias), row(ffn_gain), row(ffn_bias), up_bias.reshape(4, 480), row(down_bias),
        jnp.asarray(permutation(), BF16), jnp.asarray(spreading(), BF16), jnp.asarray(c),
        jnp.asarray(s), lengths, ids, cw,
    )


def local(
    tokens, attn_norm_gain, attn_norm_bias, qkv_weight, qkv_bias, out_weight, out_bias,
    ffn_norm_gain, ffn_norm_bias, up_weight, up_bias, down_weight, down_bias, lengths,
    cluster_ids, cluster_weight, grad_out,
):
    width = tokens.shape[1]
    ff = up_bias.shape[0]
    inner = lax.axis_size("dp") == 8
    if inner:
        w_in = [up_weight, down_weight]
    else:
        part = jnp.stack([up_weight.T, down_weight], axis=0)
        part = lax.all_gather(part, "dp", axis=1, tiled=True)
        part = lax.all_gather(part, "heads", axis=0)
        part = jnp.pad(part, ((0, 0),) * 3 + ((0, LANES - USED),))
        part = part.reshape(2, 2, 2, 4, 2, 240, LANES)
        w_in = [part.transpose(1, 0, 3, 4, 2, 5, 6).reshape(2, 2, 4, 2, 480, LANES)]
    result, dtok, first, small, _ = layer(
        inner, tokens, qkv_weight, out_weight, w_in, attn_norm_gain, attn_norm_bias,
        qkv_bias, out_bias, ffn_norm_gain, ffn_norm_bias, up_bias, down_bias, lengths,
        cluster_ids, cluster_weight, grad_out,
    )
    if inner:
        dwqkv, dwout, dup, ddown = first
    else:
        acc, grads = first
        acc, own_sums = lax.psum((acc, small[2]), "dp")
        small = lax.psum(small, ("dp", "heads")).at[2].set(own_sums)
        gain_sum = (small[0, :width] - attn_norm_bias * small[1, :width]) / attn_norm_gain
        small = small.at[0, :width].set(gain_sum)
        grads = grads.reshape(2, 2, 4, 2, 2, 240, LANES).transpose(1, 0, 4, 2, 3, 5, 6)
        grads = grads.reshape(4, 2, ff, LANES)[..., :USED]
        grads = lax.psum_scatter(grads, "heads", scatter_dimension=0).astype(F32)
        grads = lax.psum_scatter(grads, "dp", scatter_dimension=1, tiled=True)
        dup, ddown = grads[0].T, grads[1]
        dwqkv = acc[: 3 * LANES, :width].reshape(3, LANES, width)[:, :USED]
        dwqkv = dwqkv.reshape(3, HEADS, HD, width).transpose(3, 1, 0, 2).reshape(width, 3 * USED)
        dwout = acc[3 * LANES : 3 * LANES + USED, :width]
    dqkvb = small[2, : 3 * LANES].reshape(3, LANES)[:, :USED].reshape(3, HEADS, HD)
    dqkvb = dqkvb.transpose(1, 0, 2).reshape(-1)
    return (
        result.T, dtok.T, small[0, :width], small[1, :width], dwqkv, dqkvb, dwout,
        small[12, :width], small[13, :width], small[14, :width], dup,
        small[8:12, :480].reshape(ff), ddown, small[15, :width],
    )


def solution(mesh):
    placed = (
        P(("dp", "heads"), None), P(), P(), P(None, "heads"), P("heads"), P("heads", None), P(),
        P(), P(), P("heads", "dp"), P(), P("dp", "heads"), P(), P("dp", None), P("dp", None),
        P(), P(("dp", "heads"), None),
    )
    given = (
        P(("dp", "heads"), None), P(("dp", "heads"), None), P(), P(), P(None, "heads"), P("heads"),
        P("heads", None), P(), P(), P(), P("heads", "dp"), P(), P("dp", "heads"), P(),
    )
    return jax.shard_map(local, mesh=mesh, in_specs=placed, out_specs=given, check_vma=False)
```

```python
from functools import partial

import jax
import jax.numpy as jnp
import numpy as np
from jax import lax
from jax.experimental import pallas as pl
from jax.experimental.pallas import tpu as pltpu
from jax.sharding import PartitionSpec as P

F32, BF16 = jnp.float32, jnp.bfloat16
MESH = pl.DeviceIdType.MESH
HD = 24
HEADS = 5
USED = HEADS * HD
LANES = 128
EPSILON = 1e-05
LOG2E = 1.4426950408889634
BIG = 1e30
BLOCK = 256


def dims(a, b, ca, cb, precision=None):
    return lax.dot_general(
        a, b, (((ca,), (cb,)), ((), ())), preferred_element_type=F32, precision=precision
    )


def nn(a, b):
    return dims(a, b, 1, 0)


def nt(a, b):
    return dims(a, b, 1, 1)


def tn(a, b):
    return dims(a, b, 0, 0)


def lane(rows, width=LANES):
    return lax.broadcasted_iota(jnp.int32, (rows, width), 1)


def head_lanes(rows, j):
    at = lane(rows)
    return (at >= HD * j) & (at < HD * (j + 1))


def partner(x):
    at = lane(x.shape[0])
    half = HD // 2
    return jnp.where(
        at % HD < half, pltpu.roll(x, LANES - half, 1), pltpu.roll(x, half, 1)
    )


def norm(x):
    centred = x - jnp.mean(x, axis=-1, keepdims=True)
    rstd = lax.rsqrt(jnp.mean(centred * centred, axis=-1, keepdims=True) + EPSILON)
    return centred * rstd, rstd


def norm_back(g, gain, xhat, rstd):
    n = g * gain
    return rstd * (
        n
        - jnp.mean(n, axis=-1, keepdims=True)
        - xhat * jnp.mean(n * xhat, axis=-1, keepdims=True)
    )


def body(
    inner, tok_hbm, grad_hbm, wqkv, wout, w_in, attn_gain, attn_bias, qkv_bias, out_bias, ffn_gain,
    ffn_bias, up_bias, down_bias, perm, spread, cos, sin, lengths, ids, cw,
    result, dtok_out, d_first, small, phbm,
    grad_t, tok, grad, in_s,
    n1, wq, wqt, wo, qkv_b, q_s, k_s, v_s, ctx, invl, pslot,
    rs_core_out, rs_core_in, rs_y_out, rs_y_in, rs_own,
    mid, n2, df, n2p, dfp, facc, dn2, wup, wdown, da, do_s, dot_t, q_t, dq, dk_t, dv_t, dqkv,
    sums, acc, ag_s, ag_r, rs_s, rs_r, p_s, remote,
):
    d, h = lax.axis_index("dp"), lax.axis_index("heads")
    core, y = h % 2, h // 2
    h_sib = h + 1 - 2 * core
    h_y = (h + 2) % 4
    sib, ypart = (d, h_sib), (d, h_y)
    groups = lengths.shape[0]
    width = tok.shape[1]
    group_rows = 4 * BLOCK
    steps = 4

    def send(src, dst, s, r, to):
        return pltpu.make_async_remote_copy(
            src_ref=src, dst_ref=dst, send_sem=s, recv_sem=r, device_id=to, device_id_type=MESH
        )

    def gather_copy(use, buf, k, n):
        block, to = ((h, sib), (h, ypart), (h_y, sib))[n]
        return send(
            buf.at[k, block], buf.at[k, block], ag_s.at[use, k, n], ag_r.at[use, k, n], to
        )

    def gather_start(use, buf, k):
        gather_copy(use, buf, k, 1).start()
        gather_copy(use, buf, k, 0).start()

    def gather_forward(use, buf, k):
        gather_copy(use, buf, k, 1).wait_recv()
        gather_copy(use, buf, k, 2).start()

    def gather_finish(use, buf, k):
        gather_copy(use, buf, k, 0).wait_recv()
        gather_copy(use, buf, k, 2).wait_recv()

    def gather_sent(use, buf, k):
        for n in range(3):
            gather_copy(use, buf, k, n).wait_send()

    def sum_copy(use, k, n):
        src, dst, to = ((rs_core_out, rs_core_in, sib), (rs_y_out, rs_y_in, ypart))[n]
        return send(src.at[k], dst.at[k], rs_s.at[use, k, n], rs_r.at[use, k, n], to)

    def sum_start(use, k, part):
        for other in (0, 1):
            rs_core_out[k, other] = part(2 * other + 1 - core).astype(BF16)
        sum_copy(use, k, 0).start()
        rs_y_out[k] = part(2 * (1 - y) + core).astype(BF16)
        rs_own[k] = part(h)

    def sum_forward(use, k):
        sum_copy(use, k, 0).wait_recv()
        rs_y_out[k] = (rs_y_out[k].astype(F32) + rs_core_in[k, 1 - y].astype(F32)).astype(BF16)
        sum_copy(use, k, 1).start()

    def sum_finish(use, k):
        sum_copy(use, k, 1).wait_recv()
        return rs_own[k] + rs_core_in[k, y].astype(F32) + rs_y_in[k].astype(F32)

    def sum_sent(use, k):
        for n in range(2):
            sum_copy(use, k, n).wait_send()

    if inner:
        (g, rc, rx, rz, ry, f_send, f_got, wres, vecs, heads_in, dp_out, dp_in,
         w_s, w_r, c_s, c_r, f_s, f_r, m_s, m_r) = remote
        wup_in, wdown_in = w_in
        dwqkv, dwout, dup, ddown = d_first
        gw = gg = g
        z, x = d // 2, d % 2
        xpart, above, below = (d + 1 - 2 * x, h), (d + 2, h), (d - 2, h)
        peers = [lax.rem(d + n, 8) for n in range(1, 8)]
        greeted = [sib, ypart, (d, (h_sib + 2) % 4)] + [(p, h) for p in peers]
    else:
        gw, (acc_out, gg) = w_in[0], d_first
        greeted = [sib, ypart]

    def w_y():
        block = g.at[core, y, z, x]
        return send(block, block, w_s.at[0], w_r.at[0], ypart)

    def w_up(v, s, origin):
        block = g.at[core, y + v - 2 * y * v, origin, x]
        n = 3 * v + s
        return send(block, block, w_s.at[n], w_r.at[n], above)

    def w_down(v, s, origin):
        block = g.at[core, y + v - 2 * y * v, origin, x]
        n = 6 + 3 * v + s
        return send(block, block, w_s.at[n], w_r.at[n], below)

    def w_x(v, origin, side):
        block = g.at[core, y + v - 2 * y * v, origin, side]
        n = 13 + 4 * v + origin
        return send(block, block, w_s.at[n], w_r.at[n], xpart)

    def w_core(v, origin, side, at):
        block = g.at[at, y + v - 2 * y * v, origin, side]
        n = 21 + 8 * v + 2 * origin + side
        return send(block, block, w_s.at[n], w_r.at[n], sib)

    def w_begin():
        g[core, y, z, x] = jnp.zeros((480, LANES), BF16)
        g[core, y, z, x, 0:240, 0:USED] = wup_in[...].astype(F32).T.astype(BF16)
        g[core, y, z, x, 240:480, 0:USED] = wdown_in[...]

    def w_here(v, origin):
        w_x(v, origin, x).start()
        w_core(v, origin, x, core).start()

    def w_first(v):
        if v:
            w_y().wait_recv()
        else:
            w_y().start()
        pl.when(z < 3)(lambda: w_up(v, 1, z).start())
        pl.when(z > 0)(lambda: w_down(v, 1, z).start())
        w_here(v, z)

    def w_step(v, s):
        @pl.when(z >= s)
        def _():
            w_up(v, s, z - s).wait_recv()
            if s < 3:
                pl.when(z < 3)(lambda: w_up(v, s + 1, z - s).start())
            w_here(v, z - s)

        @pl.when(z + s <= 3)
        def _():
            w_down(v, s, z + s).wait_recv()
            if s < 3:
                pl.when(z > 0)(lambda: w_down(v, s + 1, z + s).start())
            w_here(v, z + s)

    def w_other(v, s):
        def one(origin):
            w_x(v, origin, 1 - x).wait_recv()
            w_core(v, origin, 1 - x, core).start()

        if s == 0:
            one(z)
        else:
            pl.when(z >= s)(lambda: one(z - s))
            pl.when(z + s <= 3)(lambda: one(z + s))

    def w_end():
        for v in (0, 1):
            for origin in range(4):
                for side in (0, 1):
                    w_core(v, origin, side, 1 - core).wait_recv()

    def w_sent():
        w_y().wait_send()
        for v in (0, 1):
            for s in (1, 2, 3):
                pl.when((z >= s - 1) & (z < 3))(lambda: w_up(v, s, z - s + 1).wait_send())
                pl.when((z + s - 1 <= 3) & (z > 0))(lambda: w_down(v, s, z + s - 1).wait_send())
            for origin in range(4):
                w_x(v, origin, x).wait_send()
                for side in (0, 1):
                    w_core(v, origin, side, core).wait_send()

    def assemble():
        def step(i, _):
            parts = [gw[n % 2, n // 2, i // 2, i % 2] for n in range(4)]
            full = nn(jnp.concatenate(parts, axis=1), spread[...]).astype(BF16)
            r = pl.ds(pl.multiple_of(i * 240, 240), 240)
            wup[r, :] = full[0:240]
            wdown[r, :] = full[240:480]
            return 0

        lax.fori_loop(0, 8, step, 0)

    order = (3, 0, 2, 1)

    def g_core(v, origin):
        n = 4 * v + origin
        return send(g.at[1 - core, v, origin], rc.at[v, origin], c_s.at[n], c_r.at[n], sib)

    def g_x(v, origin):
        n = 8 + 4 * v + origin
        return send(g.at[core, v, origin, 1 - x], rx.at[v, origin], c_s.at[n], c_r.at[n], xpart)

    def g_up(v, s, to):
        n = 15 + 3 * v + s
        return send(g.at[core, v, to, x], rz.at[0, v, s - 1], c_s.at[n], c_r.at[n], above)

    def g_down(v, s, to):
        n = 21 + 3 * v + s
        return send(g.at[core, v, to, x], rz.at[1, v, s - 1], c_s.at[n], c_r.at[n], below)

    def g_y():
        return send(g.at[core, 1 - y, z, x], ry, c_s.at[28], c_r.at[28], ypart)

    def add_block(v, origin, side, ref):
        g[core, v, origin, side] = (
            g[core, v, origin, side].astype(F32) + ref[...].astype(F32)
        ).astype(BF16)

    def g_begin():
        for v in (0, 1):
            for origin in order:
                g_core(v, origin).start()

    def g_first(v):
        for origin in order:
            g_core(v, origin).wait_recv()
            add_block(v, origin, 1 - x, rc.at[v, origin, 1 - x])
            g_x(v, origin).start()
        for origin in order:
            add_block(v, origin, x, rc.at[v, origin, x])

    def g_add_x(v, origins):
        for origin in origins:
            g_x(v, origin).wait_recv()
            add_block(v, origin, x, rx.at[v, origin])

    def g_send(v, s):
        pl.when(z < s)(lambda: g_up(v, s, 4 - s + z).start())
        pl.when(3 - z < s)(lambda: g_down(v, s, s + z - 4).start())

    def g_recv(v, s):
        @pl.when((z >= 1) & (z <= s))
        def _():
            g_up(v, s, 0).wait_recv()
            add_block(v, 3 - s + z, x, rz.at[0, v, s - 1])

        @pl.when((z <= 2) & (z >= 3 - s))
        def _():
            g_down(v, s, 0).wait_recv()
            add_block(v, s + z - 3, x, rz.at[1, v, s - 1])

    def g_y_begin(v):
        pl.when(y != v)(lambda: g_y().start())

    def g_last():
        g_y().wait_recv()
        total = g[core, y, z, x].astype(F32) + ry[...].astype(F32)
        dup[...] = total[0:240].T[0:USED]
        ddown[...] = total[240:480, 0:USED]
        for v in (0, 1):
            for n in range(4):
                g_core(v, n).wait_send()
                g_x(v, n).wait_send()
            for s in (1, 2, 3):
                pl.when(z < s)(lambda: g_up(v, s, 0).wait_send())
                pl.when(3 - z < s)(lambda: g_down(v, s, 0).wait_send())
        g_y().wait_send()

    spans = ((384, 512), (256, 384), (0, 256))

    def f_size(n):
        return (spans[n][1] - spans[n][0]) // 8

    def f_rows(n, p):
        return pl.ds(pl.multiple_of(spans[n][0] + p * f_size(n), 16), f_size(n))

    def f_out(n, p, slot):
        return send(
            f_send[n].at[p], f_got[n].at[slot], f_s.at[0, n, p], f_r.at[0, n, slot], (p, h)
        )

    def f_home(n, p, at):
        rows = wres.at[f_rows(n, at)]
        return send(rows, rows, f_s.at[1, n, p], f_r.at[1, n, at], (p, h))

    def f_begin(n):
        first, size = spans[n][0], f_size(n)
        if n == 2:
            for at in range(3):
                row = sums[0, at : at + 1, :]
                top = row.astype(BF16).astype(F32)
                vecs[2 * at : 2 * at + 1, :] = top
                vecs[2 * at + 1 : 2 * at + 2, :] = row - top
            extra = vecs[...].astype(BF16)
        for p in range(8):
            f_send[n][p, 0:size, :] = acc[first + p * size : first + (p + 1) * size, :].astype(BF16)
            if n == 2:
                f_send[n][p, size : size + 16, :] = extra
        f_got[n][d] = f_send[n][d]
        for p in peers:
            f_out(n, p, d).start()

    def f_back(n):
        size = f_size(n)
        for p in peers:
            f_out(n, p, p).wait_recv()
        total = f_got[n][0].astype(F32)
        for p in range(1, 8):
            total = total + f_got[n][p].astype(F32)
        wres[f_rows(n, d), :] = total[0:size].astype(BF16)
        for p in peers:
            f_home(n, p, d).start()
        if n == 2:
            for at in range(3):
                row = size + 2 * at
                sums[0, at : at + 1, :] = total[row : row + 1] + total[row + 1 : row + 2]
            m_begin(0)

    def f_end(n):
        for p in peers:
            f_home(n, p, p).wait_recv()

    def f_sent(n):
        for p in peers:
            f_out(n, p, d).wait_send()
            f_home(n, p, d).wait_send()

    near = (sib, ypart, (d, (h_sib + 2) % 4))

    def m_heads(b, n, at):
        return send(sums.at[b], heads_in.at[b, at], m_s.at[b, n], m_r.at[b, at], near[n])

    def m_dp(n, at):
        return send(dp_out, dp_in.at[at], m_s.at[1, 3 + n], m_r.at[1, 4 + at], (peers[n], h))

    def m_begin(b):
        heads_in[b, h] = sums[b]
        for n in range(3):
            m_heads(b, n, h).start()

    def m_total(b):
        for n in range(3):
            m_heads(b, n, near[n][1]).wait_recv()
        return heads_in[b, 0] + heads_in[b, 1] + heads_in[b, 2] + heads_in[b, 3]

    def m_middle():
        dp_out[...] = m_total(1)
        dp_in[d] = dp_out[...]
        for n in range(7):
            m_dp(n, d).start()

    def m_end():
        for n in range(7):
            m_dp(n, peers[n]).wait_recv()
        total = dp_in[0]
        for p in range(1, 8):
            total = total + dp_in[p]
        small[8:16, :] = total
        for n in range(3):
            m_heads(1, n, h).wait_send()
        for n in range(7):
            m_dp(n, d).wait_send()

    def m_last():
        total = m_total(0)
        small[0:8, :] = total
        small[0:1, 0:width] = (
            total[0:1, 0:width] - attn_bias[...] * total[1:2, 0:width]
        ) / attn_gain[...]
        small[2:3, :] = sums[0, 2:3, :]
        for n in range(3):
            m_heads(0, n, h).wait_send()

    def rows_of(k):
        return slice(k * BLOCK, (k + 1) * BLOCK)

    def add_sum(row, value):
        b, at = row // 8, row % 8
        sums[b, at : at + 1, 0 : value.shape[1]] += value

    barrier = pltpu.get_barrier_semaphore()
    for other in greeted:
        pl.semaphore_signal(barrier, inc=1, device_id=other, device_id_type=MESH)

    def first_norm(k):
        tok_in(k).wait()
        x_ = result[:, rows_of(k)].astype(F32).T
        tok[rows_of(k), :] = x_.astype(BF16)
        xhat, _ = norm(x_)
        n1[k, h, :, 0:width] = (xhat * attn_gain[...] + attn_bias[...]).astype(BF16)
        n1[k, h, :, width:512] = jnp.zeros((BLOCK, 512 - width), BF16)

    def tok_in(k):
        cols = pl.ds(k * BLOCK, BLOCK)
        return pltpu.make_async_copy(tok_hbm.at[:, cols], result.at[:, cols], in_s.at[k])

    grad_in = pltpu.make_async_copy(grad_hbm, grad_t, in_s.at[groups])
    for k in range(groups):
        tok_in(k).start()
    grad_in.start()
    first_norm(0)
    pl.semaphore_wait(barrier, len(greeted))
    gather_start(0, n1, 0)
    if inner:
        w_begin()
        w_first(0)
    for k in range(1, groups):
        first_norm(k)
        gather_start(0, n1, k)

    wq[0:width, :] = nn(wqkv[...], perm[...]).astype(BF16)
    wq[width:512, :] = jnp.zeros((512 - width, 3 * LANES), BF16)
    wqt[:, 0:width] = dims(perm[...], wqkv[...], 0, 1).astype(BF16)
    wqt[:, width:512] = jnp.zeros((3 * LANES, 512 - width), BF16)
    qkv_b[...] = dims(qkv_bias[...], perm[...].astype(F32), 1, 0, lax.Precision.HIGHEST)
    wo[:, width:512] = jnp.zeros((LANES, 512 - width), BF16)
    wo[:, 0:width] = jnp.concatenate(
        [wout[...].astype(F32), jnp.zeros((LANES - USED, width), F32)], axis=0
    ).astype(BF16)
    sums[...] = jnp.zeros_like(sums)
    acc[...] = jnp.zeros_like(acc)
    n2[:, width:512] = jnp.zeros((groups * BLOCK, 512 - width), BF16)
    df[:, width:512] = jnp.zeros((groups * BLOCK, 512 - width), BF16)
    for k in range(groups):
        da[k, h, :, width:512] = jnp.zeros((BLOCK, 512 - width), BF16)

    def ends_of(k):
        total, ends = 0, []
        for p in range(4):
            total = total + lengths[k, p]
            ends.append(total)
        return ends

    def project(k):
        ends = ends_of(k)
        at1 = lane(1)
        lo = jnp.where(at1 == USED, 0, group_rows + 1)
        hi = jnp.where(at1 == USED + 4, group_rows + 1, 0)
        for p in range(4):
            lo = jnp.where(at1 == USED + 1 + p, ends[p], lo)
            hi = jnp.where(at1 == USED + p, ends[p], hi)

        def step(i, _):
            r = pl.ds(pl.multiple_of(i * BLOCK, BLOCK), BLOCK)
            x_ = nn(n1[k, i], wq[...]) + qkv_b[...]
            c, s = cos[r, :], sin[r, :]
            at = lane(BLOCK)
            row = lax.broadcasted_iota(jnp.int32, (BLOCK, LANES), 0) + i * BLOCK
            inside = (row >= lo) & (row < hi)
            marks = (at >= USED) & (at < USED + 5)
            q = x_[:, 0:LANES]
            q = (q * c + partner(q) * s) * (HD ** (-0.5) * LOG2E)
            q_s[k, r, :] = jnp.where(at < USED, q, jnp.where(inside, 1.0, 0.0)).astype(BF16)
            key = x_[:, LANES : 2 * LANES]
            key = key * c + partner(key) * s
            k_s[k, r, :] = jnp.where(
                at < USED, key, jnp.where(marks & jnp.logical_not(inside), -BIG, 0.0)
            ).astype(BF16)
            v_s[k, r, :] = jnp.where(
                at < USED, x_[:, 2 * LANES : 3 * LANES], jnp.where(at < USED + 2, 1.0, 0.0)
            ).astype(BF16)
            return 0

        lax.fori_loop(0, steps, step, 0)

    def p_out(k, i):
        slot = (k * steps + i) % 2
        return pltpu.make_async_copy(pslot.at[slot], phbm.at[k, i], p_s.at[slot])

    def p_in(n):
        slot = n % 2
        return pltpu.make_async_copy(phbm.at[n // steps, n % steps], pslot.at[slot], p_s.at[slot])

    def run_hooks(hooks, i):
        for at, todo in hooks.items():

            @pl.when(i == at)
            def _():
                for one in todo:
                    one()

    def attend(k, hooks):
        def step(i, _):
            n = k * steps + i
            slot = n % 2
            run_hooks(hooks, i)

            @pl.when(n >= 2)
            def _():
                p_out(k, i).wait()

            r = pl.ds(pl.multiple_of(i * BLOCK, BLOCK), BLOCK)
            q = q_s[k, r, :]
            keys, vals = k_s[k], v_s[k]
            at = lane(BLOCK)

            def score(j):
                return nt(jnp.where(head_lanes(BLOCK, j) | (at >= USED), q, 0), keys)

            out = jnp.zeros((BLOCK, LANES), F32)
            inv = jnp.zeros((BLOCK, LANES), F32)
            s = score(0)
            for j in range(HEADS):
                later = score(j + 1) if j + 1 < HEADS else None
                e = jnp.exp2(s - jnp.max(s, axis=1, keepdims=True)).astype(BF16)
                pslot[slot, j] = e
                o = nn(e, vals)
                one = 1.0 / o[:, USED : USED + 1]
                out = jnp.where(head_lanes(BLOCK, j), o * one, out)
                inv = jnp.where(head_lanes(BLOCK, j), one, inv)
                s = later
            ctx[k, r, :] = out
            invl[k, r, :] = inv
            p_out(k, i).start()
            return 0

        lax.fori_loop(0, steps, step, 0)

    def out_part(k):
        def part(i):
            r = pl.ds(pl.multiple_of(i * BLOCK, BLOCK), BLOCK)
            return nn(ctx[k, r, :].astype(BF16), wo[...])

        return part

    if inner:
        first, step, other = (
            (lambda *a, f=f: partial(f, *a)) for f in (w_first, w_step, w_other)
        )
        w_plan = (
            {1: [first(1), step(0, 2)], 3: [step(1, 1), step(0, 3)]},
            {0: [step(1, 2), other(0, 0), other(0, 1), other(1, 0)],
             2: [step(1, 3), other(0, 2), other(1, 1)]},
            {0: [other(0, 3), other(1, 2)], 2: [other(1, 3)]},
        )
    gather_forward(0, n1, 0)
    if inner:
        w_step(0, 1)
    for k in range(groups):
        gather_finish(0, n1, k)
        project(k)
        if k > 0:
            sum_forward(0, k - 1)
        hooks = {}
        if k + 1 < groups:
            hooks[3] = [partial(gather_forward, 0, n1, k + 1)]
        if inner:
            for at, todo in w_plan[k].items():
                hooks.setdefault(at, []).extend(todo)
        attend(k, hooks)
        sum_start(0, k, out_part(k))
    sum_forward(0, groups - 1)
    for n in (groups * steps, groups * steps + 1):
        p_in(n % 2).wait()
    p_in(0).start()
    p_in(1).start()
    if inner:
        w_end()
    assemble()
    if inner:
        w_sent()

    grad_in.wait()

    def weight_of(k):
        ends = ends_of(k)
        row = lax.broadcasted_iota(jnp.int32, (BLOCK, 1), 0) + h * BLOCK
        w = jnp.zeros((BLOCK, 1), F32)
        for p in reversed(range(4)):
            w = jnp.where(row < ends[p], cw[ids[k, p]], w)
        return w

    def ffn_pre(k):
        r = rows_of(k)
        middle = tok[r, :].astype(F32) + sum_finish(0, k)[:, 0:width] + out_bias[...]
        mid[r, :] = middle
        xhat, _ = norm(middle)
        n2[r, 0:width] = (xhat * ffn_gain[...] + ffn_bias[...]).astype(BF16)
        grad[r, :] = grad_t[:, r].astype(F32).T.astype(BF16)
        d_ffn = (grad[r, :].astype(F32) * weight_of(k)).astype(BF16)
        df[r, 0:width] = d_ffn
        add_sum(15, jnp.sum(d_ffn.astype(F32), axis=0, keepdims=True))
        n2p[r, :] = nt(n2[r, :], spread[...]).astype(BF16)
        dfp[r, :] = nt(df[r, :], spread[...]).astype(BF16)

    def ffn_core(first, last):
        r = slice(first * BLOCK, last * BLOCK)

        def step(t, _):
            f = pl.ds(pl.multiple_of(t * 480, 480), 480)
            wu, wd = wup[f, :], wdown[f, :]
            u = nt(n2[r, :], wu) + up_bias[pl.ds(t, 1), :]
            phi = 0.5 + 0.5 * lax.erf(u * (0.5**0.5))
            hid = (u * phi).astype(BF16)
            slope = phi + u * (jnp.exp(u * u * -0.5) * 0.3989422804014327)
            out = nn(hid, wd)
            du = (nt(df[r, :], wd) * slope).astype(BF16)
            dx = nn(du, wu)
            sums[1, pl.ds(t, 1), 0:480] += jnp.sum(du.astype(F32), axis=0, keepdims=True)

            @pl.when(t == 0)
            def _():
                facc[r, :] = out
                dn2[r, :] = dx

            @pl.when(t > 0)
            def _():
                facc[r, :] += out
                dn2[r, :] += dx

            for part, wide in enumerate((tn(du, n2p[r, :]), tn(hid, dfp[r, :]))):
                fr = slice(part * 240, part * 240 + 240)
                for side in (0, 1):
                    for n in range(4):
                        new = wide[side * 240 : side * 240 + 240, n * LANES : (n + 1) * LANES]
                        if first > 0:
                            new = new + gg[n % 2, n // 2, t, side, fr, :].astype(F32)
                        gg[n % 2, n // 2, t, side, fr, :] = new.astype(BF16)
            return 0

        lax.fori_loop(0, 4, step, 0)

    def ffn_post(k):
        r = rows_of(k)
        middle = mid[r, :]
        result[:, r] = (middle + facc[r, 0:width] + down_bias[...]).T.astype(BF16)
        g_ = dn2[r, 0:width]
        xhat, rstd = norm(middle)
        add_sum(13, jnp.sum(g_ * xhat, axis=0, keepdims=True))
        add_sum(14, jnp.sum(g_, axis=0, keepdims=True))
        d_result = grad[r, :].astype(F32) * weight_of(k)
        d_middle = d_result + norm_back(g_, ffn_gain[...], xhat, rstd)
        mid[r, :] = d_middle
        low = d_middle.astype(BF16)
        da[k, h, :, 0:width] = low
        add_sum(12, jnp.sum(low.astype(F32), axis=0, keepdims=True))
        gather_start(1, da, k)

    for k in range(groups - 1):
        ffn_pre(k)
    ffn_core(0, groups - 1)
    for k in range(groups - 1):
        ffn_post(k)
    ffn_pre(groups - 1)
    ffn_core(groups - 1, groups)
    if inner:
        g_begin()
    ffn_post(groups - 1)
    if inner:
        m_begin(1)
    for k in range(groups):
        gather_sent(0, n1, k)
        sum_sent(0, k)

    def back_prep(k):
        def step(i, _):
            r = pl.ds(pl.multiple_of(i * BLOCK, BLOCK), BLOCK)
            g_ = nt(da[k, i], wo[...]).astype(BF16).astype(F32)
            g_ = (g_ * invl[k, r, :]).astype(BF16)
            do_s[r, :] = g_
            dot_t[:, r] = g_.astype(F32).T
            q_t[:, r] = q_s[k, r, :].astype(F32).T
            acc[3 * LANES : 4 * LANES, :] += tn(ctx[k, r, :].astype(BF16), da[k, i])
            return 0

        lax.fori_loop(0, steps, step, 0)
        dk_t[...] = jnp.zeros_like(dk_t)
        dv_t[...] = jnp.zeros_like(dv_t)

    def back(k, hooks):
        def step(i, _):
            n = k * steps + i
            slot = n % 2
            run_hooks(hooks, i)
            p_in(n).wait()
            r = pl.ds(pl.multiple_of(i * BLOCK, BLOCK), BLOCK)
            g_ = do_s[r, :].astype(F32)
            prod = g_ * ctx[k, r, :]
            keys, vals = k_s[k], v_s[k]
            at = lane(BLOCK)

            def d_prob(j):
                mine = head_lanes(BLOCK, j)
                total = jnp.sum(jnp.where(mine, prod, 0.0), axis=1, keepdims=True)
                top = total.astype(BF16).astype(F32)
                row = jnp.where(at == USED, -top, jnp.where(at == USED + 1, top - total, 0.0))
                return nt(jnp.where(mine, g_, row).astype(BF16), vals)

            out = jnp.zeros((BLOCK, LANES), F32)
            dp = d_prob(0)
            for j in range(HEADS):
                later = d_prob(j + 1) if j + 1 < HEADS else None
                e = pslot[slot, j]
                ds = (e.astype(F32) * dp).astype(BF16)
                out = jnp.where(head_lanes(BLOCK, j), nn(ds, keys), out)
                hs = slice(j * HD, (j + 1) * HD)
                dk_t[hs, :] += nn(q_t[hs, r].astype(BF16), ds)
                if k < groups - 1:
                    dv_t[hs, :] += nn(dot_t[hs, r].astype(BF16), e)
                dp = later
            dq[r, :] = out

            @pl.when(n + 2 < groups * steps)
            def _():
                p_in(n + 2).start()

            return 0

        lax.fori_loop(0, steps, step, 0)

    def back_post(k):
        def step(i, _):
            r = pl.ds(pl.multiple_of(i * BLOCK, BLOCK), BLOCK)
            c, s = cos[r, :], sin[r, :]
            a = dq[r, :] * HD ** (-0.5)
            a = a * c - partner(a) * s
            b = dk_t[:, r].T * (1.0 / LOG2E)
            b = b * c - partner(b) * s
            if k < groups - 1:
                g_ = jnp.concatenate([a, b, dv_t[:, r].T], axis=1).astype(BF16)
            else:
                g_ = jnp.concatenate([a, b], axis=1).astype(BF16)
            cols = g_.shape[1]
            dqkv[r, 0:cols] = g_
            add_sum(2, jnp.sum(g_.astype(F32), axis=0, keepdims=True))
            acc[0:cols, :] += tn(g_, n1[k, i])
            return 0

        lax.fori_loop(0, steps, step, 0)

    def back_values(k):
        def step(i, _):
            n = k * steps + i
            slot = n % 2
            p_in(n).wait()
            r = pl.ds(pl.multiple_of(i * BLOCK, BLOCK), BLOCK)
            for j in range(HEADS):
                hs = slice(j * HD, (j + 1) * HD)
                dv_t[hs, :] += nn(dot_t[hs, r].astype(BF16), pslot[slot, j])
            p_in(k * steps + (i + 2) % steps).start()
            return 0

        lax.fori_loop(0, steps, step, 0)

        def post(i, _):
            r = pl.ds(pl.multiple_of(i * BLOCK, BLOCK), BLOCK)
            g_ = dv_t[:, r].T.astype(BF16)
            dqkv[r, 2 * LANES : 3 * LANES] = g_
            sums[0, 2:3, 2 * LANES : 3 * LANES] += jnp.sum(g_.astype(F32), axis=0, keepdims=True)
            acc[2 * LANES : 3 * LANES, :] += tn(g_, n1[k, i])
            return 0

        lax.fori_loop(0, steps, post, 0)

    def norm_sums():
        add_sum(0, jnp.sum(acc[0 : 3 * LANES, :] * wqt[...].astype(F32), axis=0, keepdims=True))
        add_sum(1, dims(sums[0, 2:3, 0 : 3 * LANES], wqt[...].astype(F32), 1, 0, lax.Precision.HIGHEST))

    def tokens_part(i):
        r = pl.ds(pl.multiple_of(i * BLOCK, BLOCK), BLOCK)
        return nt(dqkv[r, :], wq[...])

    def last_norm(k):
        r = rows_of(k)
        g_ = sum_finish(1, k)[:, 0:width]
        xhat, rstd = norm(tok[r, :].astype(F32))
        dtok_out[:, r] = (mid[r, :] + norm_back(g_, attn_gain[...], xhat, rstd)).T

    if inner:
        wait_x, go, take, first = (
            (lambda *a, f=f: partial(f, *a)) for f in (g_add_x, g_send, g_recv, g_first)
        )
        a, b = order[:2], order[2:]
        g_plan = (
            {0: [first(0)], 1: [first(1)], 3: [wait_x(0, a), go(0, 1)]},
            {0: [wait_x(0, b), take(0, 1), go(0, 2), m_middle],
             1: [wait_x(1, a), go(1, 1)],
             2: [take(0, 2), go(0, 3)],
             3: [wait_x(1, b), take(1, 1), go(1, 2)]},
            {0: [take(0, 3), partial(g_y_begin, 0), take(1, 2), go(1, 3)],
             2: [take(1, 3), partial(g_y_begin, 1), partial(f_back, 0), m_end],
             3: [partial(f_back, 1)]},
        )
    gather_forward(1, da, 0)
    for k in range(groups):
        gather_finish(1, da, k)
        back_prep(k)
        if k > 0:
            sum_forward(1, k - 1)
        if k == groups - 1:
            if inner:
                f_begin(0)
            back_values(k)
            if inner:
                f_begin(1)
        hooks = {}
        if k == 0:
            hooks[1] = [partial(gather_forward, 1, da, 1)]
            hooks[3] = [partial(gather_forward, 1, da, 2)]
        if inner:
            for at, todo in g_plan[k].items():
                hooks.setdefault(at, []).extend(todo)
        back(k, hooks)
        back_post(k)
        if k == groups - 1:
            norm_sums()
        if inner and k == groups - 1:
            f_begin(2)
        sum_start(1, k, tokens_part)
    for k in range(groups - 1):
        last_norm(k)
    sum_forward(1, groups - 1)
    if inner:
        f_back(2)
    last_norm(groups - 1)
    if inner:
        g_last()
        for n in range(3):
            f_end(n)
        dwqkv[...] = dims(wres[0 : 3 * LANES, :], perm[...], 0, 1)[0:width]
        dwout[...] = wres[3 * LANES : 4 * LANES, :].astype(F32)[0:USED, 0:width]
        m_last()
        for n in range(3):
            f_sent(n)
    else:
        small[0:8, :] = sums[0]
        small[8:16, :] = sums[1]
        acc_out[...] = acc[...]
    for k in range(groups):
        gather_sent(1, da, k)
        sum_sent(1, k)


def permutation():
    table = np.zeros((3 * USED, 3 * LANES), np.float32)
    for j in range(HEADS):
        for part in range(3):
            for i in range(HD):
                table[(j * 3 + part) * HD + i, part * LANES + j * HD + i] = 1.0
    return table


def turns(group_rows):
    freq = 10000.0 ** (-2.0 * np.arange(HD // 2) / HD)
    angle = np.arange(group_rows)[:, None] * freq[None, :]
    c = np.zeros((group_rows, LANES), np.float32)
    s = np.zeros((group_rows, LANES), np.float32)
    c[:, :USED] = np.tile(np.cos(angle), (1, 2 * HEADS))
    s[:, :USED] = np.tile(np.concatenate([-np.sin(angle), np.sin(angle)], axis=1), (1, HEADS))
    return c, s


def spreading():
    table = np.zeros((4 * LANES, 4 * LANES), np.float32)
    for n in range(4):
        for i in range(USED):
            table[n * LANES + i, n * USED + i] = 1.0
    return table


def layer(
    inner, tokens, wqkv, wout, w_in, attn_gain, attn_bias, qkv_bias, out_bias, ffn_gain,
    ffn_bias, up_bias, down_bias, lengths, ids, cw, grad,
):
    own, width = tokens.shape
    groups = lengths.shape[0]
    ff = up_bias.shape[0]
    group_rows = 4 * BLOCK
    c, s = turns(group_rows)
    vm = pl.BlockSpec(memory_space=pltpu.VMEM)
    sm = pl.BlockSpec(memory_space=pltpu.SMEM)
    anywhere = pl.BlockSpec(memory_space=pl.ANY)
    shape = jax.ShapeDtypeStruct
    row = lambda v: v.reshape(1, -1)
    v, dma = pltpu.VMEM, pltpu.SemaphoreType.DMA
    chunks = (2, 2, 4, 2, 480, LANES)
    if inner:
        first = (
            shape((width, 3 * USED), F32),
            shape((USED, width), F32),
            shape((USED, 240), F32),
            shape((240, USED), F32),
        )
        remote = [
            v(chunks, BF16),
            v((2, 4, 2, 480, LANES), BF16),
            v((2, 4, 480, LANES), BF16),
            v((2, 2, 3, 480, LANES), BF16),
            v((480, LANES), BF16),
            [v((8, n, 512), BF16) for n in (16, 16, 48)],
            [v((8, n, 512), BF16) for n in (16, 16, 48)],
            v((4 * LANES, 512), BF16),
            v((16, 512), F32),
            v((2, 4, 8, 512), F32),
            v((8, 512), F32),
            v((8, 8, 512), F32),
            dma((37,)),
            dma((37,)),
            dma((29,)),
            dma((29,)),
            dma((2, 3, 8)),
            dma((2, 3, 8)),
            dma((2, 10)),
            dma((2, 12)),
        ]
    else:
        first = (shape((4 * LANES, 512), F32), shape(chunks, BF16))
        remote = []
    return pl.pallas_call(
        partial(body, inner),
        out_shape=(
            shape((width, own), BF16),
            shape((width, own), F32),
            first,
            shape((16, 512), F32),
            shape((groups, 4, HEADS, BLOCK, group_rows), BF16),
        ),
        in_specs=[anywhere] * 2 + [vm] * 2 + [[vm] * len(w_in)] + [vm] * 12 + [sm] * 3,
        out_specs=(vm, vm, (vm,) * len(first), vm, anywhere),
        scratch_shapes=[
            v((width, own), BF16),
            v((own, width), BF16),
            v((own, width), BF16),
            dma((groups + 1,)),
            v((groups, 4, BLOCK, 512), BF16),
            v((512, 3 * LANES), BF16),
            v((3 * LANES, 512), BF16),
            v((LANES, 512), BF16),
            v((1, 3 * LANES), F32),
            v((groups, group_rows, LANES), BF16),
            v((groups, group_rows, LANES), BF16),
            v((groups, group_rows, LANES), BF16),
            v((groups, group_rows, LANES), F32),
            v((groups, group_rows, LANES), F32),
            v((2, HEADS, BLOCK, group_rows), BF16),
            v((groups, 2, BLOCK, 512), BF16),
            v((groups, 2, BLOCK, 512), BF16),
            v((groups, BLOCK, 512), BF16),
            v((groups, BLOCK, 512), BF16),
            v((groups, BLOCK, 512), F32),
            v((own, width), F32),
            v((own, 512), BF16),
            v((own, 512), BF16),
            v((own, 512), BF16),
            v((own, 512), BF16),
            v((own, 512), F32),
            v((own, 512), F32),
            v((ff, 512), BF16),
            v((ff, 512), BF16),
            v((groups, 4, BLOCK, 512), BF16),
            v((group_rows, LANES), BF16),
            v((LANES, group_rows), F32),
            v((LANES, group_rows), F32),
            v((group_rows, LANES), F32),
            v((LANES, group_rows), F32),
            v((LANES, group_rows), F32),
            v((group_rows, 3 * LANES), BF16),
            v((2, 8, 512), F32),
            v((4 * LANES, 512), F32),
            dma((2, groups, 3)),
            dma((2, groups, 3)),
            dma((2, groups, 2)),
            dma((2, groups, 2)),
            dma((2,)),
            remote,
        ],
        compiler_params=pltpu.CompilerParams(
            collective_id=0, has_side_effects=True, vmem_limit_bytes=62 * 2**20
        ),
        name="layer",
    )(
        tokens.T, grad.T, wqkv, wout, w_in, row(attn_gain), row(attn_bias), row(qkv_bias),
        row(out_bias), row(ffn_gain), row(ffn_bias), up_bias.reshape(4, 480), row(down_bias),
        jnp.asarray(permutation(), BF16), jnp.asarray(spreading(), BF16), jnp.asarray(c),
        jnp.asarray(s), lengths, ids, cw,
    )


def local(
    tokens, attn_norm_gain, attn_norm_bias, qkv_weight, qkv_bias, out_weight, out_bias,
    ffn_norm_gain, ffn_norm_bias, up_weight, up_bias, down_weight, down_bias, lengths,
    cluster_ids, cluster_weight, grad_out,
):
    width = tokens.shape[1]
    ff = up_bias.shape[0]
    inner = lax.axis_size("dp") == 8
    if inner:
        w_in = [up_weight, down_weight]
    else:
        part = jnp.stack([up_weight.T, down_weight], axis=0)
        part = lax.all_gather(part, "dp", axis=1, tiled=True)
        part = lax.all_gather(part, "heads", axis=0)
        part = jnp.pad(part, ((0, 0),) * 3 + ((0, LANES - USED),))
        part = part.reshape(2, 2, 2, 4, 2, 240, LANES)
        w_in = [part.transpose(1, 0, 3, 4, 2, 5, 6).reshape(2, 2, 4, 2, 480, LANES)]
    result, dtok, first, small, _ = layer(
        inner, tokens, qkv_weight, out_weight, w_in, attn_norm_gain, attn_norm_bias,
        qkv_bias, out_bias, ffn_norm_gain, ffn_norm_bias, up_bias, down_bias, lengths,
        cluster_ids, cluster_weight, grad_out,
    )
    if inner:
        dwqkv, dwout, dup, ddown = first
    else:
        acc, grads = first
        acc, own_sums = lax.psum((acc, small[2]), "dp")
        small = lax.psum(small, ("dp", "heads")).at[2].set(own_sums)
        gain_sum = (small[0, :width] - attn_norm_bias * small[1, :width]) / attn_norm_gain
        small = small.at[0, :width].set(gain_sum)
        grads = grads.reshape(2, 2, 4, 2, 2, 240, LANES).transpose(1, 0, 4, 2, 3, 5, 6)
        grads = grads.reshape(4, 2, ff, LANES)[..., :USED]
        grads = lax.psum_scatter(grads, "heads", scatter_dimension=0).astype(F32)
        grads = lax.psum_scatter(grads, "dp", scatter_dimension=1, tiled=True)
        dup, ddown = grads[0].T, grads[1]
        dwqkv = acc[: 3 * LANES, :width].reshape(3, LANES, width)[:, :USED]
        dwqkv = dwqkv.reshape(3, HEADS, HD, width).transpose(3, 1, 0, 2).reshape(width, 3 * USED)
        dwout = acc[3 * LANES : 3 * LANES + USED, :width]
    dqkvb = small[2, : 3 * LANES].reshape(3, LANES)[:, :USED].reshape(3, HEADS, HD)
    dqkvb = dqkvb.transpose(1, 0, 2).reshape(-1)
    return (
        result.T, dtok.T, small[0, :width], small[1, :width], dwqkv, dqkvb, dwout,
        small[12, :width], small[13, :width], small[14, :width], dup,
        small[8:12, :480].reshape(ff), ddown, small[15, :width],
    )


def solution(mesh):
    placed = (
        P(("dp", "heads"), None), P(), P(), P(None, "heads"), P("heads"), P("heads", None), P(),
        P(), P(), P("heads", "dp"), P(), P("dp", "heads"), P(), P("dp", None), P("dp", None),
        P(), P(("dp", "heads"), None),
    )
    given = (
        P(("dp", "heads"), None), P(("dp", "heads"), None), P(), P(), P(None, "heads"), P("heads"),
        P("heads", None), P(), P(), P(), P("heads", "dp"), P(), P("dp", "heads"), P(),
    )
    return jax.shard_map(local, mesh=mesh, in_specs=placed, out_specs=given, check_vma=False)
```

```python
from functools import partial

import jax
import jax.numpy as jnp
import numpy as np
from jax import lax
from jax.experimental import pallas as pl
from jax.experimental.pallas import tpu as pltpu
from jax.sharding import PartitionSpec as P

F32, BF16 = jnp.float32, jnp.bfloat16
MESH = pl.DeviceIdType.MESH
HD = 24
HEADS = 5
USED = HEADS * HD
LANES = 128
EPSILON = 1e-05
LOG2E = 1.4426950408889634
BIG = 1e30
BLOCK = 256


def dims(a, b, ca, cb, precision=None):
    return lax.dot_general(
        a, b, (((ca,), (cb,)), ((), ())), preferred_element_type=F32, precision=precision
    )


def nn(a, b):
    return dims(a, b, 1, 0)


def nt(a, b):
    return dims(a, b, 1, 1)


def tn(a, b):
    return dims(a, b, 0, 0)


def lane(rows, width=LANES):
    return lax.broadcasted_iota(jnp.int32, (rows, width), 1)


def head_lanes(rows, j):
    at = lane(rows)
    return (at >= HD * j) & (at < HD * (j + 1))


def partner(x):
    at = lane(x.shape[0])
    half = HD // 2
    return jnp.where(
        at % HD < half, pltpu.roll(x, LANES - half, 1), pltpu.roll(x, half, 1)
    )


def norm(x):
    centred = x - jnp.mean(x, axis=-1, keepdims=True)
    rstd = lax.rsqrt(jnp.mean(centred * centred, axis=-1, keepdims=True) + EPSILON)
    return centred * rstd, rstd


def norm_back(g, gain, xhat, rstd):
    n = g * gain
    return rstd * (
        n
        - jnp.mean(n, axis=-1, keepdims=True)
        - xhat * jnp.mean(n * xhat, axis=-1, keepdims=True)
    )


def body(
    inner, tok_hbm, grad_hbm, wqkv, wout, w_in, attn_gain, attn_bias, out_bias, ffn_gain,
    ffn_bias, wide_bias, down_bias, perm, spread, cos, sin, lengths, ids, cw,
    result, dtok_out, d_first, small, phbm,
    grad_t, tok, grad, in_s,
    n1, wq, wqt, wo, qkv_b, q_s, k_s, v_s, ctx, invl, pslot,
    rs_core_out, rs_core_in, rs_y_out, rs_y_in, rs_own,
    mid, n2, df, n2p, dfp, facc, dn2, wup, wdown, da, do_s, dot_t, q_t, dq, dk_t, dv_t, dqkv,
    sums, acc, ag_s, ag_r, rs_s, rs_r, p_s, remote,
):
    d, h = lax.axis_index("dp"), lax.axis_index("heads")
    core, y = h % 2, h // 2
    h_sib = h + 1 - 2 * core
    h_y = (h + 2) % 4
    sib, ypart = (d, h_sib), (d, h_y)
    groups = lengths.shape[0]
    width = tok.shape[1]
    group_rows = 4 * BLOCK
    steps = 4

    def send(src, dst, s, r, to):
        return pltpu.make_async_remote_copy(
            src_ref=src, dst_ref=dst, send_sem=s, recv_sem=r, device_id=to, device_id_type=MESH
        )

    def gather_copy(use, buf, k, n):
        block, to = ((h, sib), (h, ypart), (h_y, sib))[n]
        return send(
            buf.at[k, block], buf.at[k, block], ag_s.at[use, k, n], ag_r.at[use, k, n], to
        )

    def gather_start(use, buf, k):
        gather_copy(use, buf, k, 1).start()
        gather_copy(use, buf, k, 0).start()

    def gather_forward(use, buf, k):
        gather_copy(use, buf, k, 1).wait_recv()
        gather_copy(use, buf, k, 2).start()

    def gather_finish(use, buf, k):
        gather_copy(use, buf, k, 0).wait_recv()
        gather_copy(use, buf, k, 2).wait_recv()

    def gather_sent(use, buf, k):
        for n in range(3):
            gather_copy(use, buf, k, n).wait_send()

    def sum_copy(use, k, n):
        src, dst, to = ((rs_core_out, rs_core_in, sib), (rs_y_out, rs_y_in, ypart))[n]
        return send(src.at[k], dst.at[k], rs_s.at[use, k, n], rs_r.at[use, k, n], to)

    def sum_start(use, k, part):
        for other in (0, 1):
            rs_core_out[k, other] = part(2 * other + 1 - core).astype(BF16)
        sum_copy(use, k, 0).start()
        rs_y_out[k] = part(2 * (1 - y) + core).astype(BF16)
        rs_own[k] = part(h)

    def sum_forward(use, k):
        sum_copy(use, k, 0).wait_recv()
        rs_y_out[k] = (rs_y_out[k].astype(F32) + rs_core_in[k, 1 - y].astype(F32)).astype(BF16)
        sum_copy(use, k, 1).start()

    def sum_finish(use, k):
        sum_copy(use, k, 1).wait_recv()
        return rs_own[k] + rs_core_in[k, y].astype(F32) + rs_y_in[k].astype(F32)

    def sum_sent(use, k):
        for n in range(2):
            sum_copy(use, k, n).wait_send()

    if inner:
        (g, rc, rx, rz, ry, f_send, f_got, wres, vecs, heads_in, dp_out, dp_in,
         w_s, w_r, c_s, c_r, f_s, f_r, m_s, m_r) = remote
        wup_in, wdown_in = w_in
        dwqkv, dwout, dup, ddown = d_first
        gw = gg = g
        z, x = d // 2, d % 2
        xpart, above, below = (d + 1 - 2 * x, h), (d + 2, h), (d - 2, h)
        peers = [lax.rem(d + n, 8) for n in range(1, 8)]
        greeted = [sib, ypart, (d, (h_sib + 2) % 4)] + [(p, h) for p in peers]
    else:
        gw, (acc_out, gg) = w_in[0], d_first
        greeted = [sib, ypart]

    def w_y():
        block = g.at[core, y, z, x]
        return send(block, block, w_s.at[0], w_r.at[0], ypart)

    def w_up(v, s, origin):
        block = g.at[core, y + v - 2 * y * v, origin, x]
        n = 3 * v + s
        return send(block, block, w_s.at[n], w_r.at[n], above)

    def w_down(v, s, origin):
        block = g.at[core, y + v - 2 * y * v, origin, x]
        n = 6 + 3 * v + s
        return send(block, block, w_s.at[n], w_r.at[n], below)

    def w_x(v, origin, side):
        block = g.at[core, y + v - 2 * y * v, origin, side]
        n = 13 + 4 * v + origin
        return send(block, block, w_s.at[n], w_r.at[n], xpart)

    def w_core(v, origin, side, at):
        block = g.at[at, y + v - 2 * y * v, origin, side]
        n = 21 + 8 * v + 2 * origin + side
        return send(block, block, w_s.at[n], w_r.at[n], sib)

    def w_begin():
        g[core, y, z, x] = jnp.zeros((480, LANES), BF16)
        g[core, y, z, x, 0:240, 0:USED] = wup_in[...].astype(F32).T.astype(BF16)
        g[core, y, z, x, 240:480, 0:USED] = wdown_in[...]

    def w_here(v, origin):
        w_x(v, origin, x).start()
        w_core(v, origin, x, core).start()

    def w_first(v):
        if v:
            w_y().wait_recv()
        else:
            w_y().start()
        pl.when(z < 3)(lambda: w_up(v, 1, z).start())
        pl.when(z > 0)(lambda: w_down(v, 1, z).start())
        w_here(v, z)

    def w_step(v, s):
        @pl.when(z >= s)
        def _():
            w_up(v, s, z - s).wait_recv()
            if s < 3:
                pl.when(z < 3)(lambda: w_up(v, s + 1, z - s).start())
            w_here(v, z - s)

        @pl.when(z + s <= 3)
        def _():
            w_down(v, s, z + s).wait_recv()
            if s < 3:
                pl.when(z > 0)(lambda: w_down(v, s + 1, z + s).start())
            w_here(v, z + s)

    def w_other(v, s):
        def one(origin):
            w_x(v, origin, 1 - x).wait_recv()
            w_core(v, origin, 1 - x, core).start()

        if s == 0:
            one(z)
        else:
            pl.when(z >= s)(lambda: one(z - s))
            pl.when(z + s <= 3)(lambda: one(z + s))

    def w_end():
        for v in (0, 1):
            for origin in range(4):
                for side in (0, 1):
                    w_core(v, origin, side, 1 - core).wait_recv()

    def w_sent():
        w_y().wait_send()
        for v in (0, 1):
            for s in (1, 2, 3):
                pl.when((z >= s - 1) & (z < 3))(lambda: w_up(v, s, z - s + 1).wait_send())
                pl.when((z + s - 1 <= 3) & (z > 0))(lambda: w_down(v, s, z + s - 1).wait_send())
            for origin in range(4):
                w_x(v, origin, x).wait_send()
                for side in (0, 1):
                    w_core(v, origin, side, core).wait_send()

    def assemble():
        def step(i, _):
            parts = [gw[n % 2, n // 2, i // 2, i % 2] for n in range(4)]
            full = nn(jnp.concatenate(parts, axis=1), spread[...]).astype(BF16)
            r = pl.ds(pl.multiple_of(i * 240, 240), 240)
            wup[r, :] = full[0:240]
            wdown[r, :] = full[240:480]
            return 0

        lax.fori_loop(0, 8, step, 0)

    order = (3, 0, 2, 1)

    def g_core(v, origin):
        n = 4 * v + origin
        return send(g.at[1 - core, v, origin], rc.at[v, origin], c_s.at[n], c_r.at[n], sib)

    def g_x(v, origin):
        n = 8 + 4 * v + origin
        return send(g.at[core, v, origin, 1 - x], rx.at[v, origin], c_s.at[n], c_r.at[n], xpart)

    def g_up(v, s, to):
        n = 15 + 3 * v + s
        return send(g.at[core, v, to, x], rz.at[0, v, s - 1], c_s.at[n], c_r.at[n], above)

    def g_down(v, s, to):
        n = 21 + 3 * v + s
        return send(g.at[core, v, to, x], rz.at[1, v, s - 1], c_s.at[n], c_r.at[n], below)

    def g_y():
        return send(g.at[core, 1 - y, z, x], ry, c_s.at[28], c_r.at[28], ypart)

    def add_block(v, origin, side, ref):
        g[core, v, origin, side] = (
            g[core, v, origin, side].astype(F32) + ref[...].astype(F32)
        ).astype(BF16)

    def g_begin():
        for v in (0, 1):
            for origin in order:
                g_core(v, origin).start()

    def g_first(v):
        for origin in order:
            g_core(v, origin).wait_recv()
            add_block(v, origin, 1 - x, rc.at[v, origin, 1 - x])
            g_x(v, origin).start()
        for origin in order:
            add_block(v, origin, x, rc.at[v, origin, x])

    def g_add_x(v, origins):
        for origin in origins:
            g_x(v, origin).wait_recv()
            add_block(v, origin, x, rx.at[v, origin])

    def g_send(v, s):
        pl.when(z < s)(lambda: g_up(v, s, 4 - s + z).start())
        pl.when(3 - z < s)(lambda: g_down(v, s, s + z - 4).start())

    def g_recv(v, s):
        @pl.when((z >= 1) & (z <= s))
        def _():
            g_up(v, s, 0).wait_recv()
            add_block(v, 3 - s + z, x, rz.at[0, v, s - 1])

        @pl.when((z <= 2) & (z >= 3 - s))
        def _():
            g_down(v, s, 0).wait_recv()
            add_block(v, s + z - 3, x, rz.at[1, v, s - 1])

    def g_y_begin(v):
        pl.when(y != v)(lambda: g_y().start())

    def g_last():
        g_y().wait_recv()
        total = g[core, y, z, x].astype(F32) + ry[...].astype(F32)
        dup[...] = total[0:240].T[0:USED]
        ddown[...] = total[240:480, 0:USED]
        for v in (0, 1):
            for n in range(4):
                g_core(v, n).wait_send()
                g_x(v, n).wait_send()
            for s in (1, 2, 3):
                pl.when(z < s)(lambda: g_up(v, s, 0).wait_send())
                pl.when(3 - z < s)(lambda: g_down(v, s, 0).wait_send())
        g_y().wait_send()

    spans = ((384, 512), (256, 384), (0, 256))

    def f_size(n):
        return (spans[n][1] - spans[n][0]) // 8

    def f_rows(n, p):
        return pl.ds(pl.multiple_of(spans[n][0] + p * f_size(n), 16), f_size(n))

    def f_out(n, p, slot):
        return send(
            f_send[n].at[p], f_got[n].at[slot], f_s.at[0, n, p], f_r.at[0, n, slot], (p, h)
        )

    def f_home(n, p, at):
        rows = wres.at[f_rows(n, at)]
        return send(rows, rows, f_s.at[1, n, p], f_r.at[1, n, at], (p, h))

    def f_begin(n):
        first, size = spans[n][0], f_size(n)
        if n == 2:
            for at in range(3):
                row = sums[0, at : at + 1, :]
                top = row.astype(BF16).astype(F32)
                vecs[2 * at : 2 * at + 1, :] = top
                vecs[2 * at + 1 : 2 * at + 2, :] = row - top
            extra = vecs[...].astype(BF16)
        for p in range(8):
            f_send[n][p, 0:size, :] = acc[first + p * size : first + (p + 1) * size, :].astype(BF16)
            if n == 2:
                f_send[n][p, size : size + 16, :] = extra
        f_got[n][d] = f_send[n][d]
        for p in peers:
            f_out(n, p, d).start()

    def f_back(n):
        size = f_size(n)
        for p in peers:
            f_out(n, p, p).wait_recv()
        total = f_got[n][0].astype(F32)
        for p in range(1, 8):
            total = total + f_got[n][p].astype(F32)
        wres[f_rows(n, d), :] = total[0:size].astype(BF16)
        for p in peers:
            f_home(n, p, d).start()
        if n == 2:
            for at in range(3):
                row = size + 2 * at
                sums[0, at : at + 1, :] = total[row : row + 1] + total[row + 1 : row + 2]
            m_begin(0)

    def f_end(n):
        for p in peers:
            f_home(n, p, p).wait_recv()

    def f_sent(n):
        for p in peers:
            f_out(n, p, d).wait_send()
            f_home(n, p, d).wait_send()

    near = (sib, ypart, (d, (h_sib + 2) % 4))

    def m_heads(b, n, at):
        return send(sums.at[b], heads_in.at[b, at], m_s.at[b, n], m_r.at[b, at], near[n])

    def m_dp(n, at):
        return send(dp_out, dp_in.at[at], m_s.at[1, 3 + n], m_r.at[1, 4 + at], (peers[n], h))

    def m_begin(b):
        heads_in[b, h] = sums[b]
        for n in range(3):
            m_heads(b, n, h).start()

    def m_total(b):
        for n in range(3):
            m_heads(b, n, near[n][1]).wait_recv()
        return heads_in[b, 0] + heads_in[b, 1] + heads_in[b, 2] + heads_in[b, 3]

    def m_middle():
        dp_out[...] = m_total(1)
        dp_in[d] = dp_out[...]
        for n in range(7):
            m_dp(n, d).start()

    def m_end():
        for n in range(7):
            m_dp(n, peers[n]).wait_recv()
        total = dp_in[0]
        for p in range(1, 8):
            total = total + dp_in[p]
        small[8:16, :] = total
        for n in range(3):
            m_heads(1, n, h).wait_send()
        for n in range(7):
            m_dp(n, d).wait_send()

    def m_last():
        total = m_total(0)
        small[0:8, :] = total
        small[0:1, 0:width] = (
            total[0:1, 0:width] - attn_bias[...] * total[1:2, 0:width]
        ) / attn_gain[...]
        small[2:3, 0 : 3 * USED] = dims(
            sums[0, 2:3, 0 : 3 * LANES], perm[...].astype(F32), 1, 1, lax.Precision.HIGHEST
        )
        for n in range(3):
            m_heads(0, n, h).wait_send()

    def rows_of(k):
        return slice(k * BLOCK, (k + 1) * BLOCK)

    def add_sum(row, value):
        b, at = row // 8, row % 8
        sums[b, at : at + 1, 0 : value.shape[1]] += value

    barrier = pltpu.get_barrier_semaphore()
    for other in greeted:
        pl.semaphore_signal(barrier, inc=1, device_id=other, device_id_type=MESH)

    def first_norm(k):
        tok_in(k).wait()
        x_ = result[:, rows_of(k)].astype(F32).T
        tok[rows_of(k), :] = x_.astype(BF16)
        xhat, _ = norm(x_)
        n1[k, h, :, 0:width] = (xhat * attn_gain[...] + attn_bias[...]).astype(BF16)
        n1[k, h, :, width:512] = jnp.zeros((BLOCK, 512 - width), BF16)

    def tok_in(k):
        cols = pl.ds(k * BLOCK, BLOCK)
        return pltpu.make_async_copy(tok_hbm.at[:, cols], result.at[:, cols], in_s.at[k])

    grad_in = pltpu.make_async_copy(grad_hbm, grad_t, in_s.at[groups])
    for k in range(groups):
        tok_in(k).start()
    grad_in.start()
    first_norm(0)
    pl.semaphore_wait(barrier, len(greeted))
    gather_start(0, n1, 0)
    if inner:
        w_begin()
        w_first(0)
    for k in range(1, groups):
        first_norm(k)
        gather_start(0, n1, k)

    wq[0:width, :] = nn(wqkv[...], perm[...]).astype(BF16)
    wq[width:512, :] = jnp.zeros((512 - width, 3 * LANES), BF16)
    wqt[:, 0:width] = dims(perm[...], wqkv[...], 0, 1).astype(BF16)
    wqt[:, width:512] = jnp.zeros((3 * LANES, 512 - width), BF16)
    qkv_b[...] = dims(
        wide_bias[4:5, 0 : 3 * USED], perm[...].astype(F32), 1, 0, lax.Precision.HIGHEST
    )
    wo[:, width:512] = jnp.zeros((LANES, 512 - width), BF16)
    wo[:, 0:width] = jnp.concatenate(
        [wout[...].astype(F32), jnp.zeros((LANES - USED, width), F32)], axis=0
    ).astype(BF16)
    sums[...] = jnp.zeros_like(sums)
    acc[...] = jnp.zeros_like(acc)
    n2[:, width:512] = jnp.zeros((groups * BLOCK, 512 - width), BF16)
    df[:, width:512] = jnp.zeros((groups * BLOCK, 512 - width), BF16)
    for k in range(groups):
        da[k, h, :, width:512] = jnp.zeros((BLOCK, 512 - width), BF16)

    def ends_of(k):
        total, ends = 0, []
        for p in range(4):
            total = total + lengths[k, p]
            ends.append(total)
        return ends

    def project(k):
        ends = ends_of(k)
        at1 = lane(1)
        lo = jnp.where(at1 == USED, 0, group_rows + 1)
        hi = jnp.where(at1 == USED + 4, group_rows + 1, 0)
        for p in range(4):
            lo = jnp.where(at1 == USED + 1 + p, ends[p], lo)
            hi = jnp.where(at1 == USED + p, ends[p], hi)

        def step(i, _):
            r = pl.ds(pl.multiple_of(i * BLOCK, BLOCK), BLOCK)
            x_ = nn(n1[k, i], wq[...]) + qkv_b[...]
            c, s = cos[r, :], sin[r, :]
            at = lane(BLOCK)
            row = lax.broadcasted_iota(jnp.int32, (BLOCK, LANES), 0) + i * BLOCK
            inside = (row >= lo) & (row < hi)
            marks = (at >= USED) & (at < USED + 5)
            q = x_[:, 0:LANES]
            q = (q * c + partner(q) * s) * (HD ** (-0.5) * LOG2E)
            q_s[k, r, :] = jnp.where(at < USED, q, jnp.where(inside, 1.0, 0.0)).astype(BF16)
            key = x_[:, LANES : 2 * LANES]
            key = key * c + partner(key) * s
            k_s[k, r, :] = jnp.where(
                at < USED, key, jnp.where(marks & jnp.logical_not(inside), -BIG, 0.0)
            ).astype(BF16)
            v_s[k, r, :] = jnp.where(
                at < USED, x_[:, 2 * LANES : 3 * LANES], jnp.where(at < USED + 2, 1.0, 0.0)
            ).astype(BF16)
            return 0

        lax.fori_loop(0, steps, step, 0)

    def p_out(k, i):
        slot = (k * steps + i) % 2
        return pltpu.make_async_copy(pslot.at[slot], phbm.at[k, i], p_s.at[slot])

    def p_in(n):
        slot = n % 2
        return pltpu.make_async_copy(phbm.at[n // steps, n % steps], pslot.at[slot], p_s.at[slot])

    def run_hooks(hooks, i):
        for at, todo in hooks.items():

            @pl.when(i == at)
            def _():
                for one in todo:
                    one()

    def attend(k, hooks):
        def step(i, _):
            n = k * steps + i
            slot = n % 2
            run_hooks(hooks, i)

            @pl.when(n >= 2)
            def _():
                p_out(k, i).wait()

            r = pl.ds(pl.multiple_of(i * BLOCK, BLOCK), BLOCK)
            q = q_s[k, r, :]
            keys, vals = k_s[k], v_s[k]
            at = lane(BLOCK)

            def score(j):
                return nt(jnp.where(head_lanes(BLOCK, j) | (at >= USED), q, 0), keys)

            out = jnp.zeros((BLOCK, LANES), F32)
            inv = jnp.zeros((BLOCK, LANES), F32)
            s = score(0)
            for j in range(HEADS):
                later = score(j + 1) if j + 1 < HEADS else None
                e = jnp.exp2(s - jnp.max(s, axis=1, keepdims=True)).astype(BF16)
                pslot[slot, j] = e
                o = nn(e, vals)
                one = 1.0 / o[:, USED : USED + 1]
                out = jnp.where(head_lanes(BLOCK, j), o * one, out)
                inv = jnp.where(head_lanes(BLOCK, j), one, inv)
                s = later
            ctx[k, r, :] = out
            invl[k, r, :] = inv
            p_out(k, i).start()
            return 0

        lax.fori_loop(0, steps, step, 0)

    def out_part(k):
        def part(i):
            r = pl.ds(pl.multiple_of(i * BLOCK, BLOCK), BLOCK)
            return nn(ctx[k, r, :].astype(BF16), wo[...])

        return part

    if inner:
        first, step, other = (
            (lambda *a, f=f: partial(f, *a)) for f in (w_first, w_step, w_other)
        )
        w_plan = (
            {1: [first(1), step(0, 2)], 3: [step(1, 1), step(0, 3)]},
            {0: [step(1, 2), other(0, 0), other(0, 1), other(1, 0)],
             2: [step(1, 3), other(0, 2), other(1, 1)]},
            {0: [other(0, 3), other(1, 2)], 2: [other(1, 3)]},
        )
    gather_forward(0, n1, 0)
    if inner:
        w_step(0, 1)
    for k in range(groups):
        gather_finish(0, n1, k)
        project(k)
        if k > 0:
            sum_forward(0, k - 1)
        hooks = {}
        if k + 1 < groups:
            hooks[3] = [partial(gather_forward, 0, n1, k + 1)]
        if inner:
            for at, todo in w_plan[k].items():
                hooks.setdefault(at, []).extend(todo)
        attend(k, hooks)
        sum_start(0, k, out_part(k))
    sum_forward(0, groups - 1)
    for n in (groups * steps, groups * steps + 1):
        p_in(n % 2).wait()
    p_in(0).start()
    p_in(1).start()
    if inner:
        w_end()
    assemble()
    if inner:
        w_sent()

    grad_in.wait()

    def weight_of(k):
        ends = ends_of(k)
        row = lax.broadcasted_iota(jnp.int32, (BLOCK, 1), 0) + h * BLOCK
        w = jnp.zeros((BLOCK, 1), F32)
        for p in reversed(range(4)):
            w = jnp.where(row < ends[p], cw[ids[k, p]], w)
        return w

    def ffn_pre(k):
        r = rows_of(k)
        middle = tok[r, :].astype(F32) + sum_finish(0, k)[:, 0:width] + out_bias[...]
        mid[r, :] = middle
        xhat, _ = norm(middle)
        n2[r, 0:width] = (xhat * ffn_gain[...] + ffn_bias[...]).astype(BF16)
        grad[r, :] = grad_t[:, r].astype(F32).T.astype(BF16)
        d_ffn = (grad[r, :].astype(F32) * weight_of(k)).astype(BF16)
        df[r, 0:width] = d_ffn
        add_sum(15, jnp.sum(d_ffn.astype(F32), axis=0, keepdims=True))
        n2p[r, :] = nt(n2[r, :], spread[...]).astype(BF16)
        dfp[r, :] = nt(df[r, :], spread[...]).astype(BF16)

    def ffn_core(first, last):
        r = slice(first * BLOCK, last * BLOCK)

        def step(t, _):
            f = pl.ds(pl.multiple_of(t * 480, 480), 480)
            wu, wd = wup[f, :], wdown[f, :]
            u = nt(n2[r, :], wu) + wide_bias[pl.ds(t, 1), :]
            phi = 0.5 + 0.5 * lax.erf(u * (0.5**0.5))
            hid = (u * phi).astype(BF16)
            slope = phi + u * (jnp.exp(u * u * -0.5) * 0.3989422804014327)
            out = nn(hid, wd)
            du = (nt(df[r, :], wd) * slope).astype(BF16)
            dx = nn(du, wu)
            sums[1, pl.ds(t, 1), 0:480] += jnp.sum(du.astype(F32), axis=0, keepdims=True)

            @pl.when(t == 0)
            def _():
                facc[r, :] = out
                dn2[r, :] = dx

            @pl.when(t > 0)
            def _():
                facc[r, :] += out
                dn2[r, :] += dx

            for part, wide in enumerate((tn(du, n2p[r, :]), tn(hid, dfp[r, :]))):
                fr = slice(part * 240, part * 240 + 240)
                for side in (0, 1):
                    for n in range(4):
                        new = wide[side * 240 : side * 240 + 240, n * LANES : (n + 1) * LANES]
                        if first > 0:
                            new = new + gg[n % 2, n // 2, t, side, fr, :].astype(F32)
                        gg[n % 2, n // 2, t, side, fr, :] = new.astype(BF16)
            return 0

        lax.fori_loop(0, 4, step, 0)

    def ffn_post(k):
        r = rows_of(k)
        middle = mid[r, :]
        result[:, r] = (middle + facc[r, 0:width] + down_bias[...]).T.astype(BF16)
        g_ = dn2[r, 0:width]
        xhat, rstd = norm(middle)
        add_sum(13, jnp.sum(g_ * xhat, axis=0, keepdims=True))
        add_sum(14, jnp.sum(g_, axis=0, keepdims=True))
        d_result = grad[r, :].astype(F32) * weight_of(k)
        d_middle = d_result + norm_back(g_, ffn_gain[...], xhat, rstd)
        mid[r, :] = d_middle
        low = d_middle.astype(BF16)
        da[k, h, :, 0:width] = low
        add_sum(12, jnp.sum(low.astype(F32), axis=0, keepdims=True))
        gather_start(1, da, k)

    for k in range(groups - 1):
        ffn_pre(k)
    ffn_core(0, groups - 1)
    for k in range(groups - 1):
        ffn_post(k)
    ffn_pre(groups - 1)
    ffn_core(groups - 1, groups)
    if inner:
        g_begin()
    ffn_post(groups - 1)
    if inner:
        m_begin(1)
    for k in range(groups):
        gather_sent(0, n1, k)
        sum_sent(0, k)

    def back_prep(k):
        def step(i, _):
            r = pl.ds(pl.multiple_of(i * BLOCK, BLOCK), BLOCK)
            g_ = nt(da[k, i], wo[...]).astype(BF16).astype(F32)
            g_ = (g_ * invl[k, r, :]).astype(BF16)
            do_s[r, :] = g_
            dot_t[:, r] = g_.astype(F32).T
            q_t[:, r] = q_s[k, r, :].astype(F32).T
            acc[3 * LANES : 4 * LANES, :] += tn(ctx[k, r, :].astype(BF16), da[k, i])
            return 0

        lax.fori_loop(0, steps, step, 0)
        dk_t[...] = jnp.zeros_like(dk_t)
        dv_t[...] = jnp.zeros_like(dv_t)

    def back(k, hooks):
        def step(i, _):
            n = k * steps + i
            slot = n % 2
            run_hooks(hooks, i)
            p_in(n).wait()
            r = pl.ds(pl.multiple_of(i * BLOCK, BLOCK), BLOCK)
            g_ = do_s[r, :].astype(F32)
            prod = g_ * ctx[k, r, :]
            keys, vals = k_s[k], v_s[k]
            at = lane(BLOCK)

            def d_prob(j):
                mine = head_lanes(BLOCK, j)
                total = jnp.sum(jnp.where(mine, prod, 0.0), axis=1, keepdims=True)
                top = total.astype(BF16).astype(F32)
                row = jnp.where(at == USED, -top, jnp.where(at == USED + 1, top - total, 0.0))
                return nt(jnp.where(mine, g_, row).astype(BF16), vals)

            out = jnp.zeros((BLOCK, LANES), F32)
            dp = d_prob(0)
            for j in range(HEADS):
                later = d_prob(j + 1) if j + 1 < HEADS else None
                e = pslot[slot, j]
                ds = (e.astype(F32) * dp).astype(BF16)
                out = jnp.where(head_lanes(BLOCK, j), nn(ds, keys), out)
                hs = slice(j * HD, (j + 1) * HD)
                dk_t[hs, :] += nn(q_t[hs, r].astype(BF16), ds)
                if k < groups - 1:
                    dv_t[hs, :] += nn(dot_t[hs, r].astype(BF16), e)
                dp = later
            dq[r, :] = out

            @pl.when(n + 2 < groups * steps)
            def _():
                p_in(n + 2).start()

            return 0

        lax.fori_loop(0, steps, step, 0)

    def back_post(k):
        def step(i, _):
            r = pl.ds(pl.multiple_of(i * BLOCK, BLOCK), BLOCK)
            c, s = cos[r, :], sin[r, :]
            a = dq[r, :] * HD ** (-0.5)
            a = a * c - partner(a) * s
            b = dk_t[:, r].T * (1.0 / LOG2E)
            b = b * c - partner(b) * s
            if k < groups - 1:
                g_ = jnp.concatenate([a, b, dv_t[:, r].T], axis=1).astype(BF16)
            else:
                g_ = jnp.concatenate([a, b], axis=1).astype(BF16)
            cols = g_.shape[1]
            dqkv[r, 0:cols] = g_
            add_sum(2, jnp.sum(g_.astype(F32), axis=0, keepdims=True))
            acc[0:cols, :] += tn(g_, n1[k, i])
            return 0

        lax.fori_loop(0, steps, step, 0)

    def back_values(k):
        def step(i, _):
            n = k * steps + i
            slot = n % 2
            p_in(n).wait()
            r = pl.ds(pl.multiple_of(i * BLOCK, BLOCK), BLOCK)
            for j in range(HEADS):
                hs = slice(j * HD, (j + 1) * HD)
                dv_t[hs, :] += nn(dot_t[hs, r].astype(BF16), pslot[slot, j])
            p_in(k * steps + (i + 2) % steps).start()
            return 0

        lax.fori_loop(0, steps, step, 0)

        def post(i, _):
            r = pl.ds(pl.multiple_of(i * BLOCK, BLOCK), BLOCK)
            g_ = dv_t[:, r].T.astype(BF16)
            dqkv[r, 2 * LANES : 3 * LANES] = g_
            sums[0, 2:3, 2 * LANES : 3 * LANES] += jnp.sum(g_.astype(F32), axis=0, keepdims=True)
            acc[2 * LANES : 3 * LANES, :] += tn(g_, n1[k, i])
            return 0

        lax.fori_loop(0, steps, post, 0)

    def norm_sums():
        add_sum(0, jnp.sum(acc[0 : 3 * LANES, :] * wqt[...].astype(F32), axis=0, keepdims=True))
        add_sum(1, dims(sums[0, 2:3, 0 : 3 * LANES], wqt[...].astype(F32), 1, 0, lax.Precision.HIGHEST))

    def tokens_part(i):
        r = pl.ds(pl.multiple_of(i * BLOCK, BLOCK), BLOCK)
        return nt(dqkv[r, :], wq[...])

    def last_norm(k):
        r = rows_of(k)
        g_ = sum_finish(1, k)[:, 0:width]
        xhat, rstd = norm(tok[r, :].astype(F32))
        dtok_out[:, r] = (mid[r, :] + norm_back(g_, attn_gain[...], xhat, rstd)).T

    if inner:
        wait_x, go, take, first = (
            (lambda *a, f=f: partial(f, *a)) for f in (g_add_x, g_send, g_recv, g_first)
        )
        a, b = order[:2], order[2:]
        g_plan = (
            {0: [first(0)], 1: [first(1)], 3: [wait_x(0, a), go(0, 1)]},
            {0: [wait_x(0, b), take(0, 1), go(0, 2), m_middle],
             1: [wait_x(1, a), go(1, 1)],
             2: [take(0, 2), go(0, 3)],
             3: [wait_x(1, b), take(1, 1), go(1, 2)]},
            {0: [take(0, 3), partial(g_y_begin, 0), take(1, 2), go(1, 3)],
             2: [take(1, 3), partial(g_y_begin, 1), partial(f_back, 0), m_end],
             3: [partial(f_back, 1)]},
        )
    gather_forward(1, da, 0)
    for k in range(groups):
        gather_finish(1, da, k)
        back_prep(k)
        if k > 0:
            sum_forward(1, k - 1)
        if k == groups - 1:
            if inner:
                f_begin(0)
            back_values(k)
            if inner:
                f_begin(1)
        hooks = {}
        if k == 0:
            hooks[1] = [partial(gather_forward, 1, da, 1)]
            hooks[3] = [partial(gather_forward, 1, da, 2)]
        if inner:
            for at, todo in g_plan[k].items():
                hooks.setdefault(at, []).extend(todo)
        back(k, hooks)
        back_post(k)
        if k == groups - 1:
            norm_sums()
        if inner and k == groups - 1:
            f_begin(2)
        sum_start(1, k, tokens_part)
    for k in range(groups - 1):
        last_norm(k)
    sum_forward(1, groups - 1)
    if inner:
        f_back(2)
    last_norm(groups - 1)
    if inner:
        g_last()
        for n in range(3):
            f_end(n)
        dwqkv[...] = dims(wres[0 : 3 * LANES, :], perm[...], 0, 1)[0:width]
        dwout[...] = wres[3 * LANES : 4 * LANES, :].astype(F32)[0:USED, 0:width]
        m_last()
        for n in range(3):
            f_sent(n)
    else:
        small[0:8, :] = sums[0]
        small[8:16, :] = sums[1]
        acc_out[...] = acc[...]
    for k in range(groups):
        gather_sent(1, da, k)
        sum_sent(1, k)


def permutation():
    table = np.zeros((3 * USED, 3 * LANES), np.float32)
    for j in range(HEADS):
        for part in range(3):
            for i in range(HD):
                table[(j * 3 + part) * HD + i, part * LANES + j * HD + i] = 1.0
    return table


def turns(group_rows):
    freq = 10000.0 ** (-2.0 * np.arange(HD // 2) / HD)
    angle = np.arange(group_rows)[:, None] * freq[None, :]
    c = np.zeros((group_rows, LANES), np.float32)
    s = np.zeros((group_rows, LANES), np.float32)
    c[:, :USED] = np.tile(np.cos(angle), (1, 2 * HEADS))
    s[:, :USED] = np.tile(np.concatenate([-np.sin(angle), np.sin(angle)], axis=1), (1, HEADS))
    return c, s


def spreading():
    table = np.zeros((4 * LANES, 4 * LANES), np.float32)
    for n in range(4):
        for i in range(USED):
            table[n * LANES + i, n * USED + i] = 1.0
    return table


def layer(
    inner, tokens, wqkv, wout, w_in, attn_gain, attn_bias, qkv_bias, out_bias, ffn_gain,
    ffn_bias, up_bias, down_bias, lengths, ids, cw, grad,
):
    own, width = tokens.shape
    groups = lengths.shape[0]
    ff = up_bias.shape[0]
    group_rows = 4 * BLOCK
    c, s = turns(group_rows)
    vm = pl.BlockSpec(memory_space=pltpu.VMEM)
    sm = pl.BlockSpec(memory_space=pltpu.SMEM)
    anywhere = pl.BlockSpec(memory_space=pl.ANY)
    shape = jax.ShapeDtypeStruct
    row = lambda v: v.reshape(1, -1)
    wide_bias = jnp.concatenate([up_bias, jnp.pad(qkv_bias, (0, 480 - 3 * USED))]).reshape(5, 480)
    v, dma = pltpu.VMEM, pltpu.SemaphoreType.DMA
    chunks = (2, 2, 4, 2, 480, LANES)
    if inner:
        first = (
            shape((width, 3 * USED), F32),
            shape((USED, width), F32),
            shape((USED, 240), F32),
            shape((240, USED), F32),
        )
        remote = [
            v(chunks, BF16),
            v((2, 4, 2, 480, LANES), BF16),
            v((2, 4, 480, LANES), BF16),
            v((2, 2, 3, 480, LANES), BF16),
            v((480, LANES), BF16),
            [v((8, n, 512), BF16) for n in (16, 16, 48)],
            [v((8, n, 512), BF16) for n in (16, 16, 48)],
            v((4 * LANES, 512), BF16),
            v((16, 512), F32),
            v((2, 4, 8, 512), F32),
            v((8, 512), F32),
            v((8, 8, 512), F32),
            dma((37,)),
            dma((37,)),
            dma((29,)),
            dma((29,)),
            dma((2, 3, 8)),
            dma((2, 3, 8)),
            dma((2, 10)),
            dma((2, 12)),
        ]
    else:
        first = (shape((4 * LANES, 512), F32), shape(chunks, BF16))
        remote = []
    return pl.pallas_call(
        partial(body, inner),
        out_shape=(
            shape((width, own), BF16),
            shape((width, own), F32),
            first,
            shape((16, 512), F32),
            shape((groups, 4, HEADS, BLOCK, group_rows), BF16),
        ),
        in_specs=[anywhere] * 2 + [vm] * 2 + [[vm] * len(w_in)] + [vm] * 11 + [sm] * 3,
        out_specs=(vm, vm, (vm,) * len(first), vm, anywhere),
        scratch_shapes=[
            v((width, own), BF16),
            v((own, width), BF16),
            v((own, width), BF16),
            dma((groups + 1,)),
            v((groups, 4, BLOCK, 512), BF16),
            v((512, 3 * LANES), BF16),
            v((3 * LANES, 512), BF16),
            v((LANES, 512), BF16),
            v((1, 3 * LANES), F32),
            v((groups, group_rows, LANES), BF16),
            v((groups, group_rows, LANES), BF16),
            v((groups, group_rows, LANES), BF16),
            v((groups, group_rows, LANES), F32),
            v((groups, group_rows, LANES), F32),
            v((2, HEADS, BLOCK, group_rows), BF16),
            v((groups, 2, BLOCK, 512), BF16),
            v((groups, 2, BLOCK, 512), BF16),
            v((groups, BLOCK, 512), BF16),
            v((groups, BLOCK, 512), BF16),
            v((groups, BLOCK, 512), F32),
            v((own, width), F32),
            v((own, 512), BF16),
            v((own, 512), BF16),
            v((own, 512), BF16),
            v((own, 512), BF16),
            v((own, 512), F32),
            v((own, 512), F32),
            v((ff, 512), BF16),
            v((ff, 512), BF16),
            v((groups, 4, BLOCK, 512), BF16),
            v((group_rows, LANES), BF16),
            v((LANES, group_rows), F32),
            v((LANES, group_rows), F32),
            v((group_rows, LANES), F32),
            v((LANES, group_rows), F32),
            v((LANES, group_rows), F32),
            v((group_rows, 3 * LANES), BF16),
            v((2, 8, 512), F32),
            v((4 * LANES, 512), F32),
            dma((2, groups, 3)),
            dma((2, groups, 3)),
            dma((2, groups, 2)),
            dma((2, groups, 2)),
            dma((2,)),
            remote,
        ],
        compiler_params=pltpu.CompilerParams(
            collective_id=0, has_side_effects=True, vmem_limit_bytes=62 * 2**20
        ),
        name="layer",
    )(
        tokens.T, grad.T, wqkv, wout, w_in, row(attn_gain), row(attn_bias), row(out_bias),
        row(ffn_gain), row(ffn_bias), wide_bias, row(down_bias),
        jnp.asarray(permutation(), BF16), jnp.asarray(spreading(), BF16), jnp.asarray(c),
        jnp.asarray(s), lengths, ids, cw,
    )


def local(
    tokens, attn_norm_gain, attn_norm_bias, qkv_weight, qkv_bias, out_weight, out_bias,
    ffn_norm_gain, ffn_norm_bias, up_weight, up_bias, down_weight, down_bias, lengths,
    cluster_ids, cluster_weight, grad_out,
):
    width = tokens.shape[1]
    ff = up_bias.shape[0]
    inner = lax.axis_size("dp") == 8
    if inner:
        w_in = [up_weight, down_weight]
    else:
        part = jnp.stack([up_weight.T, down_weight], axis=0)
        part = lax.all_gather(part, "dp", axis=1, tiled=True)
        part = lax.all_gather(part, "heads", axis=0)
        part = jnp.pad(part, ((0, 0),) * 3 + ((0, LANES - USED),))
        part = part.reshape(2, 2, 2, 4, 2, 240, LANES)
        w_in = [part.transpose(1, 0, 3, 4, 2, 5, 6).reshape(2, 2, 4, 2, 480, LANES)]
    result, dtok, first, small, _ = layer(
        inner, tokens, qkv_weight, out_weight, w_in, attn_norm_gain, attn_norm_bias,
        qkv_bias, out_bias, ffn_norm_gain, ffn_norm_bias, up_bias, down_bias, lengths,
        cluster_ids, cluster_weight, grad_out,
    )
    if inner:
        dwqkv, dwout, dup, ddown = first
    else:
        acc, grads = first
        acc, own_sums = lax.psum((acc, small[2]), "dp")
        small = lax.psum(small, ("dp", "heads")).at[2].set(own_sums)
        gain_sum = (small[0, :width] - attn_norm_bias * small[1, :width]) / attn_norm_gain
        small = small.at[0, :width].set(gain_sum)
        grads = grads.reshape(2, 2, 4, 2, 2, 240, LANES).transpose(1, 0, 4, 2, 3, 5, 6)
        grads = grads.reshape(4, 2, ff, LANES)[..., :USED]
        grads = lax.psum_scatter(grads, "heads", scatter_dimension=0).astype(F32)
        grads = lax.psum_scatter(grads, "dp", scatter_dimension=1, tiled=True)
        dup, ddown = grads[0].T, grads[1]
        dwqkv = acc[: 3 * LANES, :width].reshape(3, LANES, width)[:, :USED]
        dwqkv = dwqkv.reshape(3, HEADS, HD, width).transpose(3, 1, 0, 2).reshape(width, 3 * USED)
        dwout = acc[3 * LANES : 3 * LANES + USED, :width]
    if inner:
        dqkvb = small[2, : 3 * USED]
    else:
        dqkvb = small[2, : 3 * LANES].reshape(3, LANES)[:, :USED].reshape(3, HEADS, HD)
        dqkvb = dqkvb.transpose(1, 0, 2).reshape(-1)
    return (
        result.T, dtok.T, small[0, :width], small[1, :width], dwqkv, dqkvb, dwout,
        small[12, :width], small[13, :width], small[14, :width], dup,
        small[8:12, :480].reshape(ff), ddown, small[15, :width],
    )


def solution(mesh):
    placed = (
        P(("dp", "heads"), None), P(), P(), P(None, "heads"), P("heads"), P("heads", None), P(),
        P(), P(), P("heads", "dp"), P(), P("dp", "heads"), P(), P("dp", None), P("dp", None),
        P(), P(("dp", "heads"), None),
    )
    given = (
        P(("dp", "heads"), None), P(("dp", "heads"), None), P(), P(), P(None, "heads"), P("heads"),
        P("heads", None), P(), P(), P(), P("heads", "dp"), P(), P("dp", "heads"), P(),
    )
    return jax.shard_map(local, mesh=mesh, in_specs=placed, out_specs=given, check_vma=False)
```
